256 devices in a mesh: gx: 4 (over y), gy: 8 (over x, core), gz: 8 (over z).
Axes of the slice: x: 4, y: 4, z: 8, core: 2. Of those that a mesh axis runs over, the one named last changes fastest.
Arguments:
- right_side: float32 [64, 256, 1024], P('gx', 'gy', 'gz'), may hold values from -48 to 48
- dielectric: float32 [64, 256, 1024], P('gx', 'gy', 'gz'), may hold values from 1 to 16
- guess: float32 [64, 256, 1024], P('gx', 'gy', 'gz'), may hold values from -1.5 to 1.5
Outputs:
- solution: float32 [64, 256, 1024], P('gx', 'gy', 'gz')
- residual: float32 [64, 256, 1024], P('gx', 'gy', 'gz')
The draws below stay inside these ranges and needn't reach their ends.
All inputs are finite; a program needn't handle non-finite values.
Results may differ from the reference program's by a relative error of at most 0.0001.
Values sent between devices are 32-bit elements; how exact they have to be, the bound alone decides.
A program may use at most 256 MiB of HBM per device.

```python
import math
import jax
import jax.numpy as jnp

LEVELS = 5
COARSE_SWEEPS = 4
NX = 64
NY = 256
NZ = 1024


def level_of(key, shape, split, smallest, largest):
    def one(position, blocks):
        draws = jax.random.uniform(jax.random.fold_in(jax.random.fold_in(key, 6), position), (blocks,), jnp.float32, smallest / len(split), largest / len(split))
        return jnp.repeat(jnp.exp(draws), shape[position] // blocks).reshape((-1,) + (1,) * (len(shape) - position - 1))

    loudness = one(*split[0])
    for cut in split[1:]:
        loudness = loudness * one(*cut)
    return loudness


def noise(key, dims, width, reach, pieces=(), held_as=jnp.bfloat16):
    entries = width * jax.random.normal(key, dims, jnp.float32)
    if pieces:
        entries = entries * level_of(key, dims, pieces, -0.22, 0.18)
    return jnp.clip(entries, -reach, reach).astype(held_as)


def setup_inputs(seed: int = 0) -> dict:
    splits = jax.random.split(jax.random.key(seed), 4)
    return {
        "right_side": noise(splits[0], (NX, NY, NZ), 8.0, 48.0, ((0, 4), (1, 8), (2, 8)), jnp.float32),
        "dielectric": jnp.clip(jnp.exp(math.log(16.0) - 2.7725887 * jax.random.uniform(splits[1], (NX, NY, NZ), jnp.float32) ** level_of(splits[1], (NX, NY, NZ), ((0, 4), (1, 8), (2, 8)), -0.2, 0.2)), 1.0, 16.0),
        "guess": noise(splits[2], (NX, NY, NZ), 0.25, 1.5, ((0, 4), (1, 8), (2, 8)), jnp.float32),
    }


OMEGA = 0.8


def coarsen(values):
    span_first, span_second, span_third = values.shape
    blocks = values.reshape(span_first // 2, 2, span_second // 2, 2, span_third // 2, 2)
    return jnp.mean(blocks, axis=(1, 3, 5))


def refine(values):
    return jnp.repeat(jnp.repeat(jnp.repeat(values, 2, axis=0), 2, axis=1), 2, axis=2)


def zero_rims(values):
    return jnp.pad(values, 1)


def neighbours(padded):
    return [padded[:-2, 1:-1, 1:-1], padded[2:, 1:-1, 1:-1], padded[1:-1, :-2, 1:-1],
            padded[1:-1, 2:, 1:-1], padded[1:-1, 1:-1, :-2], padded[1:-1, 1:-1, 2:]]


def operator_from(permit_padded, scale):
    center = permit_padded[1:-1, 1:-1, 1:-1]
    couplings = [0.5 * (center + side) for side in neighbours(permit_padded)]
    total = couplings[0]
    for extra in couplings[1:]:
        total = total + extra
    return couplings, scale * total, scale


def apply_operator(padded, stencil):
    couplings, diagonal_part, scale = stencil
    center = padded[1:-1, 1:-1, 1:-1]
    sides = neighbours(padded)
    total = couplings[0] * (center - sides[0])
    for index in range(1, 6):
        total = total + couplings[index] * (center - sides[index])
    return scale * total


def relax(values, source, stencil, padder):
    return values + OMEGA * (source - apply_operator(padder(values), stencil)) / stencil[1]


def coarsest(source, stencil, padder):
    values = OMEGA * source / stencil[1]
    for sweep_index in range(COARSE_SWEEPS - 1):
        values = relax(values, source, stencil, padder)
    return values


def cycle(level, source, stencils, padder, bottom):
    if level == len(stencils):
        return bottom(source)
    stencil = stencils[level]
    values = OMEGA * source / stencil[1]
    remainder = source - apply_operator(padder(values), stencil)
    values = values + refine(cycle(level + 1, coarsen(remainder), stencils, padder, bottom))
    return relax(values, source, stencil, padder)


def reference(right_side, dielectric, guess):
    levels = [dielectric]
    for level in range(1, LEVELS):
        levels.append(coarsen(levels[-1]))
    stencils = [operator_from(zero_rims(levels[level]), 0.25 ** level) for level in range(LEVELS)]
    finest = stencils[0]
    smoothed = relax(guess, right_side, finest, zero_rims)
    remainder = right_side - apply_operator(zero_rims(smoothed), finest)

    def bottom(source_low):
        return coarsest(source_low, stencils[LEVELS - 1], zero_rims)

    correction = cycle(1, coarsen(remainder), stencils[:LEVELS - 1], zero_rims, bottom)
    solution = relax(smoothed + refine(correction), right_side, finest, zero_rims)
    residual = right_side - apply_operator(zero_rims(solution), finest)
    return solution, residual
```

```python
import functools

import jax
import jax.numpy as jnp
from jax import lax
from jax.experimental import pallas as pl
from jax.experimental.pallas import tpu as pltpu
from jax.sharding import PartitionSpec as P

OMEGA = 0.8
MESH = pl.DeviceIdType.MESH
F32 = jnp.float32

X0, Y0, LANES = 16, 32, 128
X1, Y1 = 8, 16
X2, Y2, Z2 = 4, 8, 32
REACH = 3
ROWS = (2 * REACH + 1) * Y2
OWN = REACH * Y2


def iota(shape, dim):
    return lax.broadcasted_iota(jnp.int32, shape, dim)


def roll(v, shift, axis):
    size = v.shape[axis]
    if isinstance(shift, int):
        shift = shift % size
        if shift == 0:
            return v
    return pltpu.roll(v, shift, axis=axis)


def loop(count, body, init=0, unroll=True):
    return lax.fori_loop(0, count, body, init, unroll=unroll)


class Faces:
    def __init__(self, net, field, sent, got, nx, ny):
        self.net = net
        self.copies = {}
        lead = (slice(None),) * (len(field.shape) - 3)
        for d in (-1, 1):
            src, dst = (1, nx + 1) if d < 0 else (nx, 0)
            self.copies[(d, 0, 0)] = net.copy(
                field.at[lead + (src, pl.ds(8, ny))], field.at[lead + (dst, pl.ds(8, ny))], (d, 0, 0)
            )
            src, dst = (8, 8 + ny) if d < 0 else (7 + ny, 7)
            self.copies[(0, d, 0)] = net.copy(
                field.at[lead + (pl.ds(1, nx), pl.ds(src, 1))],
                field.at[lead + (pl.ds(1, nx), pl.ds(dst, 1))],
                (0, d, 0),
            )
            self.copies[(0, 0, d)] = net.copy(sent, got.at[0 if d > 0 else 1], (0, 0, d))

    def start(self):
        for way in ((0, 0, 1), (0, 0, -1), (1, 0, 0), (-1, 0, 0), (0, 1, 0), (0, -1, 0)):
            self.net.start(self.copies[way])

    def wait(self):
        for copy in self.copies.values():
            self.net.wait_recv(copy)


class Net:
    def __init__(self, sizes, send_sems, recv_sems):
        self.me = tuple(lax.axis_index(a) for a in ("gx", "gy", "gz"))
        self.sizes = sizes
        self.send_sems, self.recv_sems = send_sems, recv_sems
        self.used = 0
        self.started = []

    def there(self, way):
        found = None
        for at, size, d in zip(self.me, self.sizes, way):
            if d:
                ok = (at + d < size) if d > 0 else (at + d >= 0)
                found = ok if found is None else jnp.logical_and(found, ok)
        return found

    def when(self, way):
        found = self.there(way)
        return (lambda f: f()) if found is None else pl.when(found)

    def device(self, way, turn=0):
        x = self.me[0] + way[0]
        if turn:
            x = lax.rem(x + turn, self.sizes[0])
        return (x, self.me[1] + way[1], self.me[2] + way[2])

    def copy(self, src, dst, way, turn=0):
        i = self.used
        self.used += 1
        made = pltpu.make_async_remote_copy(
            src_ref=src,
            dst_ref=dst,
            send_sem=self.send_sems.at[i],
            recv_sem=self.recv_sems.at[i],
            device_id=self.device(way, turn),
            device_id_type=MESH,
        )
        return (made, way)

    def start(self, copy):
        made, way = copy
        self.started.append(copy)

        @self.when(way)
        def _():
            made.start()

    def wait_recv(self, copy):
        made, way = copy

        @self.when(tuple(-d for d in way))
        def _():
            made.wait_recv()

    def finish(self):
        for made, way in self.started:

            @self.when(way)
            def _():
                made.wait_send()


SEMS = 80


def pack_z(acc, v, first, w):
    group = iota((8, LANES), 1) // (2 * w)
    for j in range(v.shape[0] // 8):
        k = first + j
        acc = jnp.where(group == k, roll(v[8 * j : 8 * j + 8], (2 * k + 1) * w, 1), acc)
    return acc


def merge_z(got, w):
    return jnp.where((iota((8, LANES), 1) // w) % 2 == 0, got[0], got[1])


def unpack_z(both, first, tiles, w):
    return jnp.concatenate([roll(both, LANES - (2 * (first + j) + 1) * w, 1) for j in range(tiles)], axis=0)


def z_sides(v, halo, w):
    lane = iota(v.shape, 1)
    below = roll(jnp.where(lane >= LANES - w, halo, v), w, 1)
    above = roll(jnp.where(lane < w, halo, v), LANES - w, 1)
    return below, above


def sides(field, x, rows, first, step, below, above, lead=()):
    f = lambda dx, dy: field[lead + (x + 1 + dx, pl.ds(first + dy, rows))]
    return (f(-1, 0), f(1, 0), f(0, -step), f(0, step), below, above)


def weighted(cs, vs):
    total = cs[0] * vs[0]
    for c, v in zip(cs[1:], vs[1:]):
        total = total + c * v
    return total


def pair_sum(v, step, axis):
    even = (iota(v.shape, axis) // step) % 2 == 0
    size = v.shape[axis]
    return v + jnp.where(even, roll(v, size - step, axis), roll(v, step, axis))


def kernel(
    sizes,
    rhs_hbm, permit_hbm, guess_hbm,
    sol_hbm, res_hbm,
    rhs, gp, smooth, v0, sol, res, st0, zs0, zr0,
    p1, u1, v1, rw1, b1, st1, tmp, hw1, rw0, zs1, zr1, pick, spread,
    raw_p, raw_b, p2, u2, b2, st2, p3, u3, v3, b3, st3, p4, wa, wb, b4, st4, w3, v2, w2,
    local_sems, send_sems, recv_sems,
):
    nx = sizes[0]
    net = Net(sizes, send_sems, recv_sems)
    ix, iy, iz = net.me
    inner0 = (pl.ds(1, X0), pl.ds(8, Y0))

    loads = [
        pltpu.make_async_copy(guess_hbm, gp.at[(0,) + inner0], local_sems.at[0]),
        pltpu.make_async_copy(permit_hbm, gp.at[(1,) + inner0], local_sems.at[1]),
        pltpu.make_async_copy(rhs_hbm, rhs, local_sems.at[2]),
    ]
    for load in loads:
        load.start()

    ways = [(0, 0, 1), (0, 0, -1), (1, 0, 0), (-1, 0, 0), (0, 1, 0), (0, -1, 0)]
    barrier = pltpu.get_barrier_semaphore()
    for way in ways:

        @net.when(way)
        def _():
            pl.semaphore_signal(barrier, inc=1, device_id=net.device(way), device_id_type=MESH)

    fields0 = [(gp.at[0], X0, Y0), (gp.at[1], X0, Y0), (smooth, X0, Y0), (v0, X0, Y0), (sol, X0, Y0)]
    fields1 = [(p1, X1, Y1), (u1, X1, Y1)]

    def clear(fields, zr):
        for way in ways:
            out = net.there(way)

            @pl.when(jnp.logical_not(out))
            def _():
                side = sum(way) > 0
                for f, fx, fy in fields:
                    if way[0]:
                        f[fx + 1 if side else 0] = jnp.zeros((fy + 16, LANES), F32)
                    elif way[1]:
                        at = 8 + fy if side else 7
                        f[pl.ds(1, fx), pl.ds(at, 1)] = jnp.zeros((fx, 1, LANES), F32)
                if way[2]:
                    for r in range(zr.shape[0]):
                        zr[r, 1 if side else 0] = jnp.zeros(zr.shape[2:], F32)

    clear(fields0, zr0)

    loads[0].wait()
    loads[1].wait()

    def pack_gp(x, accs):
        return tuple(pack_z(a, gp[i, x + 1, 8 : 8 + Y0], 4 * x, 1) for i, a in enumerate(accs))

    zero = jnp.zeros((8, LANES), F32)
    accs = loop(X0, pack_gp, (zero, zero))
    zs0[0, :8] = accs[0]
    zs0[0, 8:] = accs[1]

    pl.semaphore_wait(barrier, sum(net.there(way).astype(jnp.int32) for way in ways))

    round_a = Faces(net, gp, zs0.at[0], zr0.at[0], X0, Y0)
    round_a.start()

    def coarse_p1(x, acc):
        tmp[x] = gp[1, 2 * x + 1, 8 : 8 + Y0] + gp[1, 2 * x + 2, 8 : 8 + Y0]
        v = tmp[x, pl.ds(0, Y1, stride=2)] + tmp[x, pl.ds(1, Y1, stride=2)]
        v = 0.125 * pair_sum(v, 1, 1)
        p1[x + 1, 8 : 8 + Y1] = v
        return pack_z(acc, v, 2 * x, 2)

    clear(fields1, zr1)
    zs1[0] = loop(X1, coarse_p1, zero)
    faces_p1 = Faces(net, p1, zs1.at[0], zr1.at[0], X1, Y1)
    faces_p1.start()

    for x in range(X2):
        row, col = iota((LANES, LANES), 0), iota((LANES, LANES), 1)
        take = jnp.logical_and(col == Z2 * x + row // 4, row % 2 == 0)
        pick[pl.ds(x * LANES, LANES)] = jnp.where(take, 0.125, 0.0).astype(F32)
    row, col = iota((LANES, LANES), 0), iota((LANES, LANES), 1)
    spread[:, :LANES] = (row == Z2 + col // 4).astype(F32)
    left = jnp.logical_and(row == Z2 - 1, col >= LANES - 2)
    right = jnp.logical_and(row == 2 * Z2, col < 2)
    spread[:, LANES:] = jnp.logical_or(left, right).astype(F32)

    def compact(planes):
        parts = []
        for x in range(X2):
            tmp[x, :Y1] = planes(2 * x) + planes(2 * x + 1)
            parts.append(tmp[x, pl.ds(0, Y2, stride=2)] + tmp[x, pl.ds(1, Y2, stride=2)])
        return lax.dot_general(
            jnp.concatenate(parts, axis=1), pick[...], (((1,), (0,)), ((), ())),
            precision=lax.Precision.HIGHEST, preferred_element_type=F32,
        )

    for raw in (raw_p, raw_b):
        for yd in range(2 * REACH + 1):
            if yd != REACH:
                d = yd - REACH

                @pl.when(jnp.logical_not(net.there((0, d, 0))))
                def _():
                    raw[yd] = jnp.zeros(raw.shape[1:], F32)

        for zd in (0, 2):

            @pl.when(jnp.logical_not(net.there((0, 0, zd - 1))))
            def _():
                if raw is raw_p:
                    raw[REACH, ix, zd] = jnp.zeros((8, LANES), F32)
                else:
                    raw[REACH, :, zd] = jnp.zeros((nx, 8, LANES), F32)

    raw_p[REACH, ix, 1] = compact(lambda x: p1[x + 1, 8 : 8 + Y1])
    p2_z = [net.copy(raw_p.at[REACH, ix, 1], raw_p.at[REACH, ix, 1 - d], (0, 0, d)) for d in (1, -1)]
    for copy in p2_z:
        net.start(copy)
    loads[2].wait()

    def couplings(scale, p, ns):
        cs = [scale * (p + n) for n in ns]
        return cs, cs[0] + cs[1] + cs[2] + cs[3] + cs[4] + cs[5]

    round_a.wait()
    both_g = merge_z([zr0[0, 0, :8], zr0[0, 1, :8]], 1)
    both_p = merge_z([zr0[0, 0, 8:], zr0[0, 1, 8:]], 1)

    def stencil_sides0(field, x, both, lead=()):
        v = field[lead + (x + 1, pl.ds(8, Y0))]
        return v, sides(field, x, Y0, 8, 1, *z_sides(v, unpack_z(both, 4 * x, 4, 1), 1), lead=lead)

    def first(x, acc):
        p, ns = stencil_sides0(gp, x, both_p, (1,))
        cs, diag = couplings(0.5, p, ns)
        for i, c in enumerate(cs):
            st0[i, x] = c
        inv = OMEGA / diag
        st0[6, x] = diag
        st0[7, x] = inv
        v, vs = stencil_sides0(gp, x, both_g, (0,))
        s = (1.0 - OMEGA) * v + inv * (rhs[x] + weighted(cs, vs))
        smooth[x + 1, 8 : 8 + Y0] = s
        return pack_z(acc, s, 4 * x, 1)

    zs0[1, :8] = loop(X0, first, zero)

    def faces0(field, r):
        return Faces(net, field, zs0.at[r, pl.ds(0, 8)], zr0.at[r, :, pl.ds(0, 8)], X0, Y0)

    round_b = faces0(smooth, 1)
    round_b.start()

    faces_p1.wait()
    both_p1 = merge_z(zr1[0], 2)

    def sides1(field, x, halo):
        v = field[x + 1, 8 : 8 + Y1]
        return v, sides(field, x, Y1, 8, 1, *z_sides(v, halo, 2))

    def couple1(x, _):
        p, ns = sides1(p1, x, unpack_z(both_p1, 2 * x, 2, 2))
        cs, diag = couplings(0.125, p, ns)
        for i, c in enumerate(cs):
            st1[i, x] = c
        st1[6, x] = diag
        st1[7, x] = OMEGA / diag
        return 0

    loop(X1, couple1)

    round_b.wait()
    both_s = merge_z([zr0[1, 0, :8], zr0[1, 1, :8]], 1)

    def remainder0(field, x, both):
        v, vs = stencil_sides0(field, x, both)
        return rhs[x] - st0[6, x] * v + weighted([st0[i, x] for i in range(6)], vs)

    def down0(x, acc):
        tmp[x] = remainder0(smooth, 2 * x, both_s) + remainder0(smooth, 2 * x + 1, both_s)
        b = tmp[x, pl.ds(0, Y1, stride=2)] + tmp[x, pl.ds(1, Y1, stride=2)]
        b = 0.125 * pair_sum(b, 1, 1)
        b1[x] = b
        u = st1[7, x] * b
        u1[x + 1, 8 : 8 + Y1] = u
        return pack_z(acc, u, 2 * x, 2)

    zs1[1] = loop(X1, down0, zero)

    round_c = Faces(net, u1, zs1.at[1], zr1.at[1], X1, Y1)
    round_c.start()

    for copy in p2_z:
        net.wait_recv(copy)
    p2_x = [net.copy(raw_p.at[REACH, ix], raw_p.at[REACH, ix], (0, 0, 0), k) for k in range(1, nx)]
    for copy in p2_x:
        net.start(copy)

    round_c.wait()
    both_u = merge_z(zr1[1], 2)

    def remainder1(x):
        u, us = sides1(u1, x, unpack_z(both_u, 2 * x, 2, 2))
        return b1[x] - st1[6, x] * u + weighted([st1[i, x] for i in range(6)], us)

    raw_b[REACH, ix, 1] = compact(remainder1)

    mine = raw_b.at[REACH, ix, 1]
    b2_xz = []
    for d in (1, -1, 0):
        for k in range(nx):
            if d or k:
                b2_xz.append(net.copy(mine, raw_b.at[REACH, ix, 1 - d], (0, 0, d), k))
    for copy in b2_xz:
        net.start(copy)

    for copy in p2_x:
        net.wait_recv(copy)
    steps = [d for k in range(1, REACH + 1) for d in (k, -k)]
    p2_y = [net.copy(raw_p.at[REACH], raw_p.at[REACH - d], (0, d, 0)) for d in steps]
    for copy in p2_y:
        net.start(copy)

    for copy in b2_xz:
        net.wait_recv(copy)
    b2_y = [net.copy(raw_b.at[REACH], raw_b.at[REACH - d], (0, d, 0)) for d in steps]
    for copy in b2_y:
        net.start(copy)

    for f in (p2, u2, p3, u3, v3, p4, wa, wb):
        n = f.shape[0]
        f[0] = jnp.zeros(f.shape[1:], F32)
        f[n - 1] = jnp.zeros(f.shape[1:], F32)

        def pad(x, _):
            f[x, :8] = jnp.zeros((8, LANES), F32)
            f[x, 8 + ROWS :] = jnp.zeros((8, LANES), F32)
            return 0

        loop(n, pad)
    for f in (v2, w2):
        loop(f.shape[0], lambda x, _: f.__setitem__(x, jnp.zeros(f.shape[1:], F32)) or 0)

    def region(raw, xd, x):
        lane = iota((ROWS, LANES), 1)
        part = [
            roll(raw[:, xd, zd].reshape(ROWS, LANES), Z2 * (zd - x), 1) for zd in range(3)
        ]
        return jnp.where(lane < Z2, part[0], jnp.where(lane < 2 * Z2, part[1], jnp.where(lane < 3 * Z2, part[2], 0.0)))

    for copy in p2_y:
        net.wait_recv(copy)

    def unpack_p(xd, _):
        for x in range(X2):
            p2[X2 * xd + x + 1, 8 : 8 + ROWS] = region(raw_p, xd, x)
        return 0

    loop(nx, unpack_p)

    def coarse(v, step):
        return 0.125 * pair_sum(pair_sum(v, step, 0), step, 1)

    def coarse_p(src, dst, step):
        def one(x, _):
            v = src[2 * x + 1, 8 : 8 + ROWS] + src[2 * x + 2, 8 : 8 + ROWS]
            dst[x + 1, 8 : 8 + ROWS] = coarse(v, step)
            return 0

        loop(dst.shape[0] - 2, one)

    coarse_p(p2, p3, 1)
    coarse_p(p3, p4, 2)

    def region_sides(field, x, step, first=8, rows=ROWS):
        v = field[x + 1, pl.ds(first, rows)]
        return v, sides(field, x, rows, first, step, roll(v, step, 1), roll(v, LANES - step, 1))

    def couple_region(p_ref, st, step, scale):
        def one(x, _):
            p, ns = region_sides(p_ref, x, step)
            cs, diag = couplings(scale, p, ns)
            for i, c in enumerate(cs):
                st[i, x] = c
            inside = p > 0.0
            st[6, x] = diag
            st[7, x] = jnp.where(inside, OMEGA / jnp.where(inside, diag, 1.0), 0.0)
            return 0

        loop(p_ref.shape[0] - 2, one)

    couple_region(p2, st2, 1, 0.5 / 16)
    couple_region(p3, st3, 2, 0.5 / 64)
    couple_region(p4, st4, 4, 0.5 / 256)

    for copy in b2_y:
        net.wait_recv(copy)

    def unpack_b(xd, _):
        for x in range(X2):
            at = X2 * xd + x
            b = region(raw_b, xd, x)
            b2[at] = b
            u2[at + 1, 8 : 8 + ROWS] = st2[7, at] * b
        return 0

    loop(nx, unpack_b)

    def remainder(u_ref, b_ref, st, x, step):
        u, us = region_sides(u_ref, x, step)
        return b_ref[x] - st[6, x] * u + weighted([st[i, x] for i in range(6)], us)

    def down(u_ref, b_ref, st, step, next_b, next_u, next_st):
        def one(x, _):
            r = remainder(u_ref, b_ref, st, 2 * x, step) + remainder(u_ref, b_ref, st, 2 * x + 1, step)
            b = coarse(r, step)
            next_b[x] = b
            next_u[x + 1, 8 : 8 + ROWS] = next_st[7, x] * b
            return 0

        loop(next_b.shape[0], one)

    down(u2, b2, st2, 1, b3, u3, st3)
    down(u3, b3, st3, 2, b4, wa, st4)

    def relaxed(field, b, st, x, step, first=8, rows=ROWS, at=0):
        v, vs = region_sides(field, x, step, first, rows)
        s = weighted([st[i, x, at : at + rows] for i in range(6)], vs)
        return (1.0 - OMEGA) * v + st[7, x, at : at + rows] * (b[x, at : at + rows] + s)

    for src, dst in ((wa, wb), (wb, wa), (wa, wb)):

        def sweep(x, _):
            dst[x + 1, 8 : 8 + ROWS] = relaxed(src, b4, st4, x, 4)
            return 0

        loop(nx, sweep)

    near, span = OWN - 8, 24

    def up3(x, _):
        v3[x + 1, 8 : 8 + ROWS] = u3[x + 1, 8 : 8 + ROWS] + wb[x // 2 + 1, 8 : 8 + ROWS]
        return 0

    loop(2 * nx, up3)

    def relax3(x, _):
        w3[x] = relaxed(v3, b3, st3, x, 2, 8 + near, span, near)
        return 0

    loop(2 * nx, relax3)

    def up2(x, _):
        v2[x + 1, 8 : 8 + span] = u2[x + 1, 8 + near : 8 + near + span] + w3[x // 2]
        return 0

    loop(4 * nx, up2)

    def relax2(x, _):
        w2[x + 1] = relaxed(v2, b2, st2, x, 1, 8, span, near)
        return 0

    loop(4 * nx, relax2)

    wide = lax.dot_general(
        w2[pl.ds(X2 * ix, X2 + 2)].reshape((X2 + 2) * span, LANES), spread[...], (((1,), (0,)), ((), ())),
        precision=lax.Precision.HIGHEST, preferred_element_type=F32,
    ).reshape(X2 + 2, span, 2 * LANES)
    for x in range(X1 + 2):
        m = wide[(x + 1) // 2, :, :LANES]
        rw1[x, pl.ds(8, Y2, stride=2)] = m[8 : 8 + Y2]
        rw1[x, pl.ds(9, Y2, stride=2)] = m[8 : 8 + Y2]
        rw1[x, 7:8] = m[7:8]
        rw1[x, 8 + Y1 : 9 + Y1] = m[8 + Y2 : 9 + Y2]
        v1[x] = u1[x] + rw1[x]
    for x in range(X2):
        h = wide[x + 1, 8 : 8 + Y2, LANES:]
        hw1[x, pl.ds(0, Y2, stride=2)] = h
        hw1[x, pl.ds(1, Y2, stride=2)] = h

    def up1(x, acc):
        halo = unpack_z(both_u, 2 * x, 2, 2) + hw1[x // 2]
        v, vs = sides1(v1, x, halo)
        w = (1.0 - OMEGA) * v + st1[7, x] * (b1[x] + weighted([st1[i, x] for i in range(6)], vs))
        rw0[x, pl.ds(0, Y1, stride=2)] = w
        rw0[x, pl.ds(1, Y1, stride=2)] = w
        for d in range(2):
            v = smooth[2 * x + d + 1, 8 : 8 + Y0] + rw0[x]
            v0[2 * x + d + 1, 8 : 8 + Y0] = v
            acc = pack_z(acc, v, 4 * (2 * x + d), 1)
        return acc

    zs0[2, :8] = loop(X1, up1, zero)

    round_f = faces0(v0, 2)
    round_f.start()
    round_f.wait()
    both_v = merge_z([zr0[2, 0, :8], zr0[2, 1, :8]], 1)

    def last(x, acc):
        v, vs = stencil_sides0(v0, x, both_v)
        s = (1.0 - OMEGA) * v + st0[7, x] * (rhs[x] + weighted([st0[i, x] for i in range(6)], vs))
        sol[x + 1, 8 : 8 + Y0] = s
        return pack_z(acc, s, 4 * x, 1)

    zs0[3, :8] = loop(X0, last, zero)

    round_g = faces0(sol, 3)
    round_g.start()
    out_sol = pltpu.make_async_copy(sol.at[inner0], sol_hbm, local_sems.at[3])
    out_sol.start()
    round_g.wait()
    both_x = merge_z([zr0[3, 0, :8], zr0[3, 1, :8]], 1)

    def residual(x, _):
        res[x] = remainder0(sol, x, both_x)
        return 0

    loop(X0, residual)
    out_res = pltpu.make_async_copy(res, res_hbm, local_sems.at[4])
    out_res.start()
    net.finish()
    out_sol.wait()
    out_res.wait()


def scratch(nx):
    def vmem(*shape):
        return pltpu.VMEM(shape + (LANES,), F32)

    padded0 = (X0 + 2, Y0 + 16)
    padded1 = (X1 + 2, Y1 + 16)
    n2, n3, n4, tall = 4 * nx, 2 * nx, nx, ROWS + 16
    reach = 2 * REACH + 1
    return [
        vmem(X0, Y0), vmem(2, *padded0), vmem(*padded0), vmem(*padded0), vmem(*padded0), vmem(X0, Y0),
        vmem(8, X0, Y0), vmem(4, 16), vmem(4, 2, 16),
        vmem(*padded1), vmem(*padded1), vmem(*padded1), vmem(*padded1), vmem(X1, Y1), vmem(8, X1, Y1),
        vmem(X1, Y0), vmem(X2, Y1), vmem(X1, Y0), vmem(2, 8), vmem(2, 2, 8),
        vmem(X2 * LANES), pltpu.VMEM((LANES, 2 * LANES), F32),
        vmem(reach, nx, 3, 8), vmem(reach, nx, 3, 8),
        vmem(n2 + 2, tall), vmem(n2 + 2, tall), vmem(n2, ROWS), vmem(8, n2, ROWS),
        vmem(n3 + 2, tall), vmem(n3 + 2, tall), vmem(n3 + 2, tall), vmem(n3, ROWS), vmem(8, n3, ROWS),
        vmem(n4 + 2, tall), vmem(n4 + 2, tall), vmem(n4 + 2, tall), vmem(n4, ROWS), vmem(8, n4, ROWS),
        vmem(n3, 24), vmem(n2 + 2, 40), vmem(n2 + 2, 24),
        pltpu.SemaphoreType.DMA((5,)), pltpu.SemaphoreType.DMA((SEMS,)), pltpu.SemaphoreType.DMA((SEMS,)),
    ]


def solution(mesh):
    sizes = tuple(mesh.shape[a] for a in ("gx", "gy", "gz"))
    block = jax.ShapeDtypeStruct((X0, Y0, LANES), F32)
    spec = P("gx", "gy", "gz")

    def shards(right_side, dielectric, guess):
        return pl.pallas_call(
            functools.partial(kernel, sizes),
            out_shape=(block, block),
            in_specs=[pl.BlockSpec(memory_space=pl.ANY)] * 3,
            out_specs=[pl.BlockSpec(memory_space=pl.ANY)] * 2,
            scratch_shapes=scratch(sizes[0]),
            compiler_params=pltpu.CompilerParams(
                collective_id=0, has_side_effects=True, vmem_limit_bytes=40 * 2**20
            ),
            name="vcycle",
        )(right_side, dielectric, guess)

    return jax.shard_map(
        shards, mesh=mesh, in_specs=(spec, spec, spec), out_specs=(spec, spec), check_vma=False
    )
```

```python
import functools

import jax
import jax.numpy as jnp
from jax import lax
from jax.experimental import pallas as pl
from jax.experimental.pallas import tpu as pltpu
from jax.sharding import PartitionSpec as P

OMEGA = 0.8
MESH = pl.DeviceIdType.MESH
F32 = jnp.float32

X0, Y0, LANES = 16, 32, 128
X1, Y1 = 8, 16
X2, Y2, Z2 = 4, 8, 32
REACH = 3
ROWS = (2 * REACH + 1) * Y2
OWN = REACH * Y2


def iota(shape, dim):
    return lax.broadcasted_iota(jnp.int32, shape, dim)


def roll(v, shift, axis):
    size = v.shape[axis]
    if isinstance(shift, int):
        shift = shift % size
        if shift == 0:
            return v
    return pltpu.roll(v, shift, axis=axis)


def loop(count, body, init=0, unroll=True):
    return lax.fori_loop(0, count, body, init, unroll=unroll)


class Faces:
    def __init__(self, net, field, sent, got, nx, ny):
        self.net = net
        self.copies = {}
        lead = (slice(None),) * (len(field.shape) - 3)
        for d in (-1, 1):
            src, dst = (1, nx + 1) if d < 0 else (nx, 0)
            self.copies[(d, 0, 0)] = net.copy(
                field.at[lead + (src, pl.ds(8, ny))], field.at[lead + (dst, pl.ds(8, ny))], (d, 0, 0)
            )
            src, dst = (8, 8 + ny) if d < 0 else (7 + ny, 7)
            self.copies[(0, d, 0)] = net.copy(
                field.at[lead + (pl.ds(1, nx), pl.ds(src, 1))],
                field.at[lead + (pl.ds(1, nx), pl.ds(dst, 1))],
                (0, d, 0),
            )
            self.copies[(0, 0, d)] = net.copy(sent, got.at[0 if d > 0 else 1], (0, 0, d))

    def start(self):
        for way in ((0, 0, 1), (0, 0, -1), (1, 0, 0), (-1, 0, 0), (0, 1, 0), (0, -1, 0)):
            self.net.start(self.copies[way])

    def wait(self):
        for copy in self.copies.values():
            self.net.wait_recv(copy)


class Net:
    def __init__(self, sizes, send_sems, recv_sems):
        self.me = tuple(lax.axis_index(a) for a in ("gx", "gy", "gz"))
        self.sizes = sizes
        self.send_sems, self.recv_sems = send_sems, recv_sems
        self.used = 0
        self.started = []

    def there(self, way):
        found = None
        for at, size, d in zip(self.me, self.sizes, way):
            if d:
                ok = (at + d < size) if d > 0 else (at + d >= 0)
                found = ok if found is None else jnp.logical_and(found, ok)
        return found

    def when(self, way):
        found = self.there(way)
        return (lambda f: f()) if found is None else pl.when(found)

    def device(self, way, turn=0):
        x = self.me[0] + way[0]
        if turn:
            x = lax.rem(x + turn, self.sizes[0])
        return (x, self.me[1] + way[1], self.me[2] + way[2])

    def copy(self, src, dst, way, turn=0):
        i = self.used
        self.used += 1
        made = pltpu.make_async_remote_copy(
            src_ref=src,
            dst_ref=dst,
            send_sem=self.send_sems.at[i],
            recv_sem=self.recv_sems.at[i],
            device_id=self.device(way, turn),
            device_id_type=MESH,
        )
        return (made, way)

    def start(self, copy):
        made, way = copy
        self.started.append(copy)

        @self.when(way)
        def _():
            made.start()

    def wait_recv(self, copy):
        made, way = copy

        @self.when(tuple(-d for d in way))
        def _():
            made.wait_recv()

    def finish(self):
        for made, way in self.started:

            @self.when(way)
            def _():
                made.wait_send()


SEMS = 104


def pack_z(acc, v, first, w):
    group = iota((8, LANES), 1) // (2 * w)
    for j in range(v.shape[0] // 8):
        k = first + j
        acc = jnp.where(group == k, roll(v[8 * j : 8 * j + 8], (2 * k + 1) * w, 1), acc)
    return acc


def cross_z(left, right):
    odd = iota((8, LANES), 1) % 2 == 1
    return jnp.where(odd, roll(left, 1, 1), roll(right, LANES - 1, 1))


def at_edges(packed, first, tiles):
    v = jnp.concatenate([roll(packed, LANES - (2 * (first + j) + 1), 1) for j in range(tiles)], axis=0)
    lane = iota(v.shape, 1)
    return jnp.where(jnp.logical_or(lane == 0, lane == LANES - 1), v, 0.0)


def merge_z(got, w):
    return jnp.where((iota((8, LANES), 1) // w) % 2 == 0, got[0], got[1])


def unpack_z(both, first, tiles, w):
    return jnp.concatenate([roll(both, LANES - (2 * (first + j) + 1) * w, 1) for j in range(tiles)], axis=0)


def z_sides(v, halo, w):
    lane = iota(v.shape, 1)
    below = roll(jnp.where(lane >= LANES - w, halo, v), w, 1)
    above = roll(jnp.where(lane < w, halo, v), LANES - w, 1)
    return below, above


def sides(field, x, rows, first, step, below, above, lead=()):
    f = lambda dx, dy: field[lead + (x + 1 + dx, pl.ds(first + dy, rows))]
    return (f(-1, 0), f(1, 0), f(0, -step), f(0, step), below, above)


def weighted(cs, vs):
    total = cs[0] * vs[0]
    for c, v in zip(cs[1:], vs[1:]):
        total = total + c * v
    return total


def pair_sum(v, step, axis):
    even = (iota(v.shape, axis) // step) % 2 == 0
    size = v.shape[axis]
    return v + jnp.where(even, roll(v, size - step, axis), roll(v, step, axis))


def kernel(
    sizes,
    rhs_hbm, permit_hbm, guess_hbm,
    sol_hbm, res_hbm,
    rhs, gp, smooth, vn, sol, res, st0, zs0, zr0, part, pack_d, cz,
    xa, ya, za, xd, yd, zd, xf, yf, zf, exy, exz, eyz, pxy, pxz, pyz,
    kx, ky, kz, cxz, cyz, rims, crossed,
    p1, u1, v1, rw1, b1, st1, tmp, hw1, rw0, zs1, zr1, pick, spread,
    raw_p, raw_b, p2, u2, b2, st2, p3, u3, v3, b3, st3, p4, wa, wb, b4, st4, w3, v2, w2,
    local_sems, send_sems, recv_sems,
):
    nx = sizes[0]
    net = Net(sizes, send_sems, recv_sems)
    ix, iy, iz = net.me
    inner0 = (pl.ds(1, X0), pl.ds(8, Y0))
    own0 = slice(8, 8 + Y0)

    loads = [
        pltpu.make_async_copy(guess_hbm, gp.at[(0,) + inner0], local_sems.at[0]),
        pltpu.make_async_copy(permit_hbm, gp.at[(1,) + inner0], local_sems.at[1]),
        pltpu.make_async_copy(rhs_hbm, rhs, local_sems.at[2]),
    ]
    for load in loads:
        load.start()

    ways = [(0, 0, 1), (0, 0, -1), (1, 0, 0), (-1, 0, 0), (0, 1, 0), (0, -1, 0)]
    barrier = pltpu.get_barrier_semaphore()
    for way in ways:

        @net.when(way)
        def _():
            pl.semaphore_signal(barrier, inc=1, device_id=net.device(way), device_id_type=MESH)

    signs = (-1, 1)
    zeros = lambda *shape: jnp.zeros(shape + (LANES,), F32)

    def clear(fields, landings):
        todo = {}
        for f, fx, fy in fields:
            for i, d in enumerate(signs):
                todo.setdefault((d, 0, 0), []).append((f, (fx + 1 if i else 0,)))
                todo.setdefault((0, d, 0), []).append((f, (pl.ds(1, fx), pl.ds(8 + fy if i else 7, 1))))
        for ref, at, way in landings:
            todo.setdefault(way, []).append((ref, at))
        for way, items in todo.items():

            @pl.when(jnp.logical_not(net.there(way)))
            def _():
                for ref, at in items:
                    ref[at] = jnp.zeros(ref.at[at].shape, F32)

    def landings(x, y, z):
        return [(ref, (i,), tuple(d if n == axis else 0 for n in range(3)))
                for axis, ref in enumerate((x, y, z)) for i, d in enumerate(signs)]

    def edge_landings(xy, xz, yz):
        out = []
        for i, d in enumerate(signs):
            for j, e in enumerate(signs):
                out += [(xy, (i, j), (d, e, 0)), (xz, (i, j), (d, 0, e)), (yz, (i, j), (0, d, e))]
        return out

    def zero_halo(f, lead=()):
        for x in (0, X0 + 1):
            f[lead + (x,)] = zeros(Y0 + 16)

        def one(x, _):
            f[lead + (x + 1, slice(0, 8))] = zeros(8)
            f[lead + (x + 1, slice(8 + Y0, 16 + Y0))] = zeros(8)
            return 0

        loop(X0, one)

    zero_halo(gp, (0,))
    zero_halo(gp, (1,))
    clear([], landings(xa, ya, za))

    for load in loads:
        load.wait()

    lane0 = iota((Y0, LANES), 1)

    def couplings(scale, p, ns):
        cs = [scale * (p + n) for n in ns]
        return cs, cs[0] + cs[1] + cs[2] + cs[3] + cs[4] + cs[5]

    def inside0(field, x, lead=()):
        v = field[lead + (x + 1, pl.ds(8, Y0))]
        return v, sides(field, x, Y0, 8, 1, roll(v, 1, 1), roll(v, LANES - 1, 1), lead=lead)

    def sum0(x, vs):
        return weighted([st0[i, x] for i in range(6)], vs)

    def first(x, accs):
        p, ns = inside0(gp, x, (1,))
        ns = ns[:4] + (jnp.where(lane0 == 0, 0.0, ns[4]), jnp.where(lane0 == LANES - 1, 0.0, ns[5]))
        cs, diag = couplings(0.5, p, ns)
        cs[4] = jnp.where(lane0 == 0, 0.0, cs[4])
        cs[5] = jnp.where(lane0 == LANES - 1, 0.0, cs[5])
        for i, c in enumerate(cs):
            st0[i, x] = c
        st0[6, x] = diag
        v, vs = inside0(gp, x, (0,))
        part[x] = rhs[x] + weighted(cs, vs)
        return pack_z(accs[0], v, 4 * x, 1), pack_z(accs[1], p, 4 * x, 1)

    zero = zeros(8)
    accs = loop(X0, first, (zero, zero))
    zs0[0, 0] = accs[0]
    zs0[0, 1] = accs[1]

    pl.semaphore_wait(barrier, sum(net.there(way).astype(jnp.int32) for way in ways))

    def face_copies(field, lead, x_to, y_to, z_from, z_to):
        copies = []
        for i, d in ((1, 1), (0, -1)):
            copies.append(net.copy(z_from, z_to(1 - i), (0, 0, d)))
        for i, d in ((1, 1), (0, -1)):
            copies.append(net.copy(field.at[lead + (X0 if i else 1, pl.ds(8, Y0))], x_to(1 - i), (d, 0, 0)))
        for i, d in ((1, 1), (0, -1)):
            row = 7 + Y0 if i else 8
            copies.append(net.copy(field.at[lead + (pl.ds(1, X0), pl.ds(row, 1))], y_to(1 - i), (0, d, 0)))
        return copies

    def edge_copies(field, lead, packed, xy, xz, yz):
        copies = []
        for i, d in enumerate(signs):
            for j, e in enumerate(signs):
                copies.append(net.copy(packed, xz.at[1 - i, 1 - j], (d, 0, e)))
                copies.append(net.copy(packed, yz.at[1 - i, 1 - j], (0, d, e)))
        for i, d in enumerate(signs):
            for j, e in enumerate(signs):
                line = field.at[lead + (X0 if i else 1, pl.ds(7 + Y0 if j else 8, 1))]
                copies.append(net.copy(line, xy.at[1 - i, 1 - j, pl.ds(0, 1)], (d, e, 0)))
        return copies

    def start(copies):
        for copy in copies:
            net.start(copy)

    def wait(copies):
        for copy in copies:
            net.wait_recv(copy)

    round_a = face_copies(
        gp, (slice(None),), lambda i: xa.at[i], lambda i: ya.at[i, :, :, pl.ds(0, 1)],
        zs0.at[0], lambda i: za.at[i],
    )
    start(round_a)

    def coarse_p1(x, acc):
        tmp[x] = gp[1, 2 * x + 1, 8 : 8 + Y0] + gp[1, 2 * x + 2, 8 : 8 + Y0]
        v = tmp[x, pl.ds(0, Y1, stride=2)] + tmp[x, pl.ds(1, Y1, stride=2)]
        v = 0.125 * pair_sum(v, 1, 1)
        p1[x + 1, 8 : 8 + Y1] = v
        return pack_z(acc, v, 2 * x, 2)

    clear([(p1, X1, Y1), (u1, X1, Y1), (smooth, X0, Y0)], [
        (zr, (r, i), (0, 0, d)) for zr, n in ((zr1, 2), (zr0, 1)) for r in range(n) for i, d in enumerate(signs)
    ])
    zs1[0] = loop(X1, coarse_p1, zero)
    faces_p1 = Faces(net, p1, zs1.at[0], zr1.at[0], X1, Y1)
    faces_p1.start()

    for x in range(X2):
        row, col = iota((LANES, LANES), 0), iota((LANES, LANES), 1)
        take = jnp.logical_and(col == Z2 * x + row // 4, row % 2 == 0)
        pick[pl.ds(x * LANES, LANES)] = jnp.where(take, 0.125, 0.0).astype(F32)
    row, col = iota((LANES, LANES), 0), iota((LANES, LANES), 1)
    spread[:, :LANES] = (row == Z2 + col // 4).astype(F32)
    left = jnp.logical_and(row == Z2 - 1, col >= LANES - 2)
    right = jnp.logical_and(row == 2 * Z2, col < 2)
    spread[:, LANES:] = jnp.logical_or(left, right).astype(F32)

    def compact(planes):
        parts = []
        for x in range(X2):
            tmp[x, :Y1] = planes(2 * x) + planes(2 * x + 1)
            parts.append(tmp[x, pl.ds(0, Y2, stride=2)] + tmp[x, pl.ds(1, Y2, stride=2)])
        return lax.dot_general(
            jnp.concatenate(parts, axis=1), pick[...], (((1,), (0,)), ((), ())),
            precision=lax.Precision.HIGHEST, preferred_element_type=F32,
        )

    steps = [d for k in range(1, REACH + 1) for d in (k, -k)]
    for raw in (raw_p, raw_b):
        raw[0, :, :, :4] = zeros(nx, 3, 4)
        raw[2 * REACH, :, :, 4:] = zeros(nx, 3, 4)
        for d in steps:

            @pl.when(jnp.logical_not(net.there((0, d, 0))))
            def _():
                raw[REACH + d] = zeros(nx, 3, 8)

        for d in signs:

            @pl.when(jnp.logical_not(net.there((0, 0, d))))
            def _():
                if raw is raw_p:
                    raw[REACH, ix, 1 + d] = zeros(8)
                else:
                    raw[REACH, :, 1 + d] = zeros(nx, 8)

    def along_y(raw):
        copies = []
        for d in steps:
            src, dst = raw.at[REACH], raw.at[REACH - d]
            if abs(d) == REACH:
                rows = pl.ds(4 if d > 0 else 0, 4)
                src, dst = src.at[:, :, rows], dst.at[:, :, rows]
            copies.append(net.copy(src, dst, (0, d, 0)))
        return copies

    raw_p[REACH, ix, 1] = compact(lambda x: p1[x + 1, 8 : 8 + Y1])
    p2_z = [net.copy(raw_p.at[REACH, ix, 1], raw_p.at[REACH, ix, 1 - d], (0, 0, d)) for d in (1, -1)]
    for copy in p2_z:
        net.start(copy)
    zero_halo(vn, (0,))

    wait(round_a)
    own_p = zs0[0, 1]
    cross_p = cross_z(za[0, 1], za[1, 1])
    cz[...] = 0.5 * (own_p + cross_p)
    z_part = cz[...] * cross_z(za[0, 0], za[1, 0])
    z_diag = 0.5 * cross_p
    ends = ((0, 0), (1, X0 - 1))
    rows0 = ((0, 0), (1, Y0 - 1))
    for i, x in ends:
        ph = xa[i, 1]
        c = 0.5 * (gp[1, x + 1, own0] + ph)
        st0[i, x] = c
        st0[6, x] += 0.5 * ph
        part[x] += c * xa[i, 0]

    def first_y(x, _):
        for i, y in rows0:
            row = slice(y, y + 1)
            ph = ya[i, 1, x, :1]
            c = 0.5 * (gp[1, x + 1, 8 + y : 9 + y] + ph)
            st0[2 + i, x, row] = c
            st0[6, x, row] += 0.5 * ph
            part[x, row] += c * ya[i, 0, x, :1]
        return 0

    loop(X0, first_y)

    def first_z(x, acc):
        diag = st0[6, x] + at_edges(z_diag, 4 * x, 4)
        inv = OMEGA / diag
        st0[6, x] = diag
        st0[7, x] = inv
        s = (1.0 - OMEGA) * gp[0, x + 1, own0] + inv * (part[x] + at_edges(z_part, 4 * x, 4))
        smooth[x + 1, own0] = s
        return pack_z(acc, s, 4 * x, 1)

    zs0[1, 0] = loop(X0, first_z, zero)

    round_b = Faces(net, smooth, zs0.at[1, 0], zr0.at[0], X0, Y0)
    round_b.start()

    faces_p1.wait()
    both_p1 = merge_z(zr1[0], 2)

    def sides1(field, x, halo):
        v = field[x + 1, 8 : 8 + Y1]
        return v, sides(field, x, Y1, 8, 1, *z_sides(v, halo, 2))

    def couple1(x, _):
        p, ns = sides1(p1, x, unpack_z(both_p1, 2 * x, 2, 2))
        cs, diag = couplings(0.125, p, ns)
        for i, c in enumerate(cs):
            st1[i, x] = c
        st1[6, x] = diag
        st1[7, x] = OMEGA / diag
        return 0

    loop(X1, couple1)

    pack_d[...] = loop(X0, lambda x, acc: pack_z(acc, st0[6, x], 4 * x, 1), zero)

    round_b.wait()

    def remainder0(field, x, z_sum):
        v, vs = inside0(field, x)
        return rhs[x] - st0[6, x] * v + sum0(x, vs) + at_edges(z_sum, 4 * x, 4)

    sum_s = cz[...] * cross_z(zr0[0, 0], zr0[0, 1])

    def down0(x, acc):
        tmp[x] = remainder0(smooth, 2 * x, sum_s) + remainder0(smooth, 2 * x + 1, sum_s)
        b = tmp[x, pl.ds(0, Y1, stride=2)] + tmp[x, pl.ds(1, Y1, stride=2)]
        b = 0.125 * pair_sum(b, 1, 1)
        b1[x] = b
        u = st1[7, x] * b
        u1[x + 1, 8 : 8 + Y1] = u
        return pack_z(acc, u, 2 * x, 2)

    zs1[1] = loop(X1, down0, zero)

    round_c = Faces(net, u1, zs1.at[1], zr1.at[1], X1, Y1)
    round_c.start()

    for copy in p2_z:
        net.wait_recv(copy)
    p2_x = [net.copy(raw_p.at[REACH, ix], raw_p.at[REACH, ix], (0, 0, 0), k) for k in range(1, nx)]
    start(p2_x)

    clear([], landings(xd, yd, zd) + landings(xf, yf, zf) + edge_landings(exy, exz, eyz) + edge_landings(pxy, pxz, pyz))
    static = edge_copies(gp, (1,), zs0.at[0, 1], pxy, pxz, pyz)
    for i, d in ((1, 1), (0, -1)):
        static.append(net.copy(pack_d, zd.at[1 - i], (0, 0, d)))
        static.append(net.copy(st0.at[6, X0 - 1 if i else 0], xd.at[1 - i], (d, 0, 0)))
        static.append(net.copy(
            st0.at[6, :, pl.ds(Y0 - 1 if i else 0, 1)], yd.at[1 - i, :, pl.ds(0, 1)], (0, d, 0)
        ))
    start(static)

    round_c.wait()
    both_u = merge_z(zr1[1], 2)

    def remainder1(x):
        u, us = sides1(u1, x, unpack_z(both_u, 2 * x, 2, 2))
        return b1[x] - st1[6, x] * u + weighted([st1[i, x] for i in range(6)], us)

    raw_b[REACH, ix, 1] = compact(remainder1)

    mine = raw_b.at[REACH, ix, 1]
    b2_xz = []
    for d in (1, -1, 0):
        for k in range(nx):
            if d or k:
                b2_xz.append(net.copy(mine, raw_b.at[REACH, ix, 1 - d], (0, 0, d), k))
    for copy in b2_xz:
        net.start(copy)

    for copy in p2_x:
        net.wait_recv(copy)
    p2_y = along_y(raw_p)
    start(p2_y)

    wait(static)
    lane8, row8 = iota((8, LANES), 1), iota((8, LANES), 0)

    def inverse(p, diag):
        inside = p > 0.0
        return jnp.where(inside, OMEGA / jnp.where(inside, diag, 1.0), 0.0)

    def to_z_faces(x_edges, y_edges):
        return (
            roll(x_edges[0], 8, 1), roll(x_edges[1], LANES - 8, 1),
            roll(roll(y_edges[0], LANES - 6, 1), 1, 0), roll(roll(y_edges[1], 6, 1), 7, 0),
        )

    quarter = (lane8 // 2) % 4
    z_masks = (
        lane8 < 8, lane8 >= LANES - 8,
        jnp.logical_and(quarter == 0, row8 == 0), jnp.logical_and(quarter == 3, row8 == 7),
    )
    far_x = ((0, X0 - 1), (1, 0))
    far_y = ((0, 3, 7), (1, 0, 0))
    kz[...] = inverse(cross_p, cross_z(zd[0], zd[1]))
    edge_x = [cross_z(pxz[i, 0], pxz[i, 1]) for i in range(2)]
    edge_y = [cross_z(pyz[i, 0], pyz[i, 1]) for i in range(2)]
    for n, (mask, p) in enumerate(zip(z_masks, to_z_faces(edge_x, edge_y))):
        rims[n] = jnp.where(mask, 0.5 * (cross_p + p), 0.0)
    edge_lane = jnp.logical_or(lane0 == 0, lane0 == LANES - 1)
    for i, x in far_x:
        ph = xa[i, 1]
        kx[i] = inverse(ph, xd[i])
        cxz[i] = jnp.where(edge_lane, 0.5 * (ph + at_edges(edge_x[i], 4 * x, 4)), 0.0)
        for j, y in rows0:
            rims[4 + 2 * i + j, :1] = 0.5 * (ph[y : y + 1] + pxy[i, j, :1])
    for i, j, r in far_y:
        crossed[i] = edge_y[i]
        for k, x in ends:
            rims[8 + 2 * i + k, :1] = 0.5 * (ya[i, 1, x, :1] + pxy[k, i, :1])

    edge_row = jnp.logical_or(iota((1, LANES), 1) == 0, iota((1, LANES), 1) == LANES - 1)

    def edge_of_y(packed, x, j):
        return roll(packed, LANES - (2 * (4 * x + j) + 1), 1)

    def static_y(x, _):
        for i, j, r in far_y:
            ph = ya[i, 1, x, :1]
            ky[i, x, :1] = inverse(ph, yd[i, x, :1])
            p = edge_of_y(crossed[i, r : r + 1], x, j)
            cyz[i, x, :1] = jnp.where(edge_row, 0.5 * (ph + p), 0.0)
        return 0

    loop(X0, static_y)

    wait(b2_xz)
    b2_y = along_y(raw_b)
    start(b2_y)

    for f in (p2, u2, p3, u3, v3, p4, wa, wb):
        n = f.shape[0]
        f[0] = jnp.zeros(f.shape[1:], F32)
        f[n - 1] = jnp.zeros(f.shape[1:], F32)

        def pad(x, _):
            f[x, :8] = jnp.zeros((8, LANES), F32)
            f[x, 8 + ROWS :] = jnp.zeros((8, LANES), F32)
            return 0

        loop(n, pad)
    for f in (v2, w2):
        loop(f.shape[0], lambda x, _: f.__setitem__(x, jnp.zeros(f.shape[1:], F32)) or 0)

    def region(raw, xd, x):
        lane = iota((ROWS, LANES), 1)
        part = [
            roll(raw[:, xd, zd].reshape(ROWS, LANES), Z2 * (zd - x), 1) for zd in range(3)
        ]
        return jnp.where(lane < Z2, part[0], jnp.where(lane < 2 * Z2, part[1], jnp.where(lane < 3 * Z2, part[2], 0.0)))

    for copy in p2_y:
        net.wait_recv(copy)

    def unpack_p(xd, _):
        for x in range(X2):
            p2[X2 * xd + x + 1, 8 : 8 + ROWS] = region(raw_p, xd, x)
        return 0

    loop(nx, unpack_p)

    def coarse(v, step):
        return 0.125 * pair_sum(pair_sum(v, step, 0), step, 1)

    def coarse_p(src, dst, step):
        def one(x, _):
            v = src[2 * x + 1, 8 : 8 + ROWS] + src[2 * x + 2, 8 : 8 + ROWS]
            dst[x + 1, 8 : 8 + ROWS] = coarse(v, step)
            return 0

        loop(dst.shape[0] - 2, one)

    coarse_p(p2, p3, 1)
    coarse_p(p3, p4, 2)

    def region_sides(field, x, step, first=8, rows=ROWS):
        v = field[x + 1, pl.ds(first, rows)]
        return v, sides(field, x, rows, first, step, roll(v, step, 1), roll(v, LANES - step, 1))

    def couple_region(p_ref, st, step, scale):
        def one(x, _):
            p, ns = region_sides(p_ref, x, step)
            cs, diag = couplings(scale, p, ns)
            for i, c in enumerate(cs):
                st[i, x] = c
            inside = p > 0.0
            st[6, x] = diag
            st[7, x] = jnp.where(inside, OMEGA / jnp.where(inside, diag, 1.0), 0.0)
            return 0

        loop(p_ref.shape[0] - 2, one)

    couple_region(p2, st2, 1, 0.5 / 16)
    couple_region(p3, st3, 2, 0.5 / 64)
    couple_region(p4, st4, 4, 0.5 / 256)

    for copy in b2_y:
        net.wait_recv(copy)

    def unpack_b(xd, _):
        for x in range(X2):
            at = X2 * xd + x
            b = region(raw_b, xd, x)
            b2[at] = b
            u2[at + 1, 8 : 8 + ROWS] = st2[7, at] * b
        return 0

    loop(nx, unpack_b)

    def remainder(u_ref, b_ref, st, x, step):
        u, us = region_sides(u_ref, x, step)
        return b_ref[x] - st[6, x] * u + weighted([st[i, x] for i in range(6)], us)

    def down(u_ref, b_ref, st, step, next_b, next_u, next_st):
        def one(x, _):
            r = remainder(u_ref, b_ref, st, 2 * x, step) + remainder(u_ref, b_ref, st, 2 * x + 1, step)
            b = coarse(r, step)
            next_b[x] = b
            next_u[x + 1, 8 : 8 + ROWS] = next_st[7, x] * b
            return 0

        loop(next_b.shape[0], one)

    down(u2, b2, st2, 1, b3, u3, st3)
    down(u3, b3, st3, 2, b4, wa, st4)

    def relaxed(field, b, st, x, step, first=8, rows=ROWS, at=0):
        v, vs = region_sides(field, x, step, first, rows)
        s = weighted([st[i, x, at : at + rows] for i in range(6)], vs)
        return (1.0 - OMEGA) * v + st[7, x, at : at + rows] * (b[x, at : at + rows] + s)

    for src, dst in ((wa, wb), (wb, wa), (wa, wb)):

        def sweep(x, _):
            dst[x + 1, 8 : 8 + ROWS] = relaxed(src, b4, st4, x, 4)
            return 0

        loop(nx, sweep)

    near, span = OWN - 8, 24

    def up3(x, _):
        v3[x + 1, 8 : 8 + ROWS] = u3[x + 1, 8 : 8 + ROWS] + wb[x // 2 + 1, 8 : 8 + ROWS]
        return 0

    loop(2 * nx, up3)

    def relax3(x, _):
        w3[x] = relaxed(v3, b3, st3, x, 2, 8 + near, span, near)
        return 0

    loop(2 * nx, relax3)

    def up2(x, _):
        v2[x + 1, 8 : 8 + span] = u2[x + 1, 8 + near : 8 + near + span] + w3[x // 2]
        return 0

    loop(4 * nx, up2)

    def relax2(x, _):
        w2[x + 1] = relaxed(v2, b2, st2, x, 1, 8, span, near)
        return 0

    loop(4 * nx, relax2)

    wide = lax.dot_general(
        w2[pl.ds(X2 * ix, X2 + 2)].reshape((X2 + 2) * span, LANES), spread[...], (((1,), (0,)), ((), ())),
        precision=lax.Precision.HIGHEST, preferred_element_type=F32,
    ).reshape(X2 + 2, span, 2 * LANES)
    for x in range(X1 + 2):
        m = wide[(x + 1) // 2, :, :LANES]
        rw1[x, pl.ds(8, Y2, stride=2)] = m[8 : 8 + Y2]
        rw1[x, pl.ds(9, Y2, stride=2)] = m[8 : 8 + Y2]
        rw1[x, 7:8] = m[7:8]
        rw1[x, 8 + Y1 : 9 + Y1] = m[8 + Y2 : 9 + Y2]
        v1[x] = u1[x] + rw1[x]
    for x in range(X2):
        h = wide[x + 1, 8 : 8 + Y2, LANES:]
        hw1[x, pl.ds(0, Y2, stride=2)] = h
        hw1[x, pl.ds(1, Y2, stride=2)] = h

    def up1(x, acc):
        halo = unpack_z(both_u, 2 * x, 2, 2) + hw1[x // 2]
        v, vs = sides1(v1, x, halo)
        w = (1.0 - OMEGA) * v + st1[7, x] * (b1[x] + weighted([st1[i, x] for i in range(6)], vs))
        rw0[x, pl.ds(0, Y1, stride=2)] = w
        rw0[x, pl.ds(1, Y1, stride=2)] = w
        for d in range(2):
            v = smooth[2 * x + d + 1, own0] + rw0[x]
            vn[0, 2 * x + d + 1, own0] = v
            acc = pack_z(acc, v, 4 * (2 * x + d), 1)
        return acc

    zs0[2, 0] = loop(X1, up1, zero)

    round_f = edge_copies(vn, (0,), zs0.at[2, 0], exy, exz, eyz)
    round_f += face_copies(
        vn, (0,), lambda i: xf.at[i, 0], lambda i: yf.at[i, 0, :, pl.ds(0, 1)],
        zs0.at[2, 0], lambda i: zf.at[i, 0],
    )
    start(round_f)

    def last_part(x, acc):
        _, vs = inside0(vn, x, (0,))
        n = rhs[x] + sum0(x, vs)
        vn[1, x + 1, own0] = n
        part[x] = n
        return pack_z(acc, n, 4 * x, 1)

    zs0[2, 1] = loop(X0, last_part, zero)
    round_n = face_copies(
        vn, (1,), lambda i: xf.at[i, 1], lambda i: yf.at[i, 1, :, pl.ds(0, 1)],
        zs0.at[2, 1], lambda i: zf.at[i, 1],
    )
    start(round_n)
    wait(round_f)
    wait(round_n)

    edge_x = [cross_z(exz[i, 0], exz[i, 1]) for i in range(2)]
    edge_y = [cross_z(eyz[i, 0], eyz[i, 1]) for i in range(2)]
    cross_v = cross_z(zf[0, 0], zf[1, 0])
    n = cross_z(zf[0, 1], zf[1, 1]) + cz[...] * zs0[2, 0]
    for k, v in enumerate(to_z_faces(edge_x, edge_y)):
        n = n + rims[k] * v
    sum_x = cz[...] * ((1.0 - OMEGA) * cross_v + kz[...] * n)
    z_part = cz[...] * cross_v
    row0 = iota((Y0, LANES), 0)
    for (i, x), (_, far) in zip(ends, far_x):
        vh = xf[i, 0]
        n = xf[i, 1] + st0[i, x] * vn[0, x + 1, own0] + cxz[i] * at_edges(edge_x[i], 4 * far, 4)
        for j, y in rows0:
            n = n + jnp.where(row0 == y, rims[4 + 2 * i + j, :1] * exy[i, j, :1], 0.0)
        sol[X0 + 1 if i else 0, own0] = (1.0 - OMEGA) * vh + kx[i] * n
        part[x] += st0[i, x] * vh
    for i, j, r in far_y:
        crossed[i] = edge_y[i]
        for k, x in ends:
            yf[i, 1, x, :1] += rims[8 + 2 * i + k, :1] * exy[k, i, :1]

    def last_y(x, _):
        for (i, y), (_, j, r) in zip(rows0, far_y):
            row = slice(y, y + 1)
            vh = yf[i, 0, x, :1]
            c = st0[2 + i, x, row]
            n = yf[i, 1, x, :1] + c * vn[0, x + 1, 8 + y : 9 + y]
            n = n + cyz[i, x, :1] * edge_of_y(crossed[i, r : r + 1], x, j)
            at = 8 + Y0 if i else 7
            sol[x + 1, at : at + 1] = (1.0 - OMEGA) * vh + ky[i, x, :1] * n
            part[x, row] += c * vh
        return 0

    loop(X0, last_y)

    def last_z(x, _):
        n = part[x] + at_edges(z_part, 4 * x, 4)
        sol[x + 1, own0] = (1.0 - OMEGA) * vn[0, x + 1, own0] + st0[7, x] * n
        return 0

    loop(X0, last_z)
    out_sol = pltpu.make_async_copy(sol.at[inner0], sol_hbm, local_sems.at[3])
    out_sol.start()

    def residual(x, _):
        res[x] = remainder0(sol, x, sum_x)
        return 0

    loop(X0, residual)
    out_res = pltpu.make_async_copy(res, res_hbm, local_sems.at[4])
    out_res.start()
    net.finish()
    out_sol.wait()
    out_res.wait()


def scratch(nx):
    def vmem(*shape):
        return pltpu.VMEM(shape + (LANES,), F32)

    padded0 = (X0 + 2, Y0 + 16)
    padded1 = (X1 + 2, Y1 + 16)
    n2, n3, n4, tall = 4 * nx, 2 * nx, nx, ROWS + 16
    reach = 2 * REACH + 1
    return [
        vmem(X0, Y0), vmem(2, *padded0), vmem(*padded0), vmem(2, *padded0), vmem(*padded0), vmem(X0, Y0),
        vmem(8, X0, Y0), vmem(3, 2, 8), vmem(1, 2, 8), vmem(X0, Y0), vmem(8), vmem(8),
        vmem(2, 2, Y0), vmem(2, 2, X0, 8), vmem(2, 2, 8), vmem(2, Y0), vmem(2, X0, 8), vmem(2, 8),
        vmem(2, 2, Y0), vmem(2, 2, X0, 8), vmem(2, 2, 8),
        vmem(2, 2, 8), vmem(2, 2, 8), vmem(2, 2, 8), vmem(2, 2, 8), vmem(2, 2, 8), vmem(2, 2, 8),
        vmem(2, Y0), vmem(2, X0, 8), vmem(8), vmem(2, Y0), vmem(2, X0, 8), vmem(12, 8), vmem(2, 8),
        vmem(*padded1), vmem(*padded1), vmem(*padded1), vmem(*padded1), vmem(X1, Y1), vmem(8, X1, Y1),
        vmem(X1, Y0), vmem(X2, Y1), vmem(X1, Y0), vmem(2, 8), vmem(2, 2, 8),
        vmem(X2 * LANES), pltpu.VMEM((LANES, 2 * LANES), F32),
        vmem(reach, nx, 3, 8), vmem(reach, nx, 3, 8),
        vmem(n2 + 2, tall), vmem(n2 + 2, tall), vmem(n2, ROWS), vmem(8, n2, ROWS),
        vmem(n3 + 2, tall), vmem(n3 + 2, tall), vmem(n3 + 2, tall), vmem(n3, ROWS), vmem(8, n3, ROWS),
        vmem(n4 + 2, tall), vmem(n4 + 2, tall), vmem(n4 + 2, tall), vmem(n4, ROWS), vmem(8, n4, ROWS),
        vmem(n3, 24), vmem(n2 + 2, 40), vmem(n2 + 2, 24),
        pltpu.SemaphoreType.DMA((5,)), pltpu.SemaphoreType.DMA((SEMS,)), pltpu.SemaphoreType.DMA((SEMS,)),
    ]


def solution(mesh):
    sizes = tuple(mesh.shape[a] for a in ("gx", "gy", "gz"))
    block = jax.ShapeDtypeStruct((X0, Y0, LANES), F32)
    spec = P("gx", "gy", "gz")

    def shards(right_side, dielectric, guess):
        return pl.pallas_call(
            functools.partial(kernel, sizes),
            out_shape=(block, block),
            in_specs=[pl.BlockSpec(memory_space=pl.ANY)] * 3,
            out_specs=[pl.BlockSpec(memory_space=pl.ANY)] * 2,
            scratch_shapes=scratch(sizes[0]),
            compiler_params=pltpu.CompilerParams(
                collective_id=0, has_side_effects=True, vmem_limit_bytes=60 * 2**20
            ),
            name="vcycle",
        )(right_side, dielectric, guess)

    return jax.shard_map(
        shards, mesh=mesh, in_specs=(spec, spec, spec), out_specs=(spec, spec), check_vma=False
    )
```

```python
import functools

import jax
import jax.numpy as jnp
from jax import lax
from jax.experimental import pallas as pl
from jax.experimental.pallas import tpu as pltpu
from jax.sharding import PartitionSpec as P

OMEGA = 0.8
MESH = pl.DeviceIdType.MESH
F32 = jnp.float32

X0, Y0, LANES = 16, 32, 128
X1, Y1 = 8, 16
X2, Y2, Z2 = 4, 8, 32
REACH = 3
ROWS = (2 * REACH + 1) * Y2
OWN = REACH * Y2


def iota(shape, dim):
    return lax.broadcasted_iota(jnp.int32, shape, dim)


def roll(v, shift, axis):
    size = v.shape[axis]
    if isinstance(shift, int):
        shift = shift % size
        if shift == 0:
            return v
    return pltpu.roll(v, shift, axis=axis)


def loop(count, body, init=0, unroll=True):
    return lax.fori_loop(0, count, body, init, unroll=unroll)


class Faces:
    def __init__(self, net, field, into, sent, got, nx, ny):
        self.net = net
        self.copies = {}
        lead = (slice(None),) * (len(field.shape) - 3)
        for d in (-1, 1):
            src, dst = (1, nx + 1) if d < 0 else (nx, 0)
            self.copies[(d, 0, 0)] = net.copy(
                field.at[lead + (src, pl.ds(8, ny))], into.at[lead + (dst, pl.ds(8, ny))], (d, 0, 0)
            )
            src, dst = (8, 8 + ny) if d < 0 else (7 + ny, 7)
            self.copies[(0, d, 0)] = net.copy(
                field.at[lead + (pl.ds(1, nx), pl.ds(src, 1))],
                into.at[lead + (pl.ds(1, nx), pl.ds(dst, 1))],
                (0, d, 0),
            )
            self.copies[(0, 0, d)] = net.copy(sent, got.at[0 if d > 0 else 1], (0, 0, d))

    def start(self):
        for way in ((0, 0, 1), (0, 0, -1), (1, 0, 0), (-1, 0, 0), (0, 1, 0), (0, -1, 0)):
            self.net.start(self.copies[way])

    def wait(self):
        for copy in self.copies.values():
            self.net.wait_recv(copy)


class Net:
    def __init__(self, sizes, send_sems, recv_sems):
        self.me = tuple(lax.axis_index(a) for a in ("gx", "gy", "gz"))
        self.sizes = sizes
        self.send_sems, self.recv_sems = send_sems, recv_sems
        self.used = 0
        self.started = []

    def there(self, way):
        found = None
        for at, size, d in zip(self.me, self.sizes, way):
            if d:
                ok = (at + d < size) if d > 0 else (at + d >= 0)
                found = ok if found is None else jnp.logical_and(found, ok)
        return found

    def when(self, way):
        found = self.there(way)
        return (lambda f: f()) if found is None else pl.when(found)

    def device(self, way, turn=0):
        x = self.me[0] + way[0]
        if turn:
            x = lax.rem(x + turn, self.sizes[0])
        return (x, self.me[1] + way[1], self.me[2] + way[2])

    def copy(self, src, dst, way, turn=0):
        i = self.used
        self.used += 1
        made = pltpu.make_async_remote_copy(
            src_ref=src,
            dst_ref=dst,
            send_sem=self.send_sems.at[i],
            recv_sem=self.recv_sems.at[i],
            device_id=self.device(way, turn),
            device_id_type=MESH,
        )
        return (made, way)

    def start(self, copy):
        made, way = copy
        self.started.append(copy)

        @self.when(way)
        def _():
            made.start()

    def wait_recv(self, copy):
        made, way = copy

        @self.when(tuple(-d for d in way))
        def _():
            made.wait_recv()

    def finish(self):
        for made, way in self.started:

            @self.when(way)
            def _():
                made.wait_send()


SEMS = 104


def pack_z(acc, v, first, w):
    group = iota((8, LANES), 1) // (2 * w)
    for j in range(v.shape[0] // 8):
        k = first + j
        acc = jnp.where(group == k, roll(v[8 * j : 8 * j + 8], (2 * k + 1) * w, 1), acc)
    return acc


def cross_z(left, right):
    odd = iota((8, LANES), 1) % 2 == 1
    return jnp.where(odd, roll(left, 1, 1), roll(right, LANES - 1, 1))


def at_edges(packed, first, tiles):
    v = jnp.concatenate([roll(packed, LANES - (2 * (first + j) + 1), 1) for j in range(tiles)], axis=0)
    lane = iota(v.shape, 1)
    return jnp.where(jnp.logical_or(lane == 0, lane == LANES - 1), v, 0.0)


def merge_z(got, w):
    return jnp.where((iota((8, LANES), 1) // w) % 2 == 0, got[0], got[1])


def unpack_z(both, first, tiles, w):
    return jnp.concatenate([roll(both, LANES - (2 * (first + j) + 1) * w, 1) for j in range(tiles)], axis=0)


def z_sides(v, halo, w):
    lane = iota(v.shape, 1)
    below = roll(jnp.where(lane >= LANES - w, halo, v), w, 1)
    above = roll(jnp.where(lane < w, halo, v), LANES - w, 1)
    return below, above


def sides(field, x, rows, first, step, below, above, lead=()):
    f = lambda dx, dy: field[lead + (x + 1 + dx, pl.ds(first + dy, rows))]
    return (f(-1, 0), f(1, 0), f(0, -step), f(0, step), below, above)


def weighted(cs, vs):
    total = cs[0] * vs[0]
    for c, v in zip(cs[1:], vs[1:]):
        total = total + c * v
    return total


def pair_sum(v, step, axis):
    even = (iota(v.shape, axis) // step) % 2 == 0
    size = v.shape[axis]
    return v + jnp.where(even, roll(v, size - step, axis), roll(v, step, axis))


def kernel(
    sizes,
    rhs_hbm, permit_hbm, guess_hbm,
    sol_hbm, res_hbm,
    rhs, gp, smooth, vn, sol, res, st0, zs0, zr0, part, pack_d, cz,
    xa, ya, za, xd, yd, zd, xf, yf, zf, exy, exz, eyz, pxy, pxz, pyz,
    kx, ky, kz, cxz, cyz, rims, crossed,
    p1, u1, u1h, v1, rw1, b1, st1, tmp, hw1, rw0, zs1, zr1, pick, spread, lhs, select,
    raw_p, raw_b, raw_e, p2, u2, b2, st2, p3, u3, v3, b3, st3, p4, wa, wb, b4, st4, w3, v2, w2,
    local_sems, send_sems, recv_sems,
):
    nx = sizes[0]
    net = Net(sizes, send_sems, recv_sems)
    ix, iy, iz = net.me
    inner0 = (pl.ds(1, X0), pl.ds(8, Y0))
    own0 = slice(8, 8 + Y0)

    loads = [
        pltpu.make_async_copy(guess_hbm, gp.at[(0,) + inner0], local_sems.at[0]),
        pltpu.make_async_copy(permit_hbm, gp.at[(1,) + inner0], local_sems.at[1]),
        pltpu.make_async_copy(rhs_hbm, rhs, local_sems.at[2]),
    ]
    for load in loads:
        load.start()

    ways = [(0, 0, 1), (0, 0, -1), (1, 0, 0), (-1, 0, 0), (0, 1, 0), (0, -1, 0)]
    greeted = ways + [(2, 0, 0), (-2, 0, 0)]
    barrier = pltpu.get_barrier_semaphore()
    for way in greeted:

        @net.when(way)
        def _():
            pl.semaphore_signal(barrier, inc=1, device_id=net.device(way), device_id_type=MESH)

    signs = (-1, 1)
    zeros = lambda *shape: jnp.zeros(shape + (LANES,), F32)

    def clear(fields, landings):
        todo = {}
        for f, fx, fy in fields:
            for i, d in enumerate(signs):
                todo.setdefault((d, 0, 0), []).append((f, (fx + 1 if i else 0,)))
                todo.setdefault((0, d, 0), []).append((f, (pl.ds(1, fx), pl.ds(8 + fy if i else 7, 1))))
        for ref, at, way in landings:
            todo.setdefault(way, []).append((ref, at))
        for way, items in todo.items():

            @pl.when(jnp.logical_not(net.there(way)))
            def _():
                for ref, at in items:
                    ref[at] = jnp.zeros(ref.at[at].shape, F32)

    def landings(x, y, z):
        return [(ref, (i,), tuple(d if n == axis else 0 for n in range(3)))
                for axis, ref in enumerate((x, y, z)) for i, d in enumerate(signs)]

    def edge_landings(xy, xz, yz):
        out = []
        for i, d in enumerate(signs):
            for j, e in enumerate(signs):
                out += [(xy, (i, j), (d, e, 0)), (xz, (i, j), (d, 0, e)), (yz, (i, j), (0, d, e))]
        return out

    def zero_halo(f, lead=(), fx=X0, fy=Y0):
        for x in (0, fx + 1):
            f[lead + (x,)] = zeros(fy + 16)

        def one(x, _):
            f[lead + (x + 1, slice(0, 8))] = zeros(8)
            f[lead + (x + 1, slice(8 + fy, 16 + fy))] = zeros(8)
            return 0

        loop(fx, one)

    zero_halo(gp, (0,))
    zero_halo(gp, (1,))
    clear([], landings(xa, ya, za))

    for load in loads:
        load.wait()

    lane0 = iota((Y0, LANES), 1)

    def couplings(scale, p, ns):
        cs = [scale * (p + n) for n in ns]
        return cs, cs[0] + cs[1] + cs[2] + cs[3] + cs[4] + cs[5]

    def inside0(field, x, lead=()):
        v = field[lead + (x + 1, pl.ds(8, Y0))]
        return v, sides(field, x, Y0, 8, 1, roll(v, 1, 1), roll(v, LANES - 1, 1), lead=lead)

    def sum0(x, vs):
        return weighted([st0[i, x] for i in range(6)], vs)

    def first(x, accs):
        p, ns = inside0(gp, x, (1,))
        ns = ns[:4] + (jnp.where(lane0 == 0, 0.0, ns[4]), jnp.where(lane0 == LANES - 1, 0.0, ns[5]))
        cs, diag = couplings(0.5, p, ns)
        cs[4] = jnp.where(lane0 == 0, 0.0, cs[4])
        cs[5] = jnp.where(lane0 == LANES - 1, 0.0, cs[5])
        for i, c in enumerate(cs):
            st0[i, x] = c
        st0[6, x] = diag
        v, vs = inside0(gp, x, (0,))
        part[x] = rhs[x] + weighted(cs, vs)
        return pack_z(accs[0], v, 4 * x, 1), pack_z(accs[1], p, 4 * x, 1)

    zero = zeros(8)
    accs = loop(X0, first, (zero, zero))
    zs0[0, 0] = accs[0]
    zs0[0, 1] = accs[1]

    pl.semaphore_wait(barrier, sum(net.there(way).astype(jnp.int32) for way in greeted))

    def face_copies(field, lead, x_to, y_to, z_from, z_to):
        copies = []
        for i, d in ((1, 1), (0, -1)):
            copies.append(net.copy(z_from, z_to(1 - i), (0, 0, d)))
        for i, d in ((1, 1), (0, -1)):
            copies.append(net.copy(field.at[lead + (X0 if i else 1, pl.ds(8, Y0))], x_to(1 - i), (d, 0, 0)))
        for i, d in ((1, 1), (0, -1)):
            row = 7 + Y0 if i else 8
            copies.append(net.copy(field.at[lead + (pl.ds(1, X0), pl.ds(row, 1))], y_to(1 - i), (0, d, 0)))
        return copies

    def edge_copies(field, lead, packed, xy, xz, yz):
        copies = []
        for i, d in enumerate(signs):
            for j, e in enumerate(signs):
                copies.append(net.copy(packed, xz.at[1 - i, 1 - j], (d, 0, e)))
                copies.append(net.copy(packed, yz.at[1 - i, 1 - j], (0, d, e)))
        for i, d in enumerate(signs):
            for j, e in enumerate(signs):
                line = field.at[lead + (X0 if i else 1, pl.ds(7 + Y0 if j else 8, 1))]
                copies.append(net.copy(line, xy.at[1 - i, 1 - j, pl.ds(0, 1)], (d, e, 0)))
        return copies

    def start(copies):
        for copy in copies:
            net.start(copy)

    def wait(copies):
        for copy in copies:
            net.wait_recv(copy)

    round_a = face_copies(
        gp, (slice(None),), lambda i: xa.at[i], lambda i: ya.at[i, :, :, pl.ds(0, 1)],
        zs0.at[0], lambda i: za.at[i],
    )
    start(round_a)

    def coarse_p1(x, acc):
        tmp[x] = gp[1, 2 * x + 1, 8 : 8 + Y0] + gp[1, 2 * x + 2, 8 : 8 + Y0]
        v = tmp[x, pl.ds(0, Y1, stride=2)] + tmp[x, pl.ds(1, Y1, stride=2)]
        v = 0.125 * pair_sum(v, 1, 1)
        p1[x + 1, 8 : 8 + Y1] = v
        return pack_z(acc, v, 2 * x, 2)

    clear([(p1, X1, Y1), (u1h, X1, Y1), (smooth, X0, Y0)], [
        (zr, (r, i), (0, 0, d)) for zr, n in ((zr1, 2), (zr0, 1)) for r in range(n) for i, d in enumerate(signs)
    ])
    zs1[0] = loop(X1, coarse_p1, zero)
    faces_p1 = Faces(net, p1, p1, zs1.at[0], zr1.at[0], X1, Y1)
    faces_p1.start()

    for x in range(X2):
        row, col = iota((LANES, LANES), 0), iota((LANES, LANES), 1)
        take = jnp.logical_and(col == Z2 * x + row // 4, row % 2 == 0)
        pick[pl.ds(x * LANES, LANES)] = jnp.where(take, 0.125, 0.0).astype(F32)
    row, col = iota((LANES, LANES), 0), iota((LANES, LANES), 1)
    spread[:, :LANES] = (row == Z2 + col // 4).astype(F32)
    left = jnp.logical_and(row == Z2 - 1, col >= LANES - 2)
    right = jnp.logical_and(row == 2 * Z2, col < 2)
    spread[:, LANES:] = jnp.logical_or(left, right).astype(F32)

    row, col = iota((LANES, LANES), 0), iota((LANES, LANES), 1)
    group, place = col // Z2, col % Z2
    for n, chosen in enumerate((
        jnp.logical_and(group == 0, row == col + Z2),
        jnp.logical_and(group == 3, row == col - 3 * Z2),
        jnp.logical_and(place == 0, row == 3 * Z2 + X2 + group),
        jnp.logical_and(place == Z2 - 1, row == 3 * Z2 + group),
    )):
        select[:, n * LANES : (n + 1) * LANES] = chosen.astype(F32)

    def to_compact(parts):
        return lax.dot_general(
            parts, pick[...], (((1,), (0,)), ((), ())),
            precision=lax.Precision.HIGHEST, preferred_element_type=F32,
        )

    def compact(planes):
        parts = []
        for x in range(X2):
            tmp[x, :Y1] = planes(2 * x) + planes(2 * x + 1)
            parts.append(tmp[x, pl.ds(0, Y2, stride=2)] + tmp[x, pl.ds(1, Y2, stride=2)])
        return to_compact(jnp.concatenate(parts, axis=1))

    steps = [d for k in range(1, REACH + 1) for d in (k, -k)]
    raw_p[0, :, :, :4] = zeros(nx, 3, 4)
    raw_p[2 * REACH, :, :, 4:] = zeros(nx, 3, 4)
    raw_e[0, :, :, :12] = zeros(nx, 3, 12)
    raw_e[2 * REACH, :, :, 12:] = zeros(nx, 3, 12)
    for d in steps:

        @pl.when(jnp.logical_not(net.there((0, d, 0))))
        def _():
            raw_p[REACH + d] = zeros(nx, 3, 8)
            raw_e[REACH + d] = zeros(nx, 3, 24)

    for d in signs:

        @pl.when(jnp.logical_not(net.there((0, 0, d))))
        def _():
            raw_p[REACH, ix, 1 + d] = zeros(8)
            raw_b[:, 1 + d] = zeros(nx, 24)

    def along_y(raw, first, rows, half):
        copies = []
        for d in steps:
            span = pl.ds(first, rows)
            if abs(d) == REACH:
                span = pl.ds(first + rows - half if d > 0 else first, half)
            copies.append(net.copy(raw.at[REACH, :, :, span], raw.at[REACH - d, :, :, span], (0, d, 0)))
        return copies

    raw_p[REACH, ix, 1] = compact(lambda x: p1[x + 1, 8 : 8 + Y1])
    p2_z = [net.copy(raw_p.at[REACH, ix, 1], raw_p.at[REACH, ix, 1 - d], (0, 0, d)) for d in (1, -1)]
    for copy in p2_z:
        net.start(copy)
    zero_halo(vn, (0,))
    zero_halo(u1, (), X1, Y1)
    lhs[...] = jnp.zeros(lhs.shape, F32)

    wait(round_a)
    own_p = zs0[0, 1]
    cross_p = cross_z(za[0, 1], za[1, 1])
    cz[...] = 0.5 * (own_p + cross_p)
    z_part = cz[...] * cross_z(za[0, 0], za[1, 0])
    z_diag = 0.5 * cross_p
    ends = ((0, 0), (1, X0 - 1))
    rows0 = ((0, 0), (1, Y0 - 1))
    for i, x in ends:
        ph = xa[i, 1]
        c = 0.5 * (gp[1, x + 1, own0] + ph)
        st0[i, x] = c
        st0[6, x] += 0.5 * ph
        part[x] += c * xa[i, 0]

    def first_y(x, _):
        for i, y in rows0:
            row = slice(y, y + 1)
            ph = ya[i, 1, x, :1]
            c = 0.5 * (gp[1, x + 1, 8 + y : 9 + y] + ph)
            st0[2 + i, x, row] = c
            st0[6, x, row] += 0.5 * ph
            part[x, row] += c * ya[i, 0, x, :1]
        return 0

    loop(X0, first_y)

    def first_z(x, acc):
        diag = st0[6, x] + at_edges(z_diag, 4 * x, 4)
        inv = OMEGA / diag
        st0[6, x] = diag
        st0[7, x] = inv
        s = (1.0 - OMEGA) * gp[0, x + 1, own0] + inv * (part[x] + at_edges(z_part, 4 * x, 4))
        smooth[x + 1, own0] = s
        return pack_z(acc, s, 4 * x, 1)

    zs0[1, 0] = loop(X0, first_z, zero)

    round_b = Faces(net, smooth, smooth, zs0.at[1, 0], zr0.at[0], X0, Y0)
    round_b.start()

    faces_p1.wait()
    both_p1 = merge_z(zr1[0], 2)

    def sides1(field, x, halo):
        v = field[x + 1, 8 : 8 + Y1]
        return v, sides(field, x, Y1, 8, 1, *z_sides(v, halo, 2))

    def couple1(x, _):
        p, ns = sides1(p1, x, unpack_z(both_p1, 2 * x, 2, 2))
        cs, diag = couplings(0.125, p, ns)
        for i, c in enumerate(cs):
            st1[i, x] = c
        st1[6, x] = diag
        st1[7, x] = OMEGA / diag
        return 0

    loop(X1, couple1)

    pack_d[...] = loop(X0, lambda x, acc: pack_z(acc, st0[6, x], 4 * x, 1), zero)

    for copy in p2_z:
        net.wait_recv(copy)
    p2_x = [net.copy(raw_p.at[REACH, ix], raw_p.at[REACH, ix], (0, 0, 0), k) for k in range(1, nx)]
    start(p2_x)

    clear([], landings(xd, yd, zd) + landings(xf, yf, zf) + edge_landings(exy, exz, eyz) + edge_landings(pxy, pxz, pyz))
    static = edge_copies(gp, (1,), zs0.at[0, 1], pxy, pxz, pyz)
    for i, d in ((1, 1), (0, -1)):
        static.append(net.copy(pack_d, zd.at[1 - i], (0, 0, d)))
        static.append(net.copy(st0.at[6, X0 - 1 if i else 0], xd.at[1 - i], (d, 0, 0)))
        static.append(net.copy(
            st0.at[6, :, pl.ds(Y0 - 1 if i else 0, 1)], yd.at[1 - i, :, pl.ds(0, 1)], (0, d, 0)
        ))
    start(static)

    round_b.wait()

    def remainder0(field, x, z_sum):
        v, vs = inside0(field, x)
        return rhs[x] - st0[6, x] * v + sum0(x, vs) + at_edges(z_sum, 4 * x, 4)

    sum_s = cz[...] * cross_z(zr0[0, 0], zr0[0, 1])

    def down0(x, acc):
        tmp[x] = remainder0(smooth, 2 * x, sum_s) + remainder0(smooth, 2 * x + 1, sum_s)
        b = tmp[x, pl.ds(0, Y1, stride=2)] + tmp[x, pl.ds(1, Y1, stride=2)]
        b = 0.125 * pair_sum(b, 1, 1)
        b1[x] = b
        u = st1[7, x] * b
        u1[x + 1, 8 : 8 + Y1] = u
        return pack_z(acc, u, 2 * x, 2)

    zs1[1] = loop(X1, down0, zero)


    lane16 = iota((Y1, LANES), 1)
    nothing = jnp.zeros((Y1, LANES), F32)

    def remainder1(x):
        u, us = sides1(u1, x, nothing)
        return b1[x] - st1[6, x] * u + weighted([st1[i, x] for i in range(6)], us)

    def halves(v, at):
        tmp[at, :Y1] = v
        return tmp[at, pl.ds(0, Y2, stride=2)] + tmp[at, pl.ds(1, Y2, stride=2)]

    lane8 = iota((8, LANES), 1)
    z_out = zero
    for x in range(X2):
        cols = pl.ds(x * LANES, LANES)
        lhs[:8, cols] = halves(remainder1(2 * x) + remainder1(2 * x + 1), x)
        for i, y in ((0, 0), (1, Y1 - 1)):
            lhs[8 + i : 9 + i, cols] = sum(
                st1[2 + i, k, y : y + 1] * u1[k + 1, 8 + y : 9 + y] for k in (2 * x, 2 * x + 1)
            )
        out = [
            jnp.where(lane16 == 0, st1[4, k], jnp.where(lane16 == LANES - 1, st1[5, k], 0.0)) * u1[k + 1, 8 : 8 + Y1]
            for k in (2 * x, 2 * x + 1)
        ]
        out = 0.125 * halves(out[0] + out[1], X2 + x)
        z_out = z_out + jnp.where(lane8 == 3 * Z2 + x, roll(out, 3 * Z2 + x, 1), 0.0)
        z_out = z_out + jnp.where(lane8 == 3 * Z2 + X2 + x, roll(out, 3 * Z2 + X2 + 1 + x, 1), 0.0)
    for i, x in ((0, 0), (1, X1 - 1)):
        lhs[16:, i * LANES : (i + 1) * LANES] = halves(st1[i, x] * u1[x + 1, 8 : 8 + Y1], i)
    known = to_compact(lhs[...])
    raw_b[ix, 1, :16] = known[:16]
    raw_b[ix, 1, 16:] = known[16:] + z_out

    mine = raw_b.at[ix, 1]
    b2_xz = []
    for d in (1, -1, 0):
        for k in range(nx):
            if d or k:
                b2_xz.append(net.copy(mine, raw_b.at[ix, 1 - d], (0, 0, d), k))
    start(b2_xz)

    round_c = Faces(net, u1, u1h, zs1.at[1], zr1.at[1], X1, Y1)
    round_c.start()

    for copy in p2_x:
        net.wait_recv(copy)
    p2_y = along_y(raw_p, 0, 8, 4)
    start(p2_y)

    wait(static)
    row8 = iota((8, LANES), 0)

    def inverse(p, diag):
        inside = p > 0.0
        return jnp.where(inside, OMEGA / jnp.where(inside, diag, 1.0), 0.0)

    def to_z_faces(x_edges, y_edges):
        return (
            roll(x_edges[0], 8, 1), roll(x_edges[1], LANES - 8, 1),
            roll(roll(y_edges[0], LANES - 6, 1), 1, 0), roll(roll(y_edges[1], 6, 1), 7, 0),
        )

    quarter = (lane8 // 2) % 4
    z_masks = (
        lane8 < 8, lane8 >= LANES - 8,
        jnp.logical_and(quarter == 0, row8 == 0), jnp.logical_and(quarter == 3, row8 == 7),
    )
    far_x = ((0, X0 - 1), (1, 0))
    far_y = ((0, 3, 7), (1, 0, 0))
    kz[...] = inverse(cross_p, cross_z(zd[0], zd[1]))
    edge_x = [cross_z(pxz[i, 0], pxz[i, 1]) for i in range(2)]
    edge_y = [cross_z(pyz[i, 0], pyz[i, 1]) for i in range(2)]
    for n, (mask, p) in enumerate(zip(z_masks, to_z_faces(edge_x, edge_y))):
        rims[n] = jnp.where(mask, 0.5 * (cross_p + p), 0.0)
    edge_lane = jnp.logical_or(lane0 == 0, lane0 == LANES - 1)
    for i, x in far_x:
        ph = xa[i, 1]
        kx[i] = inverse(ph, xd[i])
        cxz[i] = jnp.where(edge_lane, 0.5 * (ph + at_edges(edge_x[i], 4 * x, 4)), 0.0)
        for j, y in rows0:
            rims[4 + 2 * i + j, :1] = 0.5 * (ph[y : y + 1] + pxy[i, j, :1])
    for i, j, r in far_y:
        crossed[i] = edge_y[i]
        for k, x in ends:
            rims[8 + 2 * i + k, :1] = 0.5 * (ya[i, 1, x, :1] + pxy[k, i, :1])

    edge_row = jnp.logical_or(iota((1, LANES), 1) == 0, iota((1, LANES), 1) == LANES - 1)

    def edge_of_y(packed, x, j):
        return roll(packed, LANES - (2 * (4 * x + j) + 1), 1)

    def static_y(x, _):
        for i, j, r in far_y:
            ph = ya[i, 1, x, :1]
            ky[i, x, :1] = inverse(ph, yd[i, x, :1])
            p = edge_of_y(crossed[i, r : r + 1], x, j)
            cyz[i, x, :1] = jnp.where(edge_row, 0.5 * (ph + p), 0.0)
        return 0

    loop(X0, static_y)

    wait(b2_xz)
    crossing = lax.dot_general(
        raw_b[:, :, 16:].reshape(nx * 24, LANES), select[...], (((1,), (0,)), ((), ())),
        precision=lax.Precision.HIGHEST, preferred_element_type=F32,
    ).reshape(nx, 3, 8, 4 * LANES)
    across = lambda n, xd, zd: crossing[xd, zd, :, n * LANES : (n + 1) * LANES]
    for xd in range(nx):
        for zd in range(3):
            b = raw_b[xd, zd, :8]
            if xd > 0:
                b = b + across(0, xd - 1, zd)
            if xd < nx - 1:
                b = b + across(1, xd + 1, zd)
            if zd > 0:
                b = b + across(2, xd, zd - 1)
            if zd < 2:
                b = b + across(3, xd, zd + 1)
            raw_e[REACH, xd, zd, 8:16] = b
            raw_e[REACH, xd, zd, 7:8] = raw_b[xd, zd, 8:9]
            raw_e[REACH, xd, zd, 16:17] = raw_b[xd, zd, 9:10]
    b2_y = along_y(raw_e, 7, 10, 5)
    start(b2_y)

    for f in (p2, u2, p3, u3, v3, p4, wa, wb):
        n = f.shape[0]
        f[0] = jnp.zeros(f.shape[1:], F32)
        f[n - 1] = jnp.zeros(f.shape[1:], F32)

        def pad(x, _):
            f[x, :8] = jnp.zeros((8, LANES), F32)
            f[x, 8 + ROWS :] = jnp.zeros((8, LANES), F32)
            return 0

        loop(n, pad)
    for f in (v2, w2):
        loop(f.shape[0], lambda x, _: f.__setitem__(x, jnp.zeros(f.shape[1:], F32)) or 0)

    def region(blocks, x):
        lane = iota((ROWS, LANES), 1)
        part = [roll(blocks[zd], Z2 * (zd - x), 1) for zd in range(3)]
        return jnp.where(lane < Z2, part[0], jnp.where(lane < 2 * Z2, part[1], jnp.where(lane < 3 * Z2, part[2], 0.0)))

    for copy in p2_y:
        net.wait_recv(copy)

    def unpack_p(xd, _):
        blocks = [raw_p[:, xd, zd].reshape(ROWS, LANES) for zd in range(3)]
        for x in range(X2):
            p2[X2 * xd + x + 1, 8 : 8 + ROWS] = region(blocks, x)
        return 0

    loop(nx, unpack_p)

    def coarse(v, step):
        return 0.125 * pair_sum(pair_sum(v, step, 0), step, 1)

    def coarse_p(src, dst, step):
        def one(x, _):
            v = src[2 * x + 1, 8 : 8 + ROWS] + src[2 * x + 2, 8 : 8 + ROWS]
            dst[x + 1, 8 : 8 + ROWS] = coarse(v, step)
            return 0

        loop(dst.shape[0] - 2, one)

    coarse_p(p2, p3, 1)
    coarse_p(p3, p4, 2)

    def region_sides(field, x, step, first=8, rows=ROWS):
        v = field[x + 1, pl.ds(first, rows)]
        return v, sides(field, x, rows, first, step, roll(v, step, 1), roll(v, LANES - step, 1))

    def couple_region(p_ref, st, step, scale):
        def one(x, _):
            p, ns = region_sides(p_ref, x, step)
            cs, diag = couplings(scale, p, ns)
            for i, c in enumerate(cs):
                st[i, x] = c
            inside = p > 0.0
            st[6, x] = diag
            st[7, x] = jnp.where(inside, OMEGA / jnp.where(inside, diag, 1.0), 0.0)
            return 0

        loop(p_ref.shape[0] - 2, one)

    couple_region(p2, st2, 1, 0.5 / 16)
    couple_region(p3, st3, 2, 0.5 / 64)
    couple_region(p4, st4, 4, 0.5 / 256)

    for copy in b2_y:
        net.wait_recv(copy)

    def unpack_b(xd, _):
        blocks = []
        for zd in range(3):
            tiles = []
            for yd in range(2 * REACH + 1):
                b = raw_e[yd, xd, zd, 8:16]
                if yd > 0:
                    b = b + jnp.where(row8 == 0, raw_e[yd - 1, xd, zd, 16:17], 0.0)
                if yd < 2 * REACH:
                    b = b + jnp.where(row8 == 7, raw_e[yd + 1, xd, zd, 7:8], 0.0)
                tiles.append(b)
            blocks.append(jnp.concatenate(tiles, axis=0))
        for x in range(X2):
            at = X2 * xd + x
            b = region(blocks, x)
            b2[at] = b
            u2[at + 1, 8 : 8 + ROWS] = st2[7, at] * b
        return 0

    loop(nx, unpack_b)

    def remainder(u_ref, b_ref, st, x, step):
        u, us = region_sides(u_ref, x, step)
        return b_ref[x] - st[6, x] * u + weighted([st[i, x] for i in range(6)], us)

    def down(u_ref, b_ref, st, step, next_b, next_u, next_st):
        def one(x, _):
            r = remainder(u_ref, b_ref, st, 2 * x, step) + remainder(u_ref, b_ref, st, 2 * x + 1, step)
            b = coarse(r, step)
            next_b[x] = b
            next_u[x + 1, 8 : 8 + ROWS] = next_st[7, x] * b
            return 0

        loop(next_b.shape[0], one)

    down(u2, b2, st2, 1, b3, u3, st3)
    down(u3, b3, st3, 2, b4, wa, st4)

    def relaxed(field, b, st, x, step, first=8, rows=ROWS, at=0):
        v, vs = region_sides(field, x, step, first, rows)
        s = weighted([st[i, x, at : at + rows] for i in range(6)], vs)
        return (1.0 - OMEGA) * v + st[7, x, at : at + rows] * (b[x, at : at + rows] + s)

    for src, dst in ((wa, wb), (wb, wa), (wa, wb)):

        def sweep(x, _):
            dst[x + 1, 8 : 8 + ROWS] = relaxed(src, b4, st4, x, 4)
            return 0

        loop(nx, sweep)

    near, span = OWN - 8, 24

    def up3(x, _):
        v3[x + 1, 8 : 8 + ROWS] = u3[x + 1, 8 : 8 + ROWS] + wb[x // 2 + 1, 8 : 8 + ROWS]
        return 0

    loop(2 * nx, up3)

    def relax3(x, _):
        w3[x] = relaxed(v3, b3, st3, x, 2, 8 + near, span, near)
        return 0

    loop(2 * nx, relax3)

    def up2(x, _):
        v2[x + 1, 8 : 8 + span] = u2[x + 1, 8 + near : 8 + near + span] + w3[x // 2]
        return 0

    loop(4 * nx, up2)

    def relax2(x, _):
        w2[x + 1] = relaxed(v2, b2, st2, x, 1, 8, span, near)
        return 0

    loop(4 * nx, relax2)

    wide = lax.dot_general(
        w2[pl.ds(X2 * ix, X2 + 2)].reshape((X2 + 2) * span, LANES), spread[...], (((1,), (0,)), ((), ())),
        precision=lax.Precision.HIGHEST, preferred_element_type=F32,
    ).reshape(X2 + 2, span, 2 * LANES)
    for x in range(X1 + 2):
        m = wide[(x + 1) // 2, :, :LANES]
        rw1[x, pl.ds(8, Y2, stride=2)] = m[8 : 8 + Y2]
        rw1[x, pl.ds(9, Y2, stride=2)] = m[8 : 8 + Y2]
        rw1[x, 7:8] = m[7:8]
        rw1[x, 8 + Y1 : 9 + Y1] = m[8 + Y2 : 9 + Y2]
    round_c.wait()
    both_u = merge_z(zr1[1], 2)
    inner1 = slice(8, 8 + Y1)
    for x in range(X1):
        v1[x + 1, inner1] = u1[x + 1, inner1] + rw1[x + 1, inner1]
        for y in (7, 8 + Y1):
            v1[x + 1, y : y + 1] = u1h[x + 1, y : y + 1] + rw1[x + 1, y : y + 1]
    for x in (0, X1 + 1):
        v1[x, inner1] = u1h[x, inner1] + rw1[x, inner1]
    for x in range(X2):
        h = wide[x + 1, 8 : 8 + Y2, LANES:]
        hw1[x, pl.ds(0, Y2, stride=2)] = h
        hw1[x, pl.ds(1, Y2, stride=2)] = h

    def up1(x, acc):
        halo = unpack_z(both_u, 2 * x, 2, 2) + hw1[x // 2]
        v, vs = sides1(v1, x, halo)
        w = (1.0 - OMEGA) * v + st1[7, x] * (b1[x] + weighted([st1[i, x] for i in range(6)], vs))
        rw0[x, pl.ds(0, Y1, stride=2)] = w
        rw0[x, pl.ds(1, Y1, stride=2)] = w
        for d in range(2):
            v = smooth[2 * x + d + 1, own0] + rw0[x]
            vn[0, 2 * x + d + 1, own0] = v
            acc = pack_z(acc, v, 4 * (2 * x + d), 1)
        return acc

    zs0[2, 0] = loop(X1, up1, zero)

    round_f = edge_copies(vn, (0,), zs0.at[2, 0], exy, exz, eyz)
    round_f += face_copies(
        vn, (0,), lambda i: xf.at[i, 0], lambda i: yf.at[i, 0, :, pl.ds(0, 1)],
        zs0.at[2, 0], lambda i: zf.at[i, 0],
    )
    start(round_f)

    def last_part(x, acc):
        _, vs = inside0(vn, x, (0,))
        n = rhs[x] + sum0(x, vs)
        vn[1, x + 1, own0] = n
        part[x] = n
        return pack_z(acc, n, 4 * x, 1)

    zs0[2, 1] = loop(X0, last_part, zero)
    round_n = face_copies(
        vn, (1,), lambda i: xf.at[i, 1], lambda i: yf.at[i, 1, :, pl.ds(0, 1)],
        zs0.at[2, 1], lambda i: zf.at[i, 1],
    )
    start(round_n)
    wait(round_f)
    wait(round_n)

    edge_x = [cross_z(exz[i, 0], exz[i, 1]) for i in range(2)]
    edge_y = [cross_z(eyz[i, 0], eyz[i, 1]) for i in range(2)]
    cross_v = cross_z(zf[0, 0], zf[1, 0])
    n = cross_z(zf[0, 1], zf[1, 1]) + cz[...] * zs0[2, 0]
    for k, v in enumerate(to_z_faces(edge_x, edge_y)):
        n = n + rims[k] * v
    sum_x = cz[...] * ((1.0 - OMEGA) * cross_v + kz[...] * n)
    z_part = cz[...] * cross_v
    row0 = iota((Y0, LANES), 0)
    for (i, x), (_, far) in zip(ends, far_x):
        vh = xf[i, 0]
        n = xf[i, 1] + st0[i, x] * vn[0, x + 1, own0] + cxz[i] * at_edges(edge_x[i], 4 * far, 4)
        for j, y in rows0:
            n = n + jnp.where(row0 == y, rims[4 + 2 * i + j, :1] * exy[i, j, :1], 0.0)
        sol[X0 + 1 if i else 0, own0] = (1.0 - OMEGA) * vh + kx[i] * n
        part[x] += st0[i, x] * vh
    for i, j, r in far_y:
        crossed[i] = edge_y[i]
        for k, x in ends:
            yf[i, 1, x, :1] += rims[8 + 2 * i + k, :1] * exy[k, i, :1]

    def last_y(x, _):
        for (i, y), (_, j, r) in zip(rows0, far_y):
            row = slice(y, y + 1)
            vh = yf[i, 0, x, :1]
            c = st0[2 + i, x, row]
            n = yf[i, 1, x, :1] + c * vn[0, x + 1, 8 + y : 9 + y]
            n = n + cyz[i, x, :1] * edge_of_y(crossed[i, r : r + 1], x, j)
            at = 8 + Y0 if i else 7
            sol[x + 1, at : at + 1] = (1.0 - OMEGA) * vh + ky[i, x, :1] * n
            part[x, row] += c * vh
        return 0

    loop(X0, last_y)

    def last_z(x, _):
        n = part[x] + at_edges(z_part, 4 * x, 4)
        sol[x + 1, own0] = (1.0 - OMEGA) * vn[0, x + 1, own0] + st0[7, x] * n
        return 0

    loop(X0, last_z)
    out_sol = pltpu.make_async_copy(sol.at[inner0], sol_hbm, local_sems.at[3])
    out_sol.start()

    def residual(x, _):
        res[x] = remainder0(sol, x, sum_x)
        return 0

    loop(X0, residual)
    out_res = pltpu.make_async_copy(res, res_hbm, local_sems.at[4])
    out_res.start()
    net.finish()
    out_sol.wait()
    out_res.wait()


def scratch(nx):
    def vmem(*shape):
        return pltpu.VMEM(shape + (LANES,), F32)

    padded0 = (X0 + 2, Y0 + 16)
    padded1 = (X1 + 2, Y1 + 16)
    n2, n3, n4, tall = 4 * nx, 2 * nx, nx, ROWS + 16
    reach = 2 * REACH + 1
    return [
        vmem(X0, Y0), vmem(2, *padded0), vmem(*padded0), vmem(2, *padded0), vmem(*padded0), vmem(X0, Y0),
        vmem(8, X0, Y0), vmem(3, 2, 8), vmem(1, 2, 8), vmem(X0, Y0), vmem(8), vmem(8),
        vmem(2, 2, Y0), vmem(2, 2, X0, 8), vmem(2, 2, 8), vmem(2, Y0), vmem(2, X0, 8), vmem(2, 8),
        vmem(2, 2, Y0), vmem(2, 2, X0, 8), vmem(2, 2, 8),
        vmem(2, 2, 8), vmem(2, 2, 8), vmem(2, 2, 8), vmem(2, 2, 8), vmem(2, 2, 8), vmem(2, 2, 8),
        vmem(2, Y0), vmem(2, X0, 8), vmem(8), vmem(2, Y0), vmem(2, X0, 8), vmem(12, 8), vmem(2, 8),
        vmem(*padded1), vmem(*padded1), vmem(*padded1), vmem(*padded1), vmem(*padded1), vmem(X1, Y1), vmem(8, X1, Y1),
        vmem(X1, Y0), vmem(X2, Y1), vmem(X1, Y0), vmem(2, 8), vmem(2, 2, 8),
        vmem(X2 * LANES), pltpu.VMEM((LANES, 2 * LANES), F32),
        pltpu.VMEM((24, X2 * LANES), F32), pltpu.VMEM((LANES, 4 * LANES), F32),
        vmem(reach, nx, 3, 8), vmem(nx, 3, 24), vmem(reach, nx, 3, 24),
        vmem(n2 + 2, tall), vmem(n2 + 2, tall), vmem(n2, ROWS), vmem(8, n2, ROWS),
        vmem(n3 + 2, tall), vmem(n3 + 2, tall), vmem(n3 + 2, tall), vmem(n3, ROWS), vmem(8, n3, ROWS),
        vmem(n4 + 2, tall), vmem(n4 + 2, tall), vmem(n4 + 2, tall), vmem(n4, ROWS), vmem(8, n4, ROWS),
        vmem(n3, 24), vmem(n2 + 2, 40), vmem(n2 + 2, 24),
        pltpu.SemaphoreType.DMA((5,)), pltpu.SemaphoreType.DMA((SEMS,)), pltpu.SemaphoreType.DMA((SEMS,)),
    ]


def solution(mesh):
    sizes = tuple(mesh.shape[a] for a in ("gx", "gy", "gz"))
    block = jax.ShapeDtypeStruct((X0, Y0, LANES), F32)
    spec = P("gx", "gy", "gz")

    def shards(right_side, dielectric, guess):
        return pl.pallas_call(
            functools.partial(kernel, sizes),
            out_shape=(block, block),
            in_specs=[pl.BlockSpec(memory_space=pl.ANY)] * 3,
            out_specs=[pl.BlockSpec(memory_space=pl.ANY)] * 2,
            scratch_shapes=scratch(sizes[0]),
            compiler_params=pltpu.CompilerParams(
                collective_id=0, has_side_effects=True, vmem_limit_bytes=60 * 2**20
            ),
            name="vcycle",
        )(right_side, dielectric, guess)

    return jax.shard_map(
        shards, mesh=mesh, in_specs=(spec, spec, spec), out_specs=(spec, spec), check_vma=False
    )
```

```python
import functools

import jax
import jax.numpy as jnp
from jax import lax
from jax.experimental import pallas as pl
from jax.experimental.pallas import tpu as pltpu
from jax.sharding import PartitionSpec as P

OMEGA = 0.8
MESH = pl.DeviceIdType.MESH
F32 = jnp.float32

X0, Y0, LANES = 16, 32, 128
X1, Y1 = 8, 16
X2, Y2, Z2 = 4, 8, 32
REACH = 3
ROWS = (2 * REACH + 1) * Y2
OWN = REACH * Y2


def iota(shape, dim):
    return lax.broadcasted_iota(jnp.int32, shape, dim)


def roll(v, shift, axis):
    size = v.shape[axis]
    if isinstance(shift, int):
        shift = shift % size
        if shift == 0:
            return v
    return pltpu.roll(v, shift, axis=axis)


def loop(count, body, init=0, unroll=True):
    return lax.fori_loop(0, count, body, init, unroll=unroll)


class Faces:
    def __init__(self, net, field, into, sent, got, nx, ny):
        self.net = net
        self.copies = {}
        lead = (slice(None),) * (len(field.shape) - 3)
        for d in (-1, 1):
            src, dst = (1, nx + 1) if d < 0 else (nx, 0)
            self.copies[(d, 0, 0)] = net.copy(
                field.at[lead + (src, pl.ds(8, ny))], into.at[lead + (dst, pl.ds(8, ny))], (d, 0, 0)
            )
            src, dst = (8, 8 + ny) if d < 0 else (7 + ny, 7)
            self.copies[(0, d, 0)] = net.copy(
                field.at[lead + (pl.ds(1, nx), pl.ds(src, 1))],
                into.at[lead + (pl.ds(1, nx), pl.ds(dst, 1))],
                (0, d, 0),
            )
            self.copies[(0, 0, d)] = net.copy(sent, got.at[0 if d > 0 else 1], (0, 0, d))

    def start(self):
        for way in ((0, 0, 1), (0, 0, -1), (1, 0, 0), (-1, 0, 0), (0, 1, 0), (0, -1, 0)):
            self.net.start(self.copies[way])

    def wait(self):
        for copy in self.copies.values():
            self.net.wait_recv(copy)


class Net:
    def __init__(self, sizes, send_sems, recv_sems):
        self.me = tuple(lax.axis_index(a) for a in ("gx", "gy", "gz"))
        self.sizes = sizes
        self.send_sems, self.recv_sems = send_sems, recv_sems
        self.used = 0
        self.started = []

    def there(self, way):
        found = None
        for at, size, d in zip(self.me, self.sizes, way):
            if d:
                ok = (at + d < size) if d > 0 else (at + d >= 0)
                found = ok if found is None else jnp.logical_and(found, ok)
        return found

    def when(self, way):
        found = self.there(way)
        return (lambda f: f()) if found is None else pl.when(found)

    def device(self, way, turn=0):
        x = self.me[0] + way[0]
        if turn:
            x = lax.rem(x + turn, self.sizes[0])
        return (x, self.me[1] + way[1], self.me[2] + way[2])

    def copy(self, src, dst, way, turn=0):
        i = self.used
        self.used += 1
        made = pltpu.make_async_remote_copy(
            src_ref=src,
            dst_ref=dst,
            send_sem=self.send_sems.at[i],
            recv_sem=self.recv_sems.at[i],
            device_id=self.device(way, turn),
            device_id_type=MESH,
        )
        return (made, way)

    def start(self, copy):
        made, way = copy
        self.started.append(copy)

        @self.when(way)
        def _():
            made.start()

    def wait_recv(self, copy):
        made, way = copy

        @self.when(tuple(-d for d in way))
        def _():
            made.wait_recv()

    def finish(self):
        for made, way in self.started:

            @self.when(way)
            def _():
                made.wait_send()


SEMS = 104

DOWN_Z, DOWN_TURN = (92, 63, 95, 60), 67
UP_Z, UP_TURN = (66, 32, 64, 34), 62


def pack_z(acc, v, first, w):
    group = iota((8, LANES), 1) // (2 * w)
    for j in range(v.shape[0] // 8):
        k = first + j
        acc = jnp.where(group == k, roll(v[8 * j : 8 * j + 8], (2 * k + 1) * w, 1), acc)
    return acc


def cross_z(left, right):
    odd = iota((8, LANES), 1) % 2 == 1
    return jnp.where(odd, roll(left, 1, 1), roll(right, LANES - 1, 1))


def at_edges(packed, first, tiles):
    v = jnp.concatenate([roll(packed, LANES - (2 * (first + j) + 1), 1) for j in range(tiles)], axis=0)
    lane = iota(v.shape, 1)
    return jnp.where(jnp.logical_or(lane == 0, lane == LANES - 1), v, 0.0)


def merge_z(got, w):
    return jnp.where((iota((8, LANES), 1) // w) % 2 == 0, got[0], got[1])


def unpack_z(both, first, tiles, w):
    return jnp.concatenate([roll(both, LANES - (2 * (first + j) + 1) * w, 1) for j in range(tiles)], axis=0)


def z_sides(v, halo, w):
    lane = iota(v.shape, 1)
    below = roll(jnp.where(lane >= LANES - w, halo, v), w, 1)
    above = roll(jnp.where(lane < w, halo, v), LANES - w, 1)
    return below, above


def sides(field, x, rows, first, step, below, above, lead=()):
    f = lambda dx, dy: field[lead + (x + 1 + dx, pl.ds(first + dy, rows))]
    return (f(-1, 0), f(1, 0), f(0, -step), f(0, step), below, above)


def weighted(cs, vs):
    total = cs[0] * vs[0]
    for c, v in zip(cs[1:], vs[1:]):
        total = total + c * v
    return total


def pair_sum(v, step, axis):
    if axis == 0 and v.shape[0] > 8:
        tiles = [pair_sum(v[i : i + 8], step, 0) for i in range(0, v.shape[0], 8)]
        return jnp.concatenate(tiles, axis=0)
    size = v.shape[axis]
    if 2 * step == size:
        return v + roll(v, step, axis)
    even = (iota(v.shape, axis) // step) % 2 == 0
    return v + jnp.where(even, roll(v, size - step, axis), roll(v, step, axis))


def kernel(
    sizes,
    rhs_hbm, permit_hbm, guess_hbm,
    sol_hbm, res_hbm,
    rhs, gp, smooth, vn, sol, res, st0, zs0, zr0, part, pack_d, cz,
    xa, ya, za, xd, yd, zd, xf, yf, zf, exy, exz, eyz, pxy, pxz, pyz,
    kx, ky, kz, cxz, cyz, rims, crossed,
    p1, u1, u1h, v1, rw1, b1, st1, tmp, hw1, rw0, zs1, zr1, pick, spread, lhs,
    raw_p, raw_b, raw_e, p2, u2, b2, st2, p3, u3, v3, b3, st3, p4, wa, wb, b4, st4, w3, v2, w2,
    local_sems, send_sems, recv_sems,
):
    nx = sizes[0]
    net = Net(sizes, send_sems, recv_sems)
    ix, iy, iz = net.me
    inner0 = (pl.ds(1, X0), pl.ds(8, Y0))
    own0 = slice(8, 8 + Y0)

    loads = [
        pltpu.make_async_copy(guess_hbm, gp.at[(0,) + inner0], local_sems.at[0]),
        pltpu.make_async_copy(permit_hbm, gp.at[(1,) + inner0], local_sems.at[1]),
        pltpu.make_async_copy(rhs_hbm, rhs, local_sems.at[2]),
    ]
    for load in loads:
        load.start()

    ways = [(0, 0, 1), (0, 0, -1), (1, 0, 0), (-1, 0, 0), (0, 1, 0), (0, -1, 0)]
    greeted = ways + [(2, 0, 0), (-2, 0, 0)]
    barrier = pltpu.get_barrier_semaphore()
    for way in greeted:

        @net.when(way)
        def _():
            pl.semaphore_signal(barrier, inc=1, device_id=net.device(way), device_id_type=MESH)

    signs = (-1, 1)
    zeros = lambda *shape: jnp.zeros(shape + (LANES,), F32)

    def clear(fields, landings):
        todo = {}
        for f, fx, fy in fields:
            for i, d in enumerate(signs):
                todo.setdefault((d, 0, 0), []).append((f, (fx + 1 if i else 0,)))
                todo.setdefault((0, d, 0), []).append((f, (pl.ds(1, fx), pl.ds(8 + fy if i else 7, 1))))
        for ref, at, way in landings:
            todo.setdefault(way, []).append((ref, at))
        for way, items in todo.items():

            @pl.when(jnp.logical_not(net.there(way)))
            def _():
                for ref, at in items:
                    ref[at] = jnp.zeros(ref.at[at].shape, F32)

    def landings(x, y, z):
        return [(ref, (i,), tuple(d if n == axis else 0 for n in range(3)))
                for axis, ref in enumerate((x, y, z)) for i, d in enumerate(signs)]

    def edge_landings(xy, xz, yz):
        out = []
        for i, d in enumerate(signs):
            for j, e in enumerate(signs):
                out += [(xy, (i, j), (d, e, 0)), (xz, (i, j), (d, 0, e)), (yz, (i, j), (0, d, e))]
        return out

    def zero_halo(f, lead=(), fx=X0, fy=Y0):
        for x in (0, fx + 1):
            f[lead + (x,)] = zeros(fy + 16)

        def one(x, _):
            f[lead + (x + 1, slice(0, 8))] = zeros(8)
            f[lead + (x + 1, slice(8 + fy, 16 + fy))] = zeros(8)
            return 0

        loop(fx, one)

    zero_halo(gp, (0,))
    zero_halo(gp, (1,))
    clear([], landings(xa, ya, za))

    for load in loads:
        load.wait()

    lane0 = iota((Y0, LANES), 1)

    def couplings(scale, p, ns):
        cs = [scale * (p + n) for n in ns]
        return cs, cs[0] + cs[1] + cs[2] + cs[3] + cs[4] + cs[5]

    def inside0(field, x, lead=()):
        v = field[lead + (x + 1, pl.ds(8, Y0))]
        return v, sides(field, x, Y0, 8, 1, roll(v, 1, 1), roll(v, LANES - 1, 1), lead=lead)

    def sum0(x, vs):
        return weighted([st0[i, x] for i in range(6)], vs)

    def first(x, accs):
        p, ns = inside0(gp, x, (1,))
        ns = ns[:4] + (jnp.where(lane0 == 0, 0.0, ns[4]), jnp.where(lane0 == LANES - 1, 0.0, ns[5]))
        cs, diag = couplings(0.5, p, ns)
        cs[4] = jnp.where(lane0 == 0, 0.0, cs[4])
        cs[5] = jnp.where(lane0 == LANES - 1, 0.0, cs[5])
        for i, c in enumerate(cs):
            st0[i, x] = c
        st0[6, x] = diag
        v, vs = inside0(gp, x, (0,))
        part[x] = rhs[x] + weighted(cs, vs)
        return pack_z(accs[0], v, 4 * x, 1), pack_z(accs[1], p, 4 * x, 1)

    zero = zeros(8)
    accs = loop(X0, first, (zero, zero))
    zs0[0, 0] = accs[0]
    zs0[0, 1] = accs[1]

    pl.semaphore_wait(barrier, sum(net.there(way).astype(jnp.int32) for way in greeted))

    def face_copies(field, lead, x_to, y_to, z_from, z_to):
        copies = []
        for i, d in ((1, 1), (0, -1)):
            copies.append(net.copy(z_from, z_to(1 - i), (0, 0, d)))
        for i, d in ((1, 1), (0, -1)):
            copies.append(net.copy(field.at[lead + (X0 if i else 1, pl.ds(8, Y0))], x_to(1 - i), (d, 0, 0)))
        for i, d in ((1, 1), (0, -1)):
            row = 7 + Y0 if i else 8
            copies.append(net.copy(field.at[lead + (pl.ds(1, X0), pl.ds(row, 1))], y_to(1 - i), (0, d, 0)))
        return copies

    def edge_copies(field, lead, packed, xy, xz, yz):
        copies = []
        for i, d in enumerate(signs):
            for j, e in enumerate(signs):
                copies.append(net.copy(packed, xz.at[1 - i, 1 - j], (d, 0, e)))
                copies.append(net.copy(packed, yz.at[1 - i, 1 - j], (0, d, e)))
        for i, d in enumerate(signs):
            for j, e in enumerate(signs):
                line = field.at[lead + (X0 if i else 1, pl.ds(7 + Y0 if j else 8, 1))]
                copies.append(net.copy(line, xy.at[1 - i, 1 - j, pl.ds(0, 1)], (d, e, 0)))
        return copies

    def start(copies):
        for copy in copies:
            net.start(copy)

    def wait(copies):
        for copy in copies:
            net.wait_recv(copy)

    round_a = face_copies(
        gp, (slice(None),), lambda i: xa.at[i], lambda i: ya.at[i, :, :, pl.ds(0, 1)],
        zs0.at[0], lambda i: za.at[i],
    )
    start(round_a)

    def coarse_p1(x, acc):
        tmp[x] = gp[1, 2 * x + 1, 8 : 8 + Y0] + gp[1, 2 * x + 2, 8 : 8 + Y0]
        v = tmp[x, pl.ds(0, Y1, stride=2)] + tmp[x, pl.ds(1, Y1, stride=2)]
        v = 0.125 * pair_sum(v, 1, 1)
        p1[x + 1, 8 : 8 + Y1] = v
        return pack_z(acc, v, 2 * x, 2)

    clear([(p1, X1, Y1), (u1h, X1, Y1), (smooth, X0, Y0)], [
        (zr, (r, i), (0, 0, d)) for zr, n in ((zr1, 2), (zr0, 1)) for r in range(n) for i, d in enumerate(signs)
    ])
    zs1[0] = loop(X1, coarse_p1, zero)
    faces_p1 = Faces(net, p1, p1, zs1.at[0], zr1.at[0], X1, Y1)
    faces_p1.start()

    for x in range(X2):
        row, col = iota((LANES, LANES), 0), iota((LANES, LANES), 1)
        take = jnp.logical_and(col == Z2 * x + row // 4, row % 2 == 0)
        pick[pl.ds(x * LANES, LANES)] = jnp.where(take, 0.125, 0.0).astype(F32)
    row, col = iota((LANES, LANES), 0), iota((LANES, LANES), 1)
    spread[:, :LANES] = (row == Z2 + col // 4).astype(F32)
    left = jnp.logical_and(row == Z2 - 1, col >= LANES - 2)
    right = jnp.logical_and(row == 2 * Z2, col < 2)
    spread[:, LANES:] = jnp.logical_or(left, right).astype(F32)

    def to_compact(parts):
        return lax.dot_general(
            parts, pick[...], (((1,), (0,)), ((), ())),
            precision=lax.Precision.HIGHEST, preferred_element_type=F32,
        )

    def compact(planes):
        parts = []
        for x in range(X2):
            tmp[x, :Y1] = planes(2 * x) + planes(2 * x + 1)
            parts.append(tmp[x, pl.ds(0, Y2, stride=2)] + tmp[x, pl.ds(1, Y2, stride=2)])
        return to_compact(jnp.concatenate(parts, axis=1))

    steps = [d for k in range(1, REACH + 1) for d in (k, -k)]
    raw_p[0, :, :, :4] = zeros(nx, 3, 4)
    raw_p[2 * REACH, :, :, 4:] = zeros(nx, 3, 4)
    raw_e[0, :, :, :12] = zeros(nx, 4, 12)
    raw_e[2 * REACH, :, :, 12:] = zeros(nx, 4, 12)
    for d in steps:

        @pl.when(jnp.logical_not(net.there((0, d, 0))))
        def _():
            raw_p[REACH + d] = zeros(nx, 3, 8)
            raw_e[REACH + d] = zeros(nx, 4, 24)

    for d in signs:

        @pl.when(jnp.logical_not(net.there((0, 0, d))))
        def _():
            raw_p[REACH, ix, 1 + d] = zeros(8)
            raw_b[:, 1 + d] = zeros(nx, 24)

    def along_y(raw, first, rows, half, packed=False):
        copies = []
        for d in steps:
            span = pl.ds(first, rows)
            if abs(d) == REACH:
                span = pl.ds(first + rows - half if d > 0 else first, half)
            slots = pl.ds(2, 2) if packed and abs(d) > 1 else pl.ds(0, 3)
            copies.append(net.copy(raw.at[REACH, :, slots, span], raw.at[REACH - d, :, slots, span], (0, d, 0)))
        return copies

    raw_p[REACH, ix, 1] = compact(lambda x: p1[x + 1, 8 : 8 + Y1])
    p2_z = [net.copy(raw_p.at[REACH, ix, 1], raw_p.at[REACH, ix, 1 - d], (0, 0, d)) for d in (1, -1)]
    for copy in p2_z:
        net.start(copy)
    zero_halo(vn, (0,))
    zero_halo(u1, (), X1, Y1)
    lhs[...] = jnp.zeros(lhs.shape, F32)

    wait(round_a)
    own_p = zs0[0, 1]
    cross_p = cross_z(za[0, 1], za[1, 1])
    cz[...] = 0.5 * (own_p + cross_p)
    z_part = cz[...] * cross_z(za[0, 0], za[1, 0])
    z_diag = 0.5 * cross_p
    ends = ((0, 0), (1, X0 - 1))
    rows0 = ((0, 0), (1, Y0 - 1))
    for i, x in ends:
        ph = xa[i, 1]
        c = 0.5 * (gp[1, x + 1, own0] + ph)
        st0[i, x] = c
        st0[6, x] += 0.5 * ph
        part[x] += c * xa[i, 0]

    def first_y(x, _):
        for i, y in rows0:
            row = slice(y, y + 1)
            ph = ya[i, 1, x, :1]
            c = 0.5 * (gp[1, x + 1, 8 + y : 9 + y] + ph)
            st0[2 + i, x, row] = c
            st0[6, x, row] += 0.5 * ph
            part[x, row] += c * ya[i, 0, x, :1]
        return 0

    loop(X0, first_y)

    def first_z(x, acc):
        diag = st0[6, x] + at_edges(z_diag, 4 * x, 4)
        inv = OMEGA / diag
        st0[6, x] = diag
        st0[7, x] = inv
        s = (1.0 - OMEGA) * gp[0, x + 1, own0] + inv * (part[x] + at_edges(z_part, 4 * x, 4))
        smooth[x + 1, own0] = s
        return pack_z(acc, s, 4 * x, 1)

    zs0[1, 0] = loop(X0, first_z, zero)

    round_b = Faces(net, smooth, smooth, zs0.at[1, 0], zr0.at[0], X0, Y0)
    round_b.start()

    faces_p1.wait()
    both_p1 = merge_z(zr1[0], 2)

    def sides1(field, x, halo):
        v = field[x + 1, 8 : 8 + Y1]
        return v, sides(field, x, Y1, 8, 1, *z_sides(v, halo, 2))

    def couple1(x, _):
        p, ns = sides1(p1, x, unpack_z(both_p1, 2 * x, 2, 2))
        cs, diag = couplings(0.125, p, ns)
        for i, c in enumerate(cs):
            st1[i, x] = c
        st1[6, x] = diag
        st1[7, x] = OMEGA / diag
        return 0

    loop(X1, couple1)

    pack_d[...] = loop(X0, lambda x, acc: pack_z(acc, st0[6, x], 4 * x, 1), zero)

    for copy in p2_z:
        net.wait_recv(copy)
    p2_x = [net.copy(raw_p.at[REACH, ix], raw_p.at[REACH, ix], (0, 0, 0), k) for k in range(1, nx)]
    start(p2_x)

    clear([], landings(xd, yd, zd) + landings(xf, yf, zf) + edge_landings(exy, exz, eyz) + edge_landings(pxy, pxz, pyz))
    static = edge_copies(gp, (1,), zs0.at[0, 1], pxy, pxz, pyz)
    for i, d in ((1, 1), (0, -1)):
        static.append(net.copy(pack_d, zd.at[1 - i], (0, 0, d)))
        static.append(net.copy(st0.at[6, X0 - 1 if i else 0], xd.at[1 - i], (d, 0, 0)))
        static.append(net.copy(
            st0.at[6, :, pl.ds(Y0 - 1 if i else 0, 1)], yd.at[1 - i, :, pl.ds(0, 1)], (0, d, 0)
        ))
    start(static)

    round_b.wait()

    def remainder0(field, x, z_sum):
        v, vs = inside0(field, x)
        return rhs[x] - st0[6, x] * v + sum0(x, vs) + at_edges(z_sum, 4 * x, 4)

    sum_s = cz[...] * cross_z(zr0[0, 0], zr0[0, 1])

    def down0(x, acc):
        tmp[x] = remainder0(smooth, 2 * x, sum_s) + remainder0(smooth, 2 * x + 1, sum_s)
        b = tmp[x, pl.ds(0, Y1, stride=2)] + tmp[x, pl.ds(1, Y1, stride=2)]
        b = 0.125 * pair_sum(b, 1, 1)
        b1[x] = b
        u = st1[7, x] * b
        u1[x + 1, 8 : 8 + Y1] = u
        return pack_z(acc, u, 2 * x, 2)

    zs1[1] = loop(X1, down0, zero)


    lane16 = iota((Y1, LANES), 1)
    nothing = jnp.zeros((Y1, LANES), F32)

    def remainder1(x):
        u, us = sides1(u1, x, nothing)
        return b1[x] - st1[6, x] * u + weighted([st1[i, x] for i in range(6)], us)

    def halves(v, at):
        tmp[at, :Y1] = v
        return tmp[at, pl.ds(0, Y2, stride=2)] + tmp[at, pl.ds(1, Y2, stride=2)]

    lane8 = iota((8, LANES), 1)
    z_out = zero
    for x in range(X2):
        cols = pl.ds(x * LANES, LANES)
        lhs[:8, cols] = halves(remainder1(2 * x) + remainder1(2 * x + 1), x)
        for i, y in ((0, 0), (1, Y1 - 1)):
            lhs[8 + i : 9 + i, cols] = sum(
                st1[2 + i, k, y : y + 1] * u1[k + 1, 8 + y : 9 + y] for k in (2 * x, 2 * x + 1)
            )
        out = [
            jnp.where(lane16 == 0, st1[4, k], jnp.where(lane16 == LANES - 1, st1[5, k], 0.0)) * u1[k + 1, 8 : 8 + Y1]
            for k in (2 * x, 2 * x + 1)
        ]
        out = 0.125 * halves(out[0] + out[1], X2 + x)
        z_out = z_out + jnp.where(lane8 == DOWN_Z[x], roll(out, DOWN_Z[x], 1), 0.0)
        z_out = z_out + jnp.where(lane8 == UP_Z[x], roll(out, UP_Z[x] + 1, 1), 0.0)
    for i, x, to in ((0, 0, X2 - 1), (1, X1 - 1, 0)):
        lhs[16:, to * LANES : (to + 1) * LANES] = halves(st1[i, x] * u1[x + 1, 8 : 8 + Y1], i)
    known = to_compact(lhs[...])
    raw_b[ix, 1, :16] = known[:16]
    raw_b[ix, 1, 16:] = known[16:] + z_out

    mine = raw_b.at[ix, 1]
    b2_xz = []
    for d in (1, -1, 0):
        for k in range(nx):
            if d or k:
                b2_xz.append(net.copy(mine, raw_b.at[ix, 1 - d], (0, 0, d), k))
    start(b2_xz)

    round_c = Faces(net, u1, u1h, zs1.at[1], zr1.at[1], X1, Y1)
    round_c.start()

    for copy in p2_x:
        net.wait_recv(copy)
    p2_y = along_y(raw_p, 0, 8, 4)
    start(p2_y)

    wait(static)
    row8 = iota((8, LANES), 0)

    def inverse(p, diag):
        inside = p > 0.0
        return jnp.where(inside, OMEGA / jnp.where(inside, diag, 1.0), 0.0)

    def to_z_faces(x_edges, y_edges):
        return (
            roll(x_edges[0], 8, 1), roll(x_edges[1], LANES - 8, 1),
            roll(roll(y_edges[0], LANES - 6, 1), 1, 0), roll(roll(y_edges[1], 6, 1), 7, 0),
        )

    quarter = (lane8 // 2) % 4
    z_masks = (
        lane8 < 8, lane8 >= LANES - 8,
        jnp.logical_and(quarter == 0, row8 == 0), jnp.logical_and(quarter == 3, row8 == 7),
    )
    far_x = ((0, X0 - 1), (1, 0))
    far_y = ((0, 3, 7), (1, 0, 0))
    kz[...] = inverse(cross_p, cross_z(zd[0], zd[1]))
    edge_x = [cross_z(pxz[i, 0], pxz[i, 1]) for i in range(2)]
    edge_y = [cross_z(pyz[i, 0], pyz[i, 1]) for i in range(2)]
    for n, (mask, p) in enumerate(zip(z_masks, to_z_faces(edge_x, edge_y))):
        rims[n] = jnp.where(mask, 0.5 * (cross_p + p), 0.0)
    edge_lane = jnp.logical_or(lane0 == 0, lane0 == LANES - 1)
    for i, x in far_x:
        ph = xa[i, 1]
        kx[i] = inverse(ph, xd[i])
        cxz[i] = jnp.where(edge_lane, 0.5 * (ph + at_edges(edge_x[i], 4 * x, 4)), 0.0)
        for j, y in rows0:
            rims[4 + 2 * i + j, :1] = 0.5 * (ph[y : y + 1] + pxy[i, j, :1])
    for i, j, r in far_y:
        crossed[i] = edge_y[i]
        for k, x in ends:
            rims[8 + 2 * i + k, :1] = 0.5 * (ya[i, 1, x, :1] + pxy[k, i, :1])

    edge_row = jnp.logical_or(iota((1, LANES), 1) == 0, iota((1, LANES), 1) == LANES - 1)

    def edge_of_y(packed, x, j):
        return roll(packed, LANES - (2 * (4 * x + j) + 1), 1)

    def static_y(x, _):
        for i, j, r in far_y:
            ph = ya[i, 1, x, :1]
            ky[i, x, :1] = inverse(ph, yd[i, x, :1])
            p = edge_of_y(crossed[i, r : r + 1], x, j)
            cyz[i, x, :1] = jnp.where(edge_row, 0.5 * (ph + p), 0.0)
        return 0

    loop(X0, static_y)

    wait(b2_xz)
    def one_of(*lanes):
        return jnp.logical_or(lane8 == lanes[0], lane8 == lanes[1])

    def from_z(xd, zd, turn, straight, turned):
        f = raw_b[xd, zd, 16:]
        return jnp.where(straight, f, jnp.where(turned, roll(f, turn, 1), 0.0))

    up_masks = one_of(Z2, 2 * Z2), one_of(0, 3 * Z2)
    down_masks = one_of(2 * Z2 - 1, 3 * Z2 - 1), one_of(Z2 - 1, 4 * Z2 - 1)
    near_z = lane8 % Z2 < Z2 // 2
    for xd in range(nx):
        blocks = []
        for zd in range(3):
            b = raw_b[xd, zd, :8]
            if xd > 0:
                b = b + jnp.where(lane8 < Z2, raw_b[xd - 1, zd, 16:], 0.0)
            if xd < nx - 1:
                b = b + jnp.where(lane8 >= 3 * Z2, raw_b[xd + 1, zd, 16:], 0.0)
            if zd > 0:
                b = b + from_z(xd, zd - 1, UP_TURN, *up_masks)
            if zd < 2:
                b = b + from_z(xd, zd + 1, DOWN_TURN, *down_masks)
            blocks.append((b, raw_b[xd, zd, 8:9], raw_b[xd, zd, 9:10]))
        low, own, high = blocks
        both = tuple(jnp.where(near_z[: h.shape[0]], h, l) for l, h in zip(low, high))
        for n, (b, down_y, up_y) in enumerate((low, high, own, both)):
            raw_e[REACH, xd, n, 8:16] = b
            raw_e[REACH, xd, n, 7:8] = down_y
            raw_e[REACH, xd, n, 16:17] = up_y
    b2_y = along_y(raw_e, 7, 10, 5, True)
    start(b2_y)

    for f in (p2, u2, p3, u3, v3, p4, wa, wb):
        n = f.shape[0]
        f[0] = jnp.zeros(f.shape[1:], F32)
        f[n - 1] = jnp.zeros(f.shape[1:], F32)

        def pad(x, _):
            f[x, :8] = jnp.zeros((8, LANES), F32)
            f[x, 8 + ROWS :] = jnp.zeros((8, LANES), F32)
            return 0

        loop(n, pad)
    for f in (v2, w2):
        loop(f.shape[0], lambda x, _: f.__setitem__(x, jnp.zeros(f.shape[1:], F32)) or 0)

    def region(blocks, x):
        lane = iota((ROWS, LANES), 1)
        part = [roll(blocks[zd], Z2 * (zd - x), 1) for zd in range(3)]
        return jnp.where(lane < Z2, part[0], jnp.where(lane < 2 * Z2, part[1], jnp.where(lane < 3 * Z2, part[2], 0.0)))

    for copy in p2_y:
        net.wait_recv(copy)

    def unpack_p(xd, _):
        blocks = [raw_p[:, xd, zd].reshape(ROWS, LANES) for zd in range(3)]
        for x in range(X2):
            p2[X2 * xd + x + 1, 8 : 8 + ROWS] = region(blocks, x)
        return 0

    loop(nx, unpack_p)

    def coarse(v, step):
        return 0.125 * pair_sum(pair_sum(v, step, 0), step, 1)

    def coarse_p(src, dst, step):
        def one(x, _):
            v = src[2 * x + 1, 8 : 8 + ROWS] + src[2 * x + 2, 8 : 8 + ROWS]
            dst[x + 1, 8 : 8 + ROWS] = coarse(v, step)
            return 0

        loop(dst.shape[0] - 2, one)

    coarse_p(p2, p3, 1)
    coarse_p(p3, p4, 2)

    def region_sides(field, x, step, first=8, rows=ROWS):
        v = field[x + 1, pl.ds(first, rows)]
        return v, sides(field, x, rows, first, step, roll(v, step, 1), roll(v, LANES - step, 1))

    def couple_region(p_ref, st, step, scale):
        def one(x, _):
            p, ns = region_sides(p_ref, x, step)
            cs, diag = couplings(scale, p, ns)
            for i, c in enumerate(cs):
                st[i, x] = c
            inside = p > 0.0
            st[6, x] = diag
            st[7, x] = jnp.where(inside, OMEGA / jnp.where(inside, diag, 1.0), 0.0)
            return 0

        loop(p_ref.shape[0] - 2, one)

    couple_region(p2, st2, 1, 0.5 / 16)
    couple_region(p3, st3, 2, 0.5 / 64)
    couple_region(p4, st4, 4, 0.5 / 256)

    for copy in b2_y:
        net.wait_recv(copy)

    def unpack_b(xd, _):
        blocks = []
        for zd in range(3):

            def part(yd, rows):
                if zd == 1 or abs(yd - REACH) < 2:
                    return raw_e[yd, xd, (0, 2, 1)[zd], rows]
                v = raw_e[yd, xd, 3, rows]
                near = near_z[: v.shape[0]]
                return jnp.where(near, v, 0.0) if zd else jnp.where(near, 0.0, v)

            tiles = []
            for yd in range(2 * REACH + 1):
                b = part(yd, slice(8, 16))
                if yd > 0:
                    b = b + jnp.where(row8 == 0, part(yd - 1, slice(16, 17)), 0.0)
                if yd < 2 * REACH:
                    b = b + jnp.where(row8 == 7, part(yd + 1, slice(7, 8)), 0.0)
                tiles.append(b)
            blocks.append(jnp.concatenate(tiles, axis=0))
        for x in range(X2):
            at = X2 * xd + x
            b = region(blocks, x)
            b2[at] = b
            u2[at + 1, 8 : 8 + ROWS] = st2[7, at] * b
        return 0

    loop(nx, unpack_b)

    def remainder(u_ref, b_ref, st, x, step):
        u, us = region_sides(u_ref, x, step)
        return b_ref[x] - st[6, x] * u + weighted([st[i, x] for i in range(6)], us)

    def down(u_ref, b_ref, st, step, next_b, next_u, next_st):
        def one(x, _):
            r = remainder(u_ref, b_ref, st, 2 * x, step) + remainder(u_ref, b_ref, st, 2 * x + 1, step)
            b = coarse(r, step)
            next_b[x] = b
            next_u[x + 1, 8 : 8 + ROWS] = next_st[7, x] * b
            return 0

        loop(next_b.shape[0], one)

    down(u2, b2, st2, 1, b3, u3, st3)
    down(u3, b3, st3, 2, b4, wa, st4)

    def relaxed(field, b, st, x, step, first=8, rows=ROWS, at=0):
        v, vs = region_sides(field, x, step, first, rows)
        s = weighted([st[i, x, at : at + rows] for i in range(6)], vs)
        return (1.0 - OMEGA) * v + st[7, x, at : at + rows] * (b[x, at : at + rows] + s)

    for src, dst in ((wa, wb), (wb, wa), (wa, wb)):

        def sweep(x, _):
            dst[x + 1, 8 : 8 + ROWS] = relaxed(src, b4, st4, x, 4)
            return 0

        loop(nx, sweep)

    near, span = OWN - 8, 24

    def up3(x, _):
        v3[x + 1, 8 : 8 + ROWS] = u3[x + 1, 8 : 8 + ROWS] + wb[x // 2 + 1, 8 : 8 + ROWS]
        return 0

    loop(2 * nx, up3)

    def relax3(x, _):
        w3[x] = relaxed(v3, b3, st3, x, 2, 8 + near, span, near)
        return 0

    loop(2 * nx, relax3)

    def up2(x, _):
        v2[x + 1, 8 : 8 + span] = u2[x + 1, 8 + near : 8 + near + span] + w3[x // 2]
        return 0

    loop(4 * nx, up2)

    def relax2(x, _):
        w2[x + 1] = relaxed(v2, b2, st2, x, 1, 8, span, near)
        return 0

    loop(4 * nx, relax2)

    wide = lax.dot_general(
        w2[pl.ds(X2 * ix, X2 + 2)].reshape((X2 + 2) * span, LANES), spread[...], (((1,), (0,)), ((), ())),
        precision=lax.Precision.HIGHEST, preferred_element_type=F32,
    ).reshape(X2 + 2, span, 2 * LANES)
    for x in range(X1 + 2):
        m = wide[(x + 1) // 2, :, :LANES]
        rw1[x, pl.ds(8, Y2, stride=2)] = m[8 : 8 + Y2]
        rw1[x, pl.ds(9, Y2, stride=2)] = m[8 : 8 + Y2]
        rw1[x, 7:8] = m[7:8]
        rw1[x, 8 + Y1 : 9 + Y1] = m[8 + Y2 : 9 + Y2]
    round_c.wait()
    both_u = merge_z(zr1[1], 2)
    inner1 = slice(8, 8 + Y1)
    for x in range(X1):
        v1[x + 1, inner1] = u1[x + 1, inner1] + rw1[x + 1, inner1]
        for y in (7, 8 + Y1):
            v1[x + 1, y : y + 1] = u1h[x + 1, y : y + 1] + rw1[x + 1, y : y + 1]
    for x in (0, X1 + 1):
        v1[x, inner1] = u1h[x, inner1] + rw1[x, inner1]
    for x in range(X2):
        h = wide[x + 1, 8 : 8 + Y2, LANES:]
        hw1[x, pl.ds(0, Y2, stride=2)] = h
        hw1[x, pl.ds(1, Y2, stride=2)] = h

    def up1(x, acc):
        halo = unpack_z(both_u, 2 * x, 2, 2) + hw1[x // 2]
        v, vs = sides1(v1, x, halo)
        w = (1.0 - OMEGA) * v + st1[7, x] * (b1[x] + weighted([st1[i, x] for i in range(6)], vs))
        rw0[x, pl.ds(0, Y1, stride=2)] = w
        rw0[x, pl.ds(1, Y1, stride=2)] = w
        for d in range(2):
            v = smooth[2 * x + d + 1, own0] + rw0[x]
            vn[0, 2 * x + d + 1, own0] = v
            acc = pack_z(acc, v, 4 * (2 * x + d), 1)
        return acc

    zs0[2, 0] = loop(X1, up1, zero)

    round_f = edge_copies(vn, (0,), zs0.at[2, 0], exy, exz, eyz)
    round_f += face_copies(
        vn, (0,), lambda i: xf.at[i, 0], lambda i: yf.at[i, 0, :, pl.ds(0, 1)],
        zs0.at[2, 0], lambda i: zf.at[i, 0],
    )
    start(round_f)

    def last_part(x, acc):
        _, vs = inside0(vn, x, (0,))
        n = rhs[x] + sum0(x, vs)
        vn[1, x + 1, own0] = n
        part[x] = n
        return pack_z(acc, n, 4 * x, 1)

    zs0[2, 1] = loop(X0, last_part, zero)
    round_n = face_copies(
        vn, (1,), lambda i: xf.at[i, 1], lambda i: yf.at[i, 1, :, pl.ds(0, 1)],
        zs0.at[2, 1], lambda i: zf.at[i, 1],
    )
    start(round_n)
    wait(round_f)
    wait(round_n)

    edge_x = [cross_z(exz[i, 0], exz[i, 1]) for i in range(2)]
    edge_y = [cross_z(eyz[i, 0], eyz[i, 1]) for i in range(2)]
    cross_v = cross_z(zf[0, 0], zf[1, 0])
    n = cross_z(zf[0, 1], zf[1, 1]) + cz[...] * zs0[2, 0]
    for k, v in enumerate(to_z_faces(edge_x, edge_y)):
        n = n + rims[k] * v
    sum_x = cz[...] * ((1.0 - OMEGA) * cross_v + kz[...] * n)
    z_part = cz[...] * cross_v
    row0 = iota((Y0, LANES), 0)
    for (i, x), (_, far) in zip(ends, far_x):
        vh = xf[i, 0]
        n = xf[i, 1] + st0[i, x] * vn[0, x + 1, own0] + cxz[i] * at_edges(edge_x[i], 4 * far, 4)
        for j, y in rows0:
            n = n + jnp.where(row0 == y, rims[4 + 2 * i + j, :1] * exy[i, j, :1], 0.0)
        sol[X0 + 1 if i else 0, own0] = (1.0 - OMEGA) * vh + kx[i] * n
        part[x] += st0[i, x] * vh
    for i, j, r in far_y:
        crossed[i] = edge_y[i]
        for k, x in ends:
            yf[i, 1, x, :1] += rims[8 + 2 * i + k, :1] * exy[k, i, :1]

    def last_y(x, _):
        for (i, y), (_, j, r) in zip(rows0, far_y):
            row = slice(y, y + 1)
            vh = yf[i, 0, x, :1]
            c = st0[2 + i, x, row]
            n = yf[i, 1, x, :1] + c * vn[0, x + 1, 8 + y : 9 + y]
            n = n + cyz[i, x, :1] * edge_of_y(crossed[i, r : r + 1], x, j)
            at = 8 + Y0 if i else 7
            sol[x + 1, at : at + 1] = (1.0 - OMEGA) * vh + ky[i, x, :1] * n
            part[x, row] += c * vh
        return 0

    loop(X0, last_y)

    def last_z(x, _):
        n = part[x] + at_edges(z_part, 4 * x, 4)
        sol[x + 1, own0] = (1.0 - OMEGA) * vn[0, x + 1, own0] + st0[7, x] * n
        return 0

    loop(X0, last_z)
    out_sol = pltpu.make_async_copy(sol.at[inner0], sol_hbm, local_sems.at[3])
    out_sol.start()

    def residual(x, _):
        res[x] = remainder0(sol, x, sum_x)
        return 0

    loop(X0, residual)
    out_res = pltpu.make_async_copy(res, res_hbm, local_sems.at[4])
    out_res.start()
    net.finish()
    out_sol.wait()
    out_res.wait()


def scratch(nx):
    def vmem(*shape):
        return pltpu.VMEM(shape + (LANES,), F32)

    padded0 = (X0 + 2, Y0 + 16)
    padded1 = (X1 + 2, Y1 + 16)
    n2, n3, n4, tall = 4 * nx, 2 * nx, nx, ROWS + 16
    reach = 2 * REACH + 1
    return [
        vmem(X0, Y0), vmem(2, *padded0), vmem(*padded0), vmem(2, *padded0), vmem(*padded0), vmem(X0, Y0),
        vmem(8, X0, Y0), vmem(3, 2, 8), vmem(1, 2, 8), vmem(X0, Y0), vmem(8), vmem(8),
        vmem(2, 2, Y0), vmem(2, 2, X0, 8), vmem(2, 2, 8), vmem(2, Y0), vmem(2, X0, 8), vmem(2, 8),
        vmem(2, 2, Y0), vmem(2, 2, X0, 8), vmem(2, 2, 8),
        vmem(2, 2, 8), vmem(2, 2, 8), vmem(2, 2, 8), vmem(2, 2, 8), vmem(2, 2, 8), vmem(2, 2, 8),
        vmem(2, Y0), vmem(2, X0, 8), vmem(8), vmem(2, Y0), vmem(2, X0, 8), vmem(12, 8), vmem(2, 8),
        vmem(*padded1), vmem(*padded1), vmem(*padded1), vmem(*padded1), vmem(*padded1), vmem(X1, Y1), vmem(8, X1, Y1),
        vmem(X1, Y0), vmem(X2, Y1), vmem(X1, Y0), vmem(2, 8), vmem(2, 2, 8),
        vmem(X2 * LANES), pltpu.VMEM((LANES, 2 * LANES), F32),
        pltpu.VMEM((24, X2 * LANES), F32),
        vmem(reach, nx, 3, 8), vmem(nx, 3, 24), vmem(reach, nx, 4, 24),
        vmem(n2 + 2, tall), vmem(n2 + 2, tall), vmem(n2, ROWS), vmem(8, n2, ROWS),
        vmem(n3 + 2, tall), vmem(n3 + 2, tall), vmem(n3 + 2, tall), vmem(n3, ROWS), vmem(8, n3, ROWS),
        vmem(n4 + 2, tall), vmem(n4 + 2, tall), vmem(n4 + 2, tall), vmem(n4, ROWS), vmem(8, n4, ROWS),
        vmem(n3, 24), vmem(n2 + 2, 40), vmem(n2 + 2, 24),
        pltpu.SemaphoreType.DMA((5,)), pltpu.SemaphoreType.DMA((SEMS,)), pltpu.SemaphoreType.DMA((SEMS,)),
    ]


def solution(mesh):
    sizes = tuple(mesh.shape[a] for a in ("gx", "gy", "gz"))
    block = jax.ShapeDtypeStruct((X0, Y0, LANES), F32)
    spec = P("gx", "gy", "gz")

    def shards(right_side, dielectric, guess):
        return pl.pallas_call(
            functools.partial(kernel, sizes),
            out_shape=(block, block),
            in_specs=[pl.BlockSpec(memory_space=pl.ANY)] * 3,
            out_specs=[pl.BlockSpec(memory_space=pl.ANY)] * 2,
            scratch_shapes=scratch(sizes[0]),
            compiler_params=pltpu.CompilerParams(
                collective_id=0, has_side_effects=True, vmem_limit_bytes=213 * 2**18
            ),
            name="vcycle",
        )(right_side, dielectric, guess)

    return jax.shard_map(
        shards, mesh=mesh, in_specs=(spec, spec, spec), out_specs=(spec, spec), check_vma=False
    )
```

```python
import functools

import jax
import jax.numpy as jnp
from jax import lax
from jax.experimental import pallas as pl
from jax.experimental.pallas import tpu as pltpu
from jax.sharding import PartitionSpec as P

OMEGA = 0.8
MESH = pl.DeviceIdType.MESH
F32 = jnp.float32

X0, Y0, LANES = 16, 32, 128
X1, Y1 = 8, 16
X2, Y2, Z2 = 4, 8, 32
REACH = 3
ROWS = (2 * REACH + 1) * Y2
OWN = REACH * Y2


def iota(shape, dim):
    return lax.broadcasted_iota(jnp.int32, shape, dim)


def roll(v, shift, axis):
    size = v.shape[axis]
    if isinstance(shift, int):
        shift = shift % size
        if shift == 0:
            return v
    return pltpu.roll(v, shift, axis=axis)


def loop(count, body, init=0, unroll=True):
    return lax.fori_loop(0, count, body, init, unroll=unroll)


class Faces:
    def __init__(self, net, field, into, sent, got, nx, ny):
        self.net = net
        self.copies = {}
        lead = (slice(None),) * (len(field.shape) - 3)
        for d in (-1, 1):
            src, dst = (1, nx + 1) if d < 0 else (nx, 0)
            self.copies[(d, 0, 0)] = net.copy(
                field.at[lead + (src, pl.ds(8, ny))], into.at[lead + (dst, pl.ds(8, ny))], (d, 0, 0)
            )
            src, dst = (8, 8 + ny) if d < 0 else (7 + ny, 7)
            self.copies[(0, d, 0)] = net.copy(
                field.at[lead + (pl.ds(1, nx), pl.ds(src, 1))],
                into.at[lead + (pl.ds(1, nx), pl.ds(dst, 1))],
                (0, d, 0),
            )
            self.copies[(0, 0, d)] = net.copy(sent, got.at[0 if d > 0 else 1], (0, 0, d))

    def start(self):
        order = ((0, 0, 1), (0, 0, -1), (1, 0, 0), (-1, 0, 0), (0, 1, 0), (0, -1, 0))
        self.net.start([self.copies[way] for way in order])

    def wait(self):
        self.net.wait_recv(list(self.copies.values()))


class Net:
    def __init__(self, sizes, send_sems, recv_sems):
        self.me = tuple(lax.axis_index(a) for a in ("gx", "gy", "gz"))
        self.sizes = sizes
        self.send_sems, self.recv_sems = send_sems, recv_sems
        self.used = 0
        self.started = []

    def there(self, way):
        found = None
        for at, size, d in zip(self.me, self.sizes, way):
            if d:
                ok = (at + d < size) if d > 0 else (at + d >= 0)
                found = ok if found is None else jnp.logical_and(found, ok)
        return found

    def when(self, way):
        found = self.there(way)
        return (lambda f: f()) if found is None else pl.when(found)

    def device(self, way, turn=0):
        x = self.me[0] + way[0]
        if turn:
            x = lax.rem(x + turn, self.sizes[0])
        return (x, self.me[1] + way[1], self.me[2] + way[2])

    def copy(self, src, dst, way, turn=0):
        i = self.used
        self.used += 1
        made = pltpu.make_async_remote_copy(
            src_ref=src,
            dst_ref=dst,
            send_sem=self.send_sems.at[i],
            recv_sem=self.recv_sems.at[i],
            device_id=self.device(way, turn),
            device_id_type=MESH,
        )
        return (made, way)

    def each(self, copies, act):
        ways = {way for _, way in copies if any(way)}
        if not ways:
            for made, _ in copies:
                act(made)
            return
        found = functools.reduce(jnp.logical_and, [self.there(way) for way in sorted(ways)])

        @pl.when(found)
        def _():
            for made, _ in copies:
                act(made)

        @pl.when(jnp.logical_not(found))
        def _():
            for made, way in copies:

                @self.when(way)
                def _():
                    act(made)

    def start(self, copies):
        self.started += copies
        self.each(copies, lambda made: made.start())

    def wait_recv(self, copies):
        self.each([(made, tuple(-d for d in way)) for made, way in copies], lambda made: made.wait_recv())

    def finish(self):
        started, self.started = self.started, []
        self.each(started, lambda made: made.wait_send())


SEMS = 104

DOWN_Z, DOWN_TURN = (92, 63, 95, 60), 67
UP_Z, UP_TURN = (66, 32, 64, 34), 62


def pack_z(acc, v, first, w):
    group = iota((8, LANES), 1) // (2 * w)
    for j in range(v.shape[0] // 8):
        k = first + j
        acc = jnp.where(group == k, roll(v[8 * j : 8 * j + 8], (2 * k + 1) * w, 1), acc)
    return acc


def cross_z(left, right):
    odd = iota((8, LANES), 1) % 2 == 1
    return jnp.where(odd, roll(left, 1, 1), roll(right, LANES - 1, 1))


def at_edges(packed, first, tiles):
    v = jnp.concatenate([roll(packed, LANES - (2 * (first + j) + 1), 1) for j in range(tiles)], axis=0)
    lane = iota(v.shape, 1)
    return jnp.where(jnp.logical_or(lane == 0, lane == LANES - 1), v, 0.0)


def merge_z(got, w):
    return jnp.where((iota((8, LANES), 1) // w) % 2 == 0, got[0], got[1])


def unpack_z(both, first, tiles, w):
    return jnp.concatenate([roll(both, LANES - (2 * (first + j) + 1) * w, 1) for j in range(tiles)], axis=0)


def z_sides(v, halo, w):
    lane = iota(v.shape, 1)
    below = roll(jnp.where(lane >= LANES - w, halo, v), w, 1)
    above = roll(jnp.where(lane < w, halo, v), LANES - w, 1)
    return below, above


def sides(field, x, rows, first, step, below, above, lead=()):
    f = lambda dx, dy: field[lead + (x + 1 + dx, pl.ds(first + dy, rows))]
    return (f(-1, 0), f(1, 0), f(0, -step), f(0, step), below, above)


def weighted(cs, vs):
    total = cs[0] * vs[0]
    for c, v in zip(cs[1:], vs[1:]):
        total = total + c * v
    return total


def pair_sum(v, step, axis):
    if axis == 0 and v.shape[0] > 8:
        tiles = [pair_sum(v[i : i + 8], step, 0) for i in range(0, v.shape[0], 8)]
        return jnp.concatenate(tiles, axis=0)
    size = v.shape[axis]
    if 2 * step == size:
        return v + roll(v, step, axis)
    even = (iota(v.shape, axis) // step) % 2 == 0
    return v + jnp.where(even, roll(v, size - step, axis), roll(v, step, axis))


def kernel(
    sizes,
    rhs_hbm, permit_hbm, guess_hbm,
    sol_ref, res_ref,
    rhs, gp, smooth, vn, sol, st0, zs0, zr0, part, pack_d, cz,
    xa, ya, za, xd, yd, zd, xf, yf, zf, exy, exz, eyz, pxy, pxz, pyz,
    kx, ky, kz, cxz, cyz, rims, crossed,
    p1, u1, u1h, v1, rw1, b1, st1, tmp, hw1, rw0, zs1, zr1, pick, spread, lhs,
    raw_p, raw_b, raw_e, p2, u2, b2, st2, p3, u3, v3, b3, st3, p4, wa, wb, b4, st4, w3, v2, w2,
    local_sems, send_sems, recv_sems,
):
    nx = sizes[0]
    net = Net(sizes, send_sems, recv_sems)
    ix, iy, iz = net.me
    inner0 = (pl.ds(1, X0), pl.ds(8, Y0))
    own0 = slice(8, 8 + Y0)

    ways = [(0, 0, 1), (0, 0, -1), (1, 0, 0), (-1, 0, 0), (0, 1, 0), (0, -1, 0)]
    greeted = ways + [(2, 0, 0), (-2, 0, 0)]
    barrier = pltpu.get_barrier_semaphore()
    for way in greeted:

        @net.when(way)
        def _():
            pl.semaphore_signal(barrier, inc=1, device_id=net.device(way), device_id_type=MESH)

    loads = [
        pltpu.make_async_copy(permit_hbm, gp.at[(1,) + inner0], local_sems.at[1]),
        pltpu.make_async_copy(guess_hbm, gp.at[(0,) + inner0], local_sems.at[0]),
        pltpu.make_async_copy(rhs_hbm, rhs, local_sems.at[2]),
    ]
    for load in loads:
        load.start()

    signs = (-1, 1)
    zeros = lambda *shape: jnp.zeros(shape + (LANES,), F32)

    def clear(fields, landings):
        todo = {}
        for f, fx, fy in fields:
            for i, d in enumerate(signs):
                todo.setdefault((d, 0, 0), []).append((f, (fx + 1 if i else 0,)))
                todo.setdefault((0, d, 0), []).append((f, (pl.ds(1, fx), pl.ds(8 + fy if i else 7, 1))))
        for ref, at, way in landings:
            todo.setdefault(way, []).append((ref, at))
        for way, items in todo.items():

            @pl.when(jnp.logical_not(net.there(way)))
            def _():
                for ref, at in items:
                    ref[at] = jnp.zeros(ref.at[at].shape, F32)

    def landings(x, y, z):
        return [(ref, (i,), tuple(d if n == axis else 0 for n in range(3)))
                for axis, ref in enumerate((x, y, z)) for i, d in enumerate(signs)]

    def edge_landings(xy, xz, yz):
        out = []
        for i, d in enumerate(signs):
            for j, e in enumerate(signs):
                out += [(xy, (i, j), (d, e, 0)), (xz, (i, j), (d, 0, e)), (yz, (i, j), (0, d, e))]
        return out

    def zero_halo(f, lead=(), fx=X0, fy=Y0):
        for x in (0, fx + 1):
            f[lead + (x,)] = zeros(fy + 16)

        def one(x, _):
            f[lead + (x + 1, slice(0, 8))] = zeros(8)
            f[lead + (x + 1, slice(8 + fy, 16 + fy))] = zeros(8)
            return 0

        loop(fx, one)

    zero_halo(gp, (0,))
    zero_halo(gp, (1,))
    zero_halo(vn, (0,))
    zero_halo(u1, (), X1, Y1)
    lhs[...] = jnp.zeros(lhs.shape, F32)
    clear([], landings(xa, ya, za))
    clear([(p1, X1, Y1), (u1h, X1, Y1), (smooth, X0, Y0)], [
        (zr, (r, i), (0, 0, d)) for zr, n in ((zr1, 2), (zr0, 1)) for r in range(n) for i, d in enumerate(signs)
    ])
    for x in range(X2):
        row, col = iota((LANES, LANES), 0), iota((LANES, LANES), 1)
        take = jnp.logical_and(col == Z2 * x + row // 4, row % 2 == 0)
        pick[pl.ds(x * LANES, LANES)] = jnp.where(take, 0.125, 0.0).astype(F32)
    row, col = iota((LANES, LANES), 0), iota((LANES, LANES), 1)
    spread[:, :LANES] = (row == Z2 + col // 4).astype(F32).astype(jnp.bfloat16)
    left = jnp.logical_and(row == Z2 - 1, col >= LANES - 2)
    right = jnp.logical_and(row == 2 * Z2, col < 2)
    spread[:, LANES:] = jnp.logical_or(left, right).astype(F32).astype(jnp.bfloat16)

    steps = [d for k in range(REACH, 0, -1) for d in (k, -k)]
    raw_p[0, :, :, :4] = zeros(nx, 3, 4)
    raw_p[2 * REACH, :, :, 4:] = zeros(nx, 3, 4)
    raw_e[0, :, :, :12] = zeros(nx, 4, 12)
    raw_e[2 * REACH, :, :, 12:] = zeros(nx, 4, 12)
    for d in steps:

        @pl.when(jnp.logical_not(net.there((0, d, 0))))
        def _():
            raw_p[REACH + d] = zeros(nx, 3, 8)
            raw_e[REACH + d] = zeros(nx, 4, 24)

    for d in signs:

        @pl.when(jnp.logical_not(net.there((0, 0, d))))
        def _():
            raw_p[REACH, ix, 1 + d] = zeros(8)
            raw_b[:, 1 + d] = zeros(nx, 24)

    loads[0].wait()
    loads[1].wait()

    lane0 = iota((Y0, LANES), 1)

    def couplings(scale, p, ns):
        cs = [scale * (p + n) for n in ns]
        return cs, cs[0] + cs[1] + cs[2] + cs[3] + cs[4] + cs[5]

    def inside0(field, x, lead=()):
        v = field[lead + (x + 1, pl.ds(8, Y0))]
        return v, sides(field, x, Y0, 8, 1, roll(v, 1, 1), roll(v, LANES - 1, 1), lead=lead)

    def sum0(x, vs):
        return weighted([st0[i, x] for i in range(6)], vs)

    zero = zeros(8)
    accs = loop(X0, lambda x, accs: tuple(
        pack_z(a, gp[i, x + 1, 8 : 8 + Y0], 4 * x, 1) for i, a in enumerate(accs)
    ), (zero, zero))
    zs0[0, 0] = accs[0]
    zs0[0, 1] = accs[1]

    pl.semaphore_wait(barrier, sum(net.there(way).astype(jnp.int32) for way in greeted))

    def face_copies(field, lead, x_to, y_to, z_from, z_to):
        copies = []
        for i, d in ((1, 1), (0, -1)):
            copies.append(net.copy(z_from, z_to(1 - i), (0, 0, d)))
        for i, d in ((1, 1), (0, -1)):
            copies.append(net.copy(field.at[lead + (X0 if i else 1, pl.ds(8, Y0))], x_to(1 - i), (d, 0, 0)))
        for i, d in ((1, 1), (0, -1)):
            row = 7 + Y0 if i else 8
            copies.append(net.copy(field.at[lead + (pl.ds(1, X0), pl.ds(row, 1))], y_to(1 - i), (0, d, 0)))
        return copies

    def edge_copies(field, lead, packed, xy, xz, yz):
        copies = []
        for i, d in enumerate(signs):
            for j, e in enumerate(signs):
                copies.append(net.copy(packed, xz.at[1 - i, 1 - j], (d, 0, e)))
                copies.append(net.copy(packed, yz.at[1 - i, 1 - j], (0, d, e)))
        for i, d in enumerate(signs):
            for j, e in enumerate(signs):
                line = field.at[lead + (X0 if i else 1, pl.ds(7 + Y0 if j else 8, 1))]
                copies.append(net.copy(line, xy.at[1 - i, 1 - j, pl.ds(0, 1)], (d, e, 0)))
        return copies

    start, wait = net.start, net.wait_recv

    round_a = face_copies(
        gp, (slice(None),), lambda i: xa.at[i], lambda i: ya.at[i, :, :, pl.ds(0, 1)],
        zs0.at[0], lambda i: za.at[i],
    )
    start(round_a)
    loads[2].wait()

    def first(x, _):
        p, ns = inside0(gp, x, (1,))
        ns = ns[:4] + (jnp.where(lane0 == 0, 0.0, ns[4]), jnp.where(lane0 == LANES - 1, 0.0, ns[5]))
        cs, diag = couplings(0.5, p, ns)
        cs[4] = jnp.where(lane0 == 0, 0.0, cs[4])
        cs[5] = jnp.where(lane0 == LANES - 1, 0.0, cs[5])
        for i, c in enumerate(cs):
            st0[i, x] = c
        st0[6, x] = diag
        v, vs = inside0(gp, x, (0,))
        part[x] = rhs[x] + weighted(cs, vs)
        return 0

    loop(X0, first)

    def coarse_p1(x, acc):
        tmp[x] = gp[1, 2 * x + 1, 8 : 8 + Y0] + gp[1, 2 * x + 2, 8 : 8 + Y0]
        v = tmp[x, pl.ds(0, Y1, stride=2)] + tmp[x, pl.ds(1, Y1, stride=2)]
        v = 0.125 * pair_sum(v, 1, 1)
        p1[x + 1, 8 : 8 + Y1] = v
        return pack_z(acc, v, 2 * x, 2)

    zs1[0] = loop(X1, coarse_p1, zero)
    faces_p1 = Faces(net, p1, p1, zs1.at[0], zr1.at[0], X1, Y1)
    faces_p1.start()

    def exact_dot(v, ref):
        rows = v.shape[0]
        high = v.astype(jnp.bfloat16)
        rest = v - high.astype(F32)
        middle = rest.astype(jnp.bfloat16)
        low = (rest - middle.astype(F32)).astype(jnp.bfloat16)
        out = lax.dot_general(
            jnp.concatenate([high, middle, low], axis=0), ref[...], (((1,), (0,)), ((), ())),
            preferred_element_type=F32,
        )
        return out[:rows] + (out[rows : 2 * rows] + out[2 * rows :])

    def to_compact(parts):
        return lax.dot_general(
            parts, pick[...], (((1,), (0,)), ((), ())),
            precision=lax.Precision.HIGHEST, preferred_element_type=F32,
        )

    def compact(planes):
        parts = []
        for x in range(X2):
            tmp[x, :Y1] = planes(2 * x) + planes(2 * x + 1)
            parts.append(tmp[x, pl.ds(0, Y2, stride=2)] + tmp[x, pl.ds(1, Y2, stride=2)])
        return to_compact(jnp.concatenate(parts, axis=1))

    def along_y(raw, first, rows, half, packed=False):
        copies = []
        for d in steps:
            span = pl.ds(first, rows)
            if abs(d) == REACH:
                span = pl.ds(first + rows - half if d > 0 else first, half)
            slots = pl.ds(2, 2) if packed and abs(d) > 1 else pl.ds(0, 3)
            copies.append(net.copy(raw.at[REACH, :, slots, span], raw.at[REACH - d, :, slots, span], (0, d, 0)))
        return copies

    raw_p[REACH, ix, 1] = compact(lambda x: p1[x + 1, 8 : 8 + Y1])
    p2_z = [net.copy(raw_p.at[REACH, ix, 1], raw_p.at[REACH, ix, 1 - d], (0, 0, d)) for d in (1, -1)]
    start(p2_z)
    wait(round_a)
    own_p = zs0[0, 1]
    cross_p = cross_z(za[0, 1], za[1, 1])
    cz[...] = 0.5 * (own_p + cross_p)
    z_part = cz[...] * cross_z(za[0, 0], za[1, 0])
    z_diag = 0.5 * cross_p
    ends = ((0, 0), (1, X0 - 1))
    rows0 = ((0, 0), (1, Y0 - 1))
    for i, x in ends:
        ph = xa[i, 1]
        c = 0.5 * (gp[1, x + 1, own0] + ph)
        st0[i, x] = c
        st0[6, x] += 0.5 * ph
        part[x] += c * xa[i, 0]

    def first_y(x, _):
        for i, y in rows0:
            row = slice(y, y + 1)
            ph = ya[i, 1, x, :1]
            c = 0.5 * (gp[1, x + 1, 8 + y : 9 + y] + ph)
            st0[2 + i, x, row] = c
            st0[6, x, row] += 0.5 * ph
            part[x, row] += c * ya[i, 0, x, :1]
        return 0

    loop(X0, first_y)

    def first_z(x, acc):
        diag = st0[6, x] + at_edges(z_diag, 4 * x, 4)
        inv = OMEGA / diag
        st0[6, x] = diag
        st0[7, x] = inv
        s = (1.0 - OMEGA) * gp[0, x + 1, own0] + inv * (part[x] + at_edges(z_part, 4 * x, 4))
        smooth[x + 1, own0] = s
        return pack_z(acc, s, 4 * x, 1)

    zs0[1, 0] = loop(X0, first_z, zero)

    round_b = Faces(net, smooth, smooth, zs0.at[1, 0], zr0.at[0], X0, Y0)
    round_b.start()

    faces_p1.wait()
    both_p1 = merge_z(zr1[0], 2)

    def sides1(field, x, halo):
        v = field[x + 1, 8 : 8 + Y1]
        return v, sides(field, x, Y1, 8, 1, *z_sides(v, halo, 2))

    def couple1(x, _):
        p, ns = sides1(p1, x, unpack_z(both_p1, 2 * x, 2, 2))
        cs, diag = couplings(0.125, p, ns)
        for i, c in enumerate(cs):
            st1[i, x] = c
        st1[6, x] = diag
        st1[7, x] = OMEGA / diag
        return 0

    loop(X1, couple1)

    pack_d[...] = loop(X0, lambda x, acc: pack_z(acc, st0[6, x], 4 * x, 1), zero)

    wait(p2_z)
    p2_x = [net.copy(raw_p.at[REACH, ix], raw_p.at[REACH, ix], (0, 0, 0), k) for k in range(1, nx)]
    start(p2_x)

    clear([], landings(xd, yd, zd) + landings(xf, yf, zf) + edge_landings(exy, exz, eyz) + edge_landings(pxy, pxz, pyz))
    static = edge_copies(gp, (1,), zs0.at[0, 1], pxy, pxz, pyz)
    for i, d in ((1, 1), (0, -1)):
        static.append(net.copy(pack_d, zd.at[1 - i], (0, 0, d)))
        static.append(net.copy(st0.at[6, X0 - 1 if i else 0], xd.at[1 - i], (d, 0, 0)))
        static.append(net.copy(
            st0.at[6, :, pl.ds(Y0 - 1 if i else 0, 1)], yd.at[1 - i, :, pl.ds(0, 1)], (0, d, 0)
        ))
    start(static)

    round_b.wait()

    def remainder0(field, x, z_sum):
        v, vs = inside0(field, x)
        return rhs[x] - st0[6, x] * v + sum0(x, vs) + at_edges(z_sum, 4 * x, 4)

    sum_s = cz[...] * cross_z(zr0[0, 0], zr0[0, 1])

    def remainders0(x, _):
        tmp[x] = remainder0(smooth, 2 * x, sum_s) + remainder0(smooth, 2 * x + 1, sum_s)
        return 0

    def down0(x, acc):
        b = tmp[x, pl.ds(0, Y1, stride=2)] + tmp[x, pl.ds(1, Y1, stride=2)]
        b = 0.125 * pair_sum(b, 1, 1)
        b1[x] = b
        u = st1[7, x] * b
        u1[x + 1, 8 : 8 + Y1] = u
        return pack_z(acc, u, 2 * x, 2)

    loop(X1, remainders0)
    zs1[1] = loop(X1, down0, zero)


    lane16 = iota((Y1, LANES), 1)
    nothing = jnp.zeros((Y1, LANES), F32)

    def remainder1(x):
        u, us = sides1(u1, x, nothing)
        return b1[x] - st1[6, x] * u + weighted([st1[i, x] for i in range(6)], us)

    def halve(at):
        return tmp[at, pl.ds(0, Y2, stride=2)] + tmp[at, pl.ds(1, Y2, stride=2)]

    lane8 = iota((8, LANES), 1)
    z_out = zero
    for x in range(X2):
        pair = (2 * x, 2 * x + 1)
        tmp[x, :Y1] = remainder1(pair[0]) + remainder1(pair[1])
        out = [
            jnp.where(lane16 == 0, st1[4, k], jnp.where(lane16 == LANES - 1, st1[5, k], 0.0)) * u1[k + 1, 8 : 8 + Y1]
            for k in pair
        ]
        tmp[X2 + x, :Y1] = out[0] + out[1]
        for i, y in ((0, 0), (1, Y1 - 1)):
            lhs[8 + i : 9 + i, x * LANES : (x + 1) * LANES] = sum(
                st1[2 + i, k, y : y + 1] * u1[k + 1, 8 + y : 9 + y] for k in pair
            )
    x_out = ((0, 0, X2 - 1), (1, X1 - 1, 0))
    for i, x, _ in x_out:
        tmp[i, Y1:] = st1[i, x] * u1[x + 1, 8 : 8 + Y1]
    for x in range(X2):
        lhs[:8, x * LANES : (x + 1) * LANES] = halve(x)
        out = 0.125 * halve(X2 + x)
        z_out = z_out + jnp.where(lane8 == DOWN_Z[x], roll(out, DOWN_Z[x], 1), 0.0)
        z_out = z_out + jnp.where(lane8 == UP_Z[x], roll(out, UP_Z[x] + 1, 1), 0.0)
    for i, _, to in x_out:
        lhs[16:, to * LANES : (to + 1) * LANES] = (
            tmp[i, pl.ds(Y1, Y2, stride=2)] + tmp[i, pl.ds(Y1 + 1, Y2, stride=2)]
        )
    known = to_compact(lhs[...])
    raw_b[ix, 1, :16] = known[:16]
    raw_b[ix, 1, 16:] = known[16:] + z_out

    mine = raw_b.at[ix, 1]
    b2_xz = []
    for d in (1, -1, 0):
        for k in sorted(range(nx), key=lambda k: -min(k, nx - k)):
            if d or k:
                b2_xz.append(net.copy(mine, raw_b.at[ix, 1 - d], (0, 0, d), k))
    start(b2_xz)

    round_c = Faces(net, u1, u1h, zs1.at[1], zr1.at[1], X1, Y1)
    round_c.start()

    wait(p2_x)
    p2_y = along_y(raw_p, 0, 8, 4)
    start(p2_y)

    wait(static)
    row8 = iota((8, LANES), 0)

    def inverse(p, diag):
        inside = p > 0.0
        return jnp.where(inside, OMEGA / jnp.where(inside, diag, 1.0), 0.0)

    def to_z_faces(x_edges, y_edges):
        return (
            roll(x_edges[0], 8, 1), roll(x_edges[1], LANES - 8, 1),
            roll(roll(y_edges[0], LANES - 6, 1), 1, 0), roll(roll(y_edges[1], 6, 1), 7, 0),
        )

    quarter = (lane8 // 2) % 4
    z_masks = (
        lane8 < 8, lane8 >= LANES - 8,
        jnp.logical_and(quarter == 0, row8 == 0), jnp.logical_and(quarter == 3, row8 == 7),
    )
    far_x = ((0, X0 - 1), (1, 0))
    far_y = ((0, 3, 7), (1, 0, 0))
    kz[...] = inverse(cross_p, cross_z(zd[0], zd[1]))
    edge_x = [cross_z(pxz[i, 0], pxz[i, 1]) for i in range(2)]
    edge_y = [cross_z(pyz[i, 0], pyz[i, 1]) for i in range(2)]
    for n, (mask, p) in enumerate(zip(z_masks, to_z_faces(edge_x, edge_y))):
        rims[n] = jnp.where(mask, 0.5 * (cross_p + p), 0.0)
    edge_lane = jnp.logical_or(lane0 == 0, lane0 == LANES - 1)
    for i, x in far_x:
        ph = xa[i, 1]
        kx[i] = inverse(ph, xd[i])
        cxz[i] = jnp.where(edge_lane, 0.5 * (ph + at_edges(edge_x[i], 4 * x, 4)), 0.0)
        for j, y in rows0:
            rims[4 + 2 * i + j, :1] = 0.5 * (ph[y : y + 1] + pxy[i, j, :1])
    for i, j, r in far_y:
        crossed[i] = edge_y[i]
        for k, x in ends:
            rims[8 + 2 * i + k, :1] = 0.5 * (ya[i, 1, x, :1] + pxy[k, i, :1])

    edge_row = jnp.logical_or(iota((1, LANES), 1) == 0, iota((1, LANES), 1) == LANES - 1)

    def edge_of_y(packed, x, j):
        return roll(packed, LANES - (2 * (4 * x + j) + 1), 1)

    def static_y(x, _):
        for i, j, r in far_y:
            ph = ya[i, 1, x, :1]
            ky[i, x, :1] = inverse(ph, yd[i, x, :1])
            p = edge_of_y(crossed[i, r : r + 1], x, j)
            cyz[i, x, :1] = jnp.where(edge_row, 0.5 * (ph + p), 0.0)
        return 0

    loop(X0, static_y)

    wait(b2_xz)
    def one_of(*lanes):
        return jnp.logical_or(lane8 == lanes[0], lane8 == lanes[1])

    def from_z(xd, zd, turn, straight, turned):
        f = raw_b[xd, zd, 16:]
        return jnp.where(straight, f, jnp.where(turned, roll(f, turn, 1), 0.0))

    up_masks = one_of(Z2, 2 * Z2), one_of(0, 3 * Z2)
    down_masks = one_of(2 * Z2 - 1, 3 * Z2 - 1), one_of(Z2 - 1, 4 * Z2 - 1)
    near_z = lane8 % Z2 < Z2 // 2
    for xd in range(nx):
        blocks = []
        for zd in range(3):
            b = raw_b[xd, zd, :8]
            if xd > 0:
                b = b + jnp.where(lane8 < Z2, raw_b[xd - 1, zd, 16:], 0.0)
            if xd < nx - 1:
                b = b + jnp.where(lane8 >= 3 * Z2, raw_b[xd + 1, zd, 16:], 0.0)
            if zd > 0:
                b = b + from_z(xd, zd - 1, UP_TURN, *up_masks)
            if zd < 2:
                b = b + from_z(xd, zd + 1, DOWN_TURN, *down_masks)
            blocks.append((b, raw_b[xd, zd, 8:9], raw_b[xd, zd, 9:10]))
        low, own, high = blocks
        both = tuple(jnp.where(near_z[: h.shape[0]], h, l) for l, h in zip(low, high))
        for n, (b, down_y, up_y) in enumerate((low, high, own, both)):
            raw_e[REACH, xd, n, 8:16] = b
            raw_e[REACH, xd, n, 7:8] = down_y
            raw_e[REACH, xd, n, 16:17] = up_y
    b2_y = along_y(raw_e, 7, 10, 5, True)
    start(b2_y)

    for f in (p2, u2, p3, u3, v3, p4, wa, wb):
        n = f.shape[0]
        f[0] = jnp.zeros(f.shape[1:], F32)
        f[n - 1] = jnp.zeros(f.shape[1:], F32)

        def pad(x, _):
            f[x, :8] = jnp.zeros((8, LANES), F32)
            f[x, 8 + ROWS :] = jnp.zeros((8, LANES), F32)
            return 0

        loop(n, pad)
    for f in (v2, w2):
        loop(f.shape[0], lambda x, _: f.__setitem__(x, jnp.zeros(f.shape[1:], F32)) or 0)

    def region(blocks, x):
        lane = iota((ROWS, LANES), 1)
        part = [roll(blocks[zd], Z2 * (zd - x), 1) for zd in range(3)]
        return jnp.where(lane < Z2, part[0], jnp.where(lane < 2 * Z2, part[1], jnp.where(lane < 3 * Z2, part[2], 0.0)))

    wait(p2_y)

    def unpack_p(xd, _):
        blocks = [raw_p[:, xd, zd].reshape(ROWS, LANES) for zd in range(3)]
        for x in range(X2):
            p2[X2 * xd + x + 1, 8 : 8 + ROWS] = region(blocks, x)
        return 0

    loop(nx, unpack_p)

    def coarse(v, step):
        return 0.125 * pair_sum(pair_sum(v, step, 0), step, 1)

    def coarse_p(src, dst, step):
        def one(x, _):
            v = src[2 * x + 1, 8 : 8 + ROWS] + src[2 * x + 2, 8 : 8 + ROWS]
            dst[x + 1, 8 : 8 + ROWS] = coarse(v, step)
            return 0

        loop(dst.shape[0] - 2, one)

    coarse_p(p2, p3, 1)
    coarse_p(p3, p4, 2)

    def region_sides(field, x, step, first=8, rows=ROWS):
        v = field[x + 1, pl.ds(first, rows)]
        return v, sides(field, x, rows, first, step, roll(v, step, 1), roll(v, LANES - step, 1))

    def couple_region(p_ref, st, step, scale):
        def one(x, _):
            p, ns = region_sides(p_ref, x, step)
            cs, diag = couplings(scale, p, ns)
            for i, c in enumerate(cs):
                st[i, x] = c
            inside = p > 0.0
            st[6, x] = diag
            st[7, x] = jnp.where(inside, OMEGA / jnp.where(inside, diag, 1.0), 0.0)
            return 0

        loop(p_ref.shape[0] - 2, one)

    couple_region(p2, st2, 1, 0.5 / 16)
    couple_region(p3, st3, 2, 0.5 / 64)
    couple_region(p4, st4, 4, 0.5 / 256)

    net.finish()
    wait(b2_y)

    def unpack_b(xd, _):
        blocks = []
        for zd in range(3):

            def part(yd, rows):
                if zd == 1 or abs(yd - REACH) < 2:
                    return raw_e[yd, xd, (0, 2, 1)[zd], rows]
                v = raw_e[yd, xd, 3, rows]
                near = near_z[: v.shape[0]]
                return jnp.where(near, v, 0.0) if zd else jnp.where(near, 0.0, v)

            tiles = []
            for yd in range(2 * REACH + 1):
                b = part(yd, slice(8, 16))
                if yd > 0:
                    b = b + jnp.where(row8 == 0, part(yd - 1, slice(16, 17)), 0.0)
                if yd < 2 * REACH:
                    b = b + jnp.where(row8 == 7, part(yd + 1, slice(7, 8)), 0.0)
                tiles.append(b)
            blocks.append(jnp.concatenate(tiles, axis=0))
        for x in range(X2):
            at = X2 * xd + x
            b = region(blocks, x)
            b2[at] = b
            u2[at + 1, 8 : 8 + ROWS] = st2[7, at] * b
        return 0

    loop(nx, unpack_b)

    def remainder(u_ref, b_ref, st, x, step):
        u, us = region_sides(u_ref, x, step)
        return b_ref[x] - st[6, x] * u + weighted([st[i, x] for i in range(6)], us)

    def down(u_ref, b_ref, st, step, next_b, next_u, next_st):
        def sums(x, _):
            next_b[x] = remainder(u_ref, b_ref, st, 2 * x, step) + remainder(u_ref, b_ref, st, 2 * x + 1, step)
            return 0

        def one(x, _):
            b = coarse(next_b[x], step)
            next_b[x] = b
            next_u[x + 1, 8 : 8 + ROWS] = next_st[7, x] * b
            return 0

        loop(next_b.shape[0], sums)
        loop(next_b.shape[0], one)

    down(u2, b2, st2, 1, b3, u3, st3)
    down(u3, b3, st3, 2, b4, wa, st4)

    def relaxed(field, b, st, x, step, first=8, rows=ROWS, at=0):
        v, vs = region_sides(field, x, step, first, rows)
        s = weighted([st[i, x, at : at + rows] for i in range(6)], vs)
        return (1.0 - OMEGA) * v + st[7, x, at : at + rows] * (b[x, at : at + rows] + s)

    for src, dst in ((wa, wb), (wb, wa), (wa, wb)):

        def sweep(x, _):
            dst[x + 1, 8 : 8 + ROWS] = relaxed(src, b4, st4, x, 4)
            return 0

        loop(nx, sweep)

    near, span = OWN - 8, 24

    def up3(x, _):
        v3[x + 1, 8 : 8 + ROWS] = u3[x + 1, 8 : 8 + ROWS] + wb[x // 2 + 1, 8 : 8 + ROWS]
        return 0

    loop(2 * nx, up3)

    def relax3(x, _):
        w3[x] = relaxed(v3, b3, st3, x, 2, 8 + near, span, near)
        return 0

    loop(2 * nx, relax3)

    def up2(x, _):
        v2[x + 1, 8 : 8 + span] = u2[x + 1, 8 + near : 8 + near + span] + w3[x // 2]
        return 0

    loop(4 * nx, up2)

    def relax2(x, _):
        w2[x + 1] = relaxed(v2, b2, st2, x, 1, 8, span, near)
        return 0

    loop(4 * nx, relax2)

    wide = exact_dot(w2[pl.ds(X2 * ix, X2 + 2)].reshape((X2 + 2) * span, LANES), spread)
    wide = wide.reshape(X2 + 2, span, 2 * LANES)
    for x in range(X1 + 2):
        m = wide[(x + 1) // 2, :, :LANES]
        rw1[x, pl.ds(8, Y2, stride=2)] = m[8 : 8 + Y2]
        rw1[x, pl.ds(9, Y2, stride=2)] = m[8 : 8 + Y2]
        rw1[x, 7:8] = m[7:8]
        rw1[x, 8 + Y1 : 9 + Y1] = m[8 + Y2 : 9 + Y2]
    round_c.wait()
    both_u = merge_z(zr1[1], 2)
    inner1 = slice(8, 8 + Y1)
    for x in range(X1):
        v1[x + 1, inner1] = u1[x + 1, inner1] + rw1[x + 1, inner1]
        for y in (7, 8 + Y1):
            v1[x + 1, y : y + 1] = u1h[x + 1, y : y + 1] + rw1[x + 1, y : y + 1]
    for x in (0, X1 + 1):
        v1[x, inner1] = u1h[x, inner1] + rw1[x, inner1]
    for x in range(X2):
        h = wide[x + 1, 8 : 8 + Y2, LANES:]
        hw1[x, pl.ds(0, Y2, stride=2)] = h
        hw1[x, pl.ds(1, Y2, stride=2)] = h

    def up1(x, _):
        halo = unpack_z(both_u, 2 * x, 2, 2) + hw1[x // 2]
        v, vs = sides1(v1, x, halo)
        w = (1.0 - OMEGA) * v + st1[7, x] * (b1[x] + weighted([st1[i, x] for i in range(6)], vs))
        rw0[x, pl.ds(0, Y1, stride=2)] = w
        rw0[x, pl.ds(1, Y1, stride=2)] = w
        return 0

    def v_from(x, acc):
        for d in range(2):
            v = smooth[2 * x + d + 1, own0] + rw0[x]
            vn[0, 2 * x + d + 1, own0] = v
            acc = pack_z(acc, v, 4 * (2 * x + d), 1)
        return acc

    loop(X1, up1)
    zs0[2, 0] = loop(X1, v_from, zero)

    z_ways = ((1, 1), (0, -1))
    round_f = edge_copies(vn, (0,), zs0.at[2, 0], exy, exz, eyz)
    round_f[8:8] = [net.copy(zs0.at[2, 0], zf.at[1 - i, 0], (0, 0, d)) for i, d in z_ways]
    start(round_f)

    def last_part(x, acc):
        _, vs = inside0(vn, x, (0,))
        n = rhs[x] + sum0(x, vs)
        part[x] = n
        return pack_z(acc, n, 4 * x, 1)

    zs0[2, 1] = loop(X0, last_part, zero)
    for x in (0, X0 - 1):
        vn[1, x + 1, own0] = part[x]
    for y in (0, Y0 - 1):
        vn[1, 1 : X0 + 1, 8 + y : 9 + y] = part[:, y : y + 1]
    round_n = face_copies(
        vn, (slice(None),), lambda i: xf.at[i], lambda i: yf.at[i, :, :, pl.ds(0, 1)],
        zs0.at[2, 1], lambda i: zf.at[i, 1],
    )
    start(round_n)
    wait(round_f + round_n)

    edge_x = [cross_z(exz[i, 0], exz[i, 1]) for i in range(2)]
    edge_y = [cross_z(eyz[i, 0], eyz[i, 1]) for i in range(2)]
    cross_v = cross_z(zf[0, 0], zf[1, 0])
    n = cross_z(zf[0, 1], zf[1, 1]) + cz[...] * zs0[2, 0]
    for k, v in enumerate(to_z_faces(edge_x, edge_y)):
        n = n + rims[k] * v
    sum_x = cz[...] * ((1.0 - OMEGA) * cross_v + kz[...] * n)
    z_part = cz[...] * cross_v
    row0 = iota((Y0, LANES), 0)
    for (i, x), (_, far) in zip(ends, far_x):
        vh = xf[i, 0]
        n = xf[i, 1] + st0[i, x] * vn[0, x + 1, own0] + cxz[i] * at_edges(edge_x[i], 4 * far, 4)
        for j, y in rows0:
            n = n + jnp.where(row0 == y, rims[4 + 2 * i + j, :1] * exy[i, j, :1], 0.0)
        sol[X0 + 1 if i else 0, own0] = (1.0 - OMEGA) * vh + kx[i] * n
        part[x] += st0[i, x] * vh
    for i, j, r in far_y:
        crossed[i] = edge_y[i]
        for k, x in ends:
            yf[i, 1, x, :1] += rims[8 + 2 * i + k, :1] * exy[k, i, :1]

    def last_y(x, _):
        for (i, y), (_, j, r) in zip(rows0, far_y):
            row = slice(y, y + 1)
            vh = yf[i, 0, x, :1]
            c = st0[2 + i, x, row]
            n = yf[i, 1, x, :1] + c * vn[0, x + 1, 8 + y : 9 + y]
            n = n + cyz[i, x, :1] * edge_of_y(crossed[i, r : r + 1], x, j)
            at = 8 + Y0 if i else 7
            sol[x + 1, at : at + 1] = (1.0 - OMEGA) * vh + ky[i, x, :1] * n
            part[x, row] += c * vh
        return 0

    loop(X0, last_y)

    def last_z(x, _):
        n = part[x] + at_edges(z_part, 4 * x, 4)
        s = (1.0 - OMEGA) * vn[0, x + 1, own0] + st0[7, x] * n
        sol[x + 1, own0] = s
        sol_ref[x] = s
        return 0

    loop(X0, last_z)

    def residual(x, _):
        res_ref[x] = remainder0(sol, x, sum_x)
        return 0

    loop(X0, residual)
    net.finish()


def scratch(nx):
    def vmem(*shape):
        return pltpu.VMEM(shape + (LANES,), F32)

    padded0 = (X0 + 2, Y0 + 16)
    padded1 = (X1 + 2, Y1 + 16)
    n2, n3, n4, tall = 4 * nx, 2 * nx, nx, ROWS + 16
    reach = 2 * REACH + 1
    return [
        vmem(X0, Y0), vmem(2, *padded0), vmem(*padded0), vmem(2, *padded0), vmem(*padded0),
        vmem(8, X0, Y0), vmem(3, 2, 8), vmem(1, 2, 8), vmem(X0, Y0), vmem(8), vmem(8),
        vmem(2, 2, Y0), vmem(2, 2, X0, 8), vmem(2, 2, 8), vmem(2, Y0), vmem(2, X0, 8), vmem(2, 8),
        vmem(2, 2, Y0), vmem(2, 2, X0, 8), vmem(2, 2, 8),
        vmem(2, 2, 8), vmem(2, 2, 8), vmem(2, 2, 8), vmem(2, 2, 8), vmem(2, 2, 8), vmem(2, 2, 8),
        vmem(2, Y0), vmem(2, X0, 8), vmem(8), vmem(2, Y0), vmem(2, X0, 8), vmem(12, 8), vmem(2, 8),
        vmem(*padded1), vmem(*padded1), vmem(*padded1), vmem(*padded1), vmem(*padded1), vmem(X1, Y1), vmem(8, X1, Y1),
        vmem(X1, Y0), vmem(X2, Y1), vmem(X1, Y0), vmem(2, 8), vmem(2, 2, 8),
        vmem(X2 * LANES), pltpu.VMEM((LANES, 2 * LANES), jnp.bfloat16),
        pltpu.VMEM((24, X2 * LANES), F32),
        vmem(reach, nx, 3, 8), vmem(nx, 3, 24), vmem(reach, nx, 4, 24),
        vmem(n2 + 2, tall), vmem(n2 + 2, tall), vmem(n2, ROWS), vmem(8, n2, ROWS),
        vmem(n3 + 2, tall), vmem(n3 + 2, tall), vmem(n3 + 2, tall), vmem(n3, ROWS), vmem(8, n3, ROWS),
        vmem(n4 + 2, tall), vmem(n4 + 2, tall), vmem(n4 + 2, tall), vmem(n4, ROWS), vmem(8, n4, ROWS),
        vmem(n3, 24), vmem(n2 + 2, 40), vmem(n2 + 2, 24),
        pltpu.SemaphoreType.DMA((3,)), pltpu.SemaphoreType.DMA((SEMS,)), pltpu.SemaphoreType.DMA((SEMS,)),
    ]


def solution(mesh):
    sizes = tuple(mesh.shape[a] for a in ("gx", "gy", "gz"))
    block = jax.ShapeDtypeStruct((X0, Y0, LANES), F32)
    spec = P("gx", "gy", "gz")

    def shards(right_side, dielectric, guess):
        return pl.pallas_call(
            functools.partial(kernel, sizes),
            out_shape=(block, block),
            in_specs=[pl.BlockSpec(memory_space=pl.ANY)] * 3,
            out_specs=[pl.BlockSpec(memory_space=pltpu.VMEM)] * 2,
            scratch_shapes=scratch(sizes[0]),
            compiler_params=pltpu.CompilerParams(
                collective_id=0, has_side_effects=True, vmem_limit_bytes=213 * 2**18
            ),
            name="vcycle",
        )(right_side, dielectric, guess)

    return jax.shard_map(
        shards, mesh=mesh, in_specs=(spec, spec, spec), out_specs=(spec, spec), check_vma=False
    )
```

```python
import functools

import jax
import jax.numpy as jnp
from jax import lax
from jax.experimental import pallas as pl
from jax.experimental.pallas import tpu as pltpu
from jax.sharding import PartitionSpec as P

OMEGA = 0.8
MESH = pl.DeviceIdType.MESH
F32 = jnp.float32

X0, Y0, LANES = 16, 32, 128
X1, Y1 = 8, 16
X2, Y2, Z2 = 4, 8, 32
REACH = 3
ROWS = (2 * REACH + 1) * Y2
OWN = REACH * Y2


def iota(shape, dim):
    return lax.broadcasted_iota(jnp.int32, shape, dim)


def roll(v, shift, axis):
    size = v.shape[axis]
    if isinstance(shift, int):
        shift = shift % size
        if shift == 0:
            return v
    return pltpu.roll(v, shift, axis=axis)


def loop(count, body, init=0, unroll=True):
    return lax.fori_loop(0, count, body, init, unroll=unroll)


class Faces:
    def __init__(self, net, field, into, sent, got, nx, ny):
        self.net = net
        self.copies = {}
        lead = (slice(None),) * (len(field.shape) - 3)
        for d in (-1, 1):
            src, dst = (1, nx + 1) if d < 0 else (nx, 0)
            self.copies[(d, 0, 0)] = net.copy(
                field.at[lead + (src, pl.ds(8, ny))], into.at[lead + (dst, pl.ds(8, ny))], (d, 0, 0)
            )
            src, dst = (8, 8 + ny) if d < 0 else (7 + ny, 7)
            self.copies[(0, d, 0)] = net.copy(
                field.at[lead + (pl.ds(1, nx), pl.ds(src, 1))],
                into.at[lead + (pl.ds(1, nx), pl.ds(dst, 1))],
                (0, d, 0),
            )
            self.copies[(0, 0, d)] = net.copy(sent, got.at[0 if d > 0 else 1], (0, 0, d))

    def start(self):
        order = ((0, 0, 1), (0, 0, -1), (1, 0, 0), (-1, 0, 0), (0, 1, 0), (0, -1, 0))
        self.net.start([self.copies[way] for way in order])

    def wait(self):
        self.net.wait_recv(list(self.copies.values()))


class Net:
    def __init__(self, sizes, send_sems, recv_sems):
        self.me = tuple(lax.axis_index(a) for a in ("gx", "gy", "gz"))
        self.sizes = sizes
        self.send_sems, self.recv_sems = send_sems, recv_sems
        self.used = 0
        self.started = []

    def there(self, way):
        found = None
        for at, size, d in zip(self.me, self.sizes, way):
            if d:
                ok = (at + d < size) if d > 0 else (at + d >= 0)
                found = ok if found is None else jnp.logical_and(found, ok)
        return found

    def when(self, way):
        found = self.there(way)
        return (lambda f: f()) if found is None else pl.when(found)

    def device(self, way, turn=0):
        x = self.me[0] + way[0]
        if turn:
            x = lax.rem(x + turn, self.sizes[0])
        return (x, self.me[1] + way[1], self.me[2] + way[2])

    def copy(self, src, dst, way, turn=0):
        i = self.used
        self.used += 1
        made = pltpu.make_async_remote_copy(
            src_ref=src,
            dst_ref=dst,
            send_sem=self.send_sems.at[i],
            recv_sem=self.recv_sems.at[i],
            device_id=self.device(way, turn),
            device_id_type=MESH,
        )
        return (made, way)

    def each(self, copies, act):
        ways = {way for _, way in copies if any(way)}
        if not ways:
            for made, _ in copies:
                act(made)
            return
        found = functools.reduce(jnp.logical_and, [self.there(way) for way in sorted(ways)])

        @pl.when(found)
        def _():
            for made, _ in copies:
                act(made)

        @pl.when(jnp.logical_not(found))
        def _():
            for made, way in copies:

                @self.when(way)
                def _():
                    act(made)

    def start(self, copies):
        self.started += copies
        self.each(copies, lambda made: made.start())

    def wait_recv(self, copies):
        self.each([(made, tuple(-d for d in way)) for made, way in copies], lambda made: made.wait_recv())

    def finish(self):
        started, self.started = self.started, []
        self.each(started, lambda made: made.wait_send())


SEMS = 104

DOWN_Z, DOWN_TURN = (92, 63, 95, 60), 67
UP_Z, UP_TURN = (66, 32, 64, 34), 62


def pack_z(acc, v, first, w):
    group = iota((8, LANES), 1) // (2 * w)
    for j in range(v.shape[0] // 8):
        k = first + j
        acc = jnp.where(group == k, roll(v[8 * j : 8 * j + 8], (2 * k + 1) * w, 1), acc)
    return acc


def cross_z(left, right):
    odd = iota((8, LANES), 1) % 2 == 1
    return jnp.where(odd, roll(left, 1, 1), roll(right, LANES - 1, 1))


def at_edges(packed, first, tiles):
    v = jnp.concatenate([roll(packed, LANES - (2 * (first + j) + 1), 1) for j in range(tiles)], axis=0)
    lane = iota(v.shape, 1)
    return jnp.where(jnp.logical_or(lane == 0, lane == LANES - 1), v, 0.0)


def merge_z(got, w):
    return jnp.where((iota((8, LANES), 1) // w) % 2 == 0, got[0], got[1])


def unpack_z(both, first, tiles, w):
    return jnp.concatenate([roll(both, LANES - (2 * (first + j) + 1) * w, 1) for j in range(tiles)], axis=0)


def z_sides(v, halo, w):
    lane = iota(v.shape, 1)
    below = roll(jnp.where(lane >= LANES - w, halo, v), w, 1)
    above = roll(jnp.where(lane < w, halo, v), LANES - w, 1)
    return below, above


def sides(field, x, rows, first, step, below, above, lead=()):
    f = lambda dx, dy: field[lead + (x + 1 + dx, pl.ds(first + dy, rows))]
    return (f(-1, 0), f(1, 0), f(0, -step), f(0, step), below, above)


def weighted(cs, vs):
    total = cs[0] * vs[0]
    for c, v in zip(cs[1:], vs[1:]):
        total = total + c * v
    return total


def pair_sum(v, step, axis):
    if axis == 0 and v.shape[0] > 8:
        tiles = [pair_sum(v[i : i + 8], step, 0) for i in range(0, v.shape[0], 8)]
        return jnp.concatenate(tiles, axis=0)
    size = v.shape[axis]
    if 2 * step == size:
        return v + roll(v, step, axis)
    even = (iota(v.shape, axis) // step) % 2 == 0
    return v + jnp.where(even, roll(v, size - step, axis), roll(v, step, axis))


def kernel(
    sizes,
    rhs_hbm, permit_hbm, guess_hbm,
    sol_ref, res_ref,
    rhs, gp, smooth, vn, sol, st0, zs0, zr0, part, pack_d, cz,
    xa, ya, za, xd, yd, zd, xf, yf, zf, exy, exz, eyz, pxy, pxz, pyz,
    kx, ky, kz, cxz, cyz, rims, crossed,
    p1, u1, u1h, v1, rw1, b1, st1, tmp, hw1, rw0, zs1, zr1, pick, spread, lhs,
    raw_p, raw_b, raw_e, p2, u2, b2, st2, p3, u3, v3, b3, st3, p4, wa, wb, b4, st4, w3, v2, w2,
    local_sems, send_sems, recv_sems,
):
    nx = sizes[0]
    net = Net(sizes, send_sems, recv_sems)
    ix, iy, iz = net.me
    inner0 = (pl.ds(1, X0), pl.ds(8, Y0))
    own0 = slice(8, 8 + Y0)

    ways = [(0, 0, 1), (0, 0, -1), (1, 0, 0), (-1, 0, 0), (0, 1, 0), (0, -1, 0)]
    greeted = ways + [(2, 0, 0), (-2, 0, 0)]
    barrier = pltpu.get_barrier_semaphore()
    for way in greeted:

        @net.when(way)
        def _():
            pl.semaphore_signal(barrier, inc=1, device_id=net.device(way), device_id_type=MESH)

    loads = [
        pltpu.make_async_copy(permit_hbm, gp.at[(1,) + inner0], local_sems.at[1]),
        pltpu.make_async_copy(guess_hbm, gp.at[(0,) + inner0], local_sems.at[0]),
        pltpu.make_async_copy(rhs_hbm, rhs, local_sems.at[2]),
    ]
    for load in loads:
        load.start()

    signs = (-1, 1)
    zeros = lambda *shape: jnp.zeros(shape + (LANES,), F32)

    def clear(fields, landings):
        todo = {}
        for f, fx, fy in fields:
            for i, d in enumerate(signs):
                todo.setdefault((d, 0, 0), []).append((f, (fx + 1 if i else 0,)))
                todo.setdefault((0, d, 0), []).append((f, (pl.ds(1, fx), pl.ds(8 + fy if i else 7, 1))))
        for ref, at, way in landings:
            todo.setdefault(way, []).append((ref, at))
        for way, items in todo.items():

            @pl.when(jnp.logical_not(net.there(way)))
            def _():
                for ref, at in items:
                    ref[at] = jnp.zeros(ref.at[at].shape, F32)

    def landings(x, y, z):
        return [(ref, (i,), tuple(d if n == axis else 0 for n in range(3)))
                for axis, ref in enumerate((x, y, z)) for i, d in enumerate(signs)]

    def edge_landings(xy, xz, yz):
        out = []
        for i, d in enumerate(signs):
            for j, e in enumerate(signs):
                out += [(xy, (i, j), (d, e, 0)), (xz, (i, j), (d, 0, e)), (yz, (i, j), (0, d, e))]
        return out

    def zero_halo(f, lead=(), fx=X0, fy=Y0):
        for x in (0, fx + 1):
            f[lead + (x,)] = zeros(fy + 16)

        def one(x, _):
            f[lead + (x + 1, slice(0, 8))] = zeros(8)
            f[lead + (x + 1, slice(8 + fy, 16 + fy))] = zeros(8)
            return 0

        loop(fx, one)

    zero_halo(gp, (0,))
    zero_halo(gp, (1,))
    zero_halo(vn, (0,))
    zero_halo(u1, (), X1, Y1)
    lhs[...] = jnp.zeros(lhs.shape, F32)
    clear([], landings(xa, ya, za))
    clear([(p1, X1, Y1), (u1h, X1, Y1), (smooth, X0, Y0)], [
        (zr, (r, i), (0, 0, d)) for zr, n in ((zr1, 2), (zr0, 1)) for r in range(n) for i, d in enumerate(signs)
    ])
    for x in range(X2):
        row, col = iota((LANES, LANES), 0), iota((LANES, LANES), 1)
        take = jnp.logical_and(col == Z2 * x + row // 4, row % 2 == 0)
        pick[pl.ds(x * LANES, LANES)] = jnp.where(take, 0.125, 0.0).astype(F32)
    row, col = iota((LANES, LANES), 0), iota((LANES, LANES), 1)
    spread[:, :LANES] = (row == Z2 + col // 4).astype(F32)
    left = jnp.logical_and(row == Z2 - 1, col >= LANES - 2)
    right = jnp.logical_and(row == 2 * Z2, col < 2)
    spread[:, LANES:] = jnp.logical_or(left, right).astype(F32)

    steps = [d for k in range(REACH, 0, -1) for d in (k, -k)]
    raw_p[0, :, :, :4] = zeros(nx, 3, 4)
    raw_p[2 * REACH, :, :, 4:] = zeros(nx, 3, 4)
    raw_e[0, :, :, :12] = zeros(nx, 4, 12)
    raw_e[2 * REACH, :, :, 12:] = zeros(nx, 4, 12)
    for d in steps:

        @pl.when(jnp.logical_not(net.there((0, d, 0))))
        def _():
            raw_p[REACH + d] = zeros(nx, 3, 8)
            raw_e[REACH + d] = zeros(nx, 4, 24)

    for d in signs:

        @pl.when(jnp.logical_not(net.there((0, 0, d))))
        def _():
            raw_p[REACH, ix, 1 + d] = zeros(8)
            raw_b[:, 1 + d] = zeros(nx, 24)

    loads[0].wait()
    loads[1].wait()

    lane0 = iota((Y0, LANES), 1)

    def couplings(scale, p, ns):
        cs = [scale * (p + n) for n in ns]
        return cs, cs[0] + cs[1] + cs[2] + cs[3] + cs[4] + cs[5]

    def inside0(field, x, lead=()):
        v = field[lead + (x + 1, pl.ds(8, Y0))]
        return v, sides(field, x, Y0, 8, 1, roll(v, 1, 1), roll(v, LANES - 1, 1), lead=lead)

    def sum0(x, vs):
        return weighted([st0[i, x] for i in range(6)], vs)

    zero = zeros(8)
    accs = loop(X0, lambda x, accs: tuple(
        pack_z(a, gp[i, x + 1, 8 : 8 + Y0], 4 * x, 1) for i, a in enumerate(accs)
    ), (zero, zero))
    zs0[0, 0] = accs[0]
    zs0[0, 1] = accs[1]

    pl.semaphore_wait(barrier, sum(net.there(way).astype(jnp.int32) for way in greeted))

    def face_copies(field, lead, x_to, y_to, z_from, z_to):
        copies = []
        for i, d in ((1, 1), (0, -1)):
            copies.append(net.copy(z_from, z_to(1 - i), (0, 0, d)))
        for i, d in ((1, 1), (0, -1)):
            copies.append(net.copy(field.at[lead + (X0 if i else 1, pl.ds(8, Y0))], x_to(1 - i), (d, 0, 0)))
        for i, d in ((1, 1), (0, -1)):
            row = 7 + Y0 if i else 8
            copies.append(net.copy(field.at[lead + (pl.ds(1, X0), pl.ds(row, 1))], y_to(1 - i), (0, d, 0)))
        return copies

    def edge_copies(field, lead, packed, xy, xz, yz):
        copies = []
        for i, d in enumerate(signs):
            for j, e in enumerate(signs):
                copies.append(net.copy(packed, xz.at[1 - i, 1 - j], (d, 0, e)))
                copies.append(net.copy(packed, yz.at[1 - i, 1 - j], (0, d, e)))
        for i, d in enumerate(signs):
            for j, e in enumerate(signs):
                line = field.at[lead + (X0 if i else 1, pl.ds(7 + Y0 if j else 8, 1))]
                copies.append(net.copy(line, xy.at[1 - i, 1 - j, pl.ds(0, 1)], (d, e, 0)))
        return copies

    start, wait = net.start, net.wait_recv

    round_a = face_copies(
        gp, (slice(None),), lambda i: xa.at[i], lambda i: ya.at[i, :, :, pl.ds(0, 1)],
        zs0.at[0], lambda i: za.at[i],
    )
    start(round_a)
    loads[2].wait()

    def first(x, _):
        p, ns = inside0(gp, x, (1,))
        ns = ns[:4] + (jnp.where(lane0 == 0, 0.0, ns[4]), jnp.where(lane0 == LANES - 1, 0.0, ns[5]))
        cs, diag = couplings(0.5, p, ns)
        cs[4] = jnp.where(lane0 == 0, 0.0, cs[4])
        cs[5] = jnp.where(lane0 == LANES - 1, 0.0, cs[5])
        for i, c in enumerate(cs):
            st0[i, x] = c
        st0[6, x] = diag
        v, vs = inside0(gp, x, (0,))
        part[x] = rhs[x] + weighted(cs, vs)
        return 0

    loop(X0, first)

    def coarse_p1(x, acc):
        tmp[x] = gp[1, 2 * x + 1, 8 : 8 + Y0] + gp[1, 2 * x + 2, 8 : 8 + Y0]
        v = tmp[x, pl.ds(0, Y1, stride=2)] + tmp[x, pl.ds(1, Y1, stride=2)]
        v = 0.125 * pair_sum(v, 1, 1)
        p1[x + 1, 8 : 8 + Y1] = v
        return pack_z(acc, v, 2 * x, 2)

    zs1[0] = loop(X1, coarse_p1, zero)
    faces_p1 = Faces(net, p1, p1, zs1.at[0], zr1.at[0], X1, Y1)
    faces_p1.start()

    def to_compact(parts):
        return lax.dot_general(
            parts, pick[...], (((1,), (0,)), ((), ())),
            precision=lax.Precision.HIGHEST, preferred_element_type=F32,
        )

    def compact(planes):
        parts = []
        for x in range(X2):
            tmp[x, :Y1] = planes(2 * x) + planes(2 * x + 1)
            parts.append(tmp[x, pl.ds(0, Y2, stride=2)] + tmp[x, pl.ds(1, Y2, stride=2)])
        return to_compact(jnp.concatenate(parts, axis=1))

    def along_y(raw, first, rows, half, packed=False):
        copies = []
        for d in steps:
            span = pl.ds(first, rows)
            if abs(d) == REACH:
                span = pl.ds(first + rows - half if d > 0 else first, half)
            slots = pl.ds(2, 2) if packed and abs(d) > 1 else pl.ds(0, 3)
            copies.append(net.copy(raw.at[REACH, :, slots, span], raw.at[REACH - d, :, slots, span], (0, d, 0)))
        return copies

    raw_p[REACH, ix, 1] = compact(lambda x: p1[x + 1, 8 : 8 + Y1])
    p2_z = [net.copy(raw_p.at[REACH, ix, 1], raw_p.at[REACH, ix, 1 - d], (0, 0, d)) for d in (1, -1)]
    start(p2_z)
    wait(round_a)
    own_p = zs0[0, 1]
    cross_p = cross_z(za[0, 1], za[1, 1])
    cz[...] = 0.5 * (own_p + cross_p)
    z_part = cz[...] * cross_z(za[0, 0], za[1, 0])
    z_diag = 0.5 * cross_p
    ends = ((0, 0), (1, X0 - 1))
    rows0 = ((0, 0), (1, Y0 - 1))
    for i, x in ends:
        ph = xa[i, 1]
        c = 0.5 * (gp[1, x + 1, own0] + ph)
        st0[i, x] = c
        st0[6, x] += 0.5 * ph
        part[x] += c * xa[i, 0]

    def first_y(x, _):
        for i, y in rows0:
            row = slice(y, y + 1)
            ph = ya[i, 1, x, :1]
            c = 0.5 * (gp[1, x + 1, 8 + y : 9 + y] + ph)
            st0[2 + i, x, row] = c
            st0[6, x, row] += 0.5 * ph
            part[x, row] += c * ya[i, 0, x, :1]
        return 0

    loop(X0, first_y)

    def first_z(x, acc):
        diag = st0[6, x] + at_edges(z_diag, 4 * x, 4)
        inv = OMEGA / diag
        st0[6, x] = diag
        st0[7, x] = inv
        s = (1.0 - OMEGA) * gp[0, x + 1, own0] + inv * (part[x] + at_edges(z_part, 4 * x, 4))
        smooth[x + 1, own0] = s
        return pack_z(acc, s, 4 * x, 1)

    zs0[1, 0] = loop(X0, first_z, zero)

    round_b = Faces(net, smooth, smooth, zs0.at[1, 0], zr0.at[0], X0, Y0)
    round_b.start()

    faces_p1.wait()
    both_p1 = merge_z(zr1[0], 2)

    def sides1(field, x, halo):
        v = field[x + 1, 8 : 8 + Y1]
        return v, sides(field, x, Y1, 8, 1, *z_sides(v, halo, 2))

    def couple1(x, _):
        p, ns = sides1(p1, x, unpack_z(both_p1, 2 * x, 2, 2))
        cs, diag = couplings(0.125, p, ns)
        for i, c in enumerate(cs):
            st1[i, x] = c
        st1[6, x] = diag
        st1[7, x] = OMEGA / diag
        return 0

    loop(X1, couple1)

    pack_d[...] = loop(X0, lambda x, acc: pack_z(acc, st0[6, x], 4 * x, 1), zero)

    wait(p2_z)
    p2_x = [net.copy(raw_p.at[REACH, ix], raw_p.at[REACH, ix], (0, 0, 0), k) for k in range(1, nx)]
    start(p2_x)

    clear([], landings(xd, yd, zd) + landings(xf, yf, zf) + edge_landings(exy, exz, eyz) + edge_landings(pxy, pxz, pyz))
    static = edge_copies(gp, (1,), zs0.at[0, 1], pxy, pxz, pyz)
    for i, d in ((1, 1), (0, -1)):
        static.append(net.copy(pack_d, zd.at[1 - i], (0, 0, d)))
        static.append(net.copy(st0.at[6, X0 - 1 if i else 0], xd.at[1 - i], (d, 0, 0)))
        static.append(net.copy(
            st0.at[6, :, pl.ds(Y0 - 1 if i else 0, 1)], yd.at[1 - i, :, pl.ds(0, 1)], (0, d, 0)
        ))
    start(static)

    round_b.wait()

    def remainder0(field, x, z_sum):
        v, vs = inside0(field, x)
        return rhs[x] - st0[6, x] * v + sum0(x, vs) + at_edges(z_sum, 4 * x, 4)

    sum_s = cz[...] * cross_z(zr0[0, 0], zr0[0, 1])

    def remainders0(x, _):
        tmp[x] = remainder0(smooth, 2 * x, sum_s) + remainder0(smooth, 2 * x + 1, sum_s)
        return 0

    def down0(x, acc):
        b = tmp[x, pl.ds(0, Y1, stride=2)] + tmp[x, pl.ds(1, Y1, stride=2)]
        b = 0.125 * pair_sum(b, 1, 1)
        b1[x] = b
        u = st1[7, x] * b
        u1[x + 1, 8 : 8 + Y1] = u
        return pack_z(acc, u, 2 * x, 2)

    loop(X1, remainders0)
    zs1[1] = loop(X1, down0, zero)


    lane16 = iota((Y1, LANES), 1)
    nothing = jnp.zeros((Y1, LANES), F32)

    def remainder1(x):
        u, us = sides1(u1, x, nothing)
        return b1[x] - st1[6, x] * u + weighted([st1[i, x] for i in range(6)], us)

    def halve(at):
        return tmp[at, pl.ds(0, Y2, stride=2)] + tmp[at, pl.ds(1, Y2, stride=2)]

    lane8 = iota((8, LANES), 1)
    z_out = zero
    for x in range(X2):
        pair = (2 * x, 2 * x + 1)
        tmp[x, :Y1] = remainder1(pair[0]) + remainder1(pair[1])
        out = [
            jnp.where(lane16 == 0, st1[4, k], jnp.where(lane16 == LANES - 1, st1[5, k], 0.0)) * u1[k + 1, 8 : 8 + Y1]
            for k in pair
        ]
        tmp[X2 + x, :Y1] = out[0] + out[1]
        for i, y in ((0, 0), (1, Y1 - 1)):
            lhs[8 + i : 9 + i, x * LANES : (x + 1) * LANES] = sum(
                st1[2 + i, k, y : y + 1] * u1[k + 1, 8 + y : 9 + y] for k in pair
            )
    x_out = ((0, 0, X2 - 1), (1, X1 - 1, 0))
    for i, x, _ in x_out:
        tmp[i, Y1:] = st1[i, x] * u1[x + 1, 8 : 8 + Y1]
    for x in range(X2):
        lhs[:8, x * LANES : (x + 1) * LANES] = halve(x)
        out = 0.125 * halve(X2 + x)
        z_out = z_out + jnp.where(lane8 == DOWN_Z[x], roll(out, DOWN_Z[x], 1), 0.0)
        z_out = z_out + jnp.where(lane8 == UP_Z[x], roll(out, UP_Z[x] + 1, 1), 0.0)
    for i, _, to in x_out:
        lhs[16:, to * LANES : (to + 1) * LANES] = (
            tmp[i, pl.ds(Y1, Y2, stride=2)] + tmp[i, pl.ds(Y1 + 1, Y2, stride=2)]
        )
    known = to_compact(lhs[...])
    raw_b[ix, 1, :16] = known[:16]
    raw_b[ix, 1, 16:] = known[16:] + z_out

    mine = raw_b.at[ix, 1]
    b2_xz = []
    for d in (1, -1, 0):
        for k in sorted(range(nx), key=lambda k: -min(k, nx - k)):
            if d or k:
                b2_xz.append(net.copy(mine, raw_b.at[ix, 1 - d], (0, 0, d), k))
    start(b2_xz)

    round_c = Faces(net, u1, u1h, zs1.at[1], zr1.at[1], X1, Y1)
    round_c.start()

    wait(p2_x)
    p2_y = along_y(raw_p, 0, 8, 4)
    start(p2_y)

    wait(static)
    row8 = iota((8, LANES), 0)

    def inverse(p, diag):
        inside = p > 0.0
        return jnp.where(inside, OMEGA / jnp.where(inside, diag, 1.0), 0.0)

    def to_z_faces(x_edges, y_edges):
        return (
            roll(x_edges[0], 8, 1), roll(x_edges[1], LANES - 8, 1),
            roll(roll(y_edges[0], LANES - 6, 1), 1, 0), roll(roll(y_edges[1], 6, 1), 7, 0),
        )

    quarter = (lane8 // 2) % 4
    z_masks = (
        lane8 < 8, lane8 >= LANES - 8,
        jnp.logical_and(quarter == 0, row8 == 0), jnp.logical_and(quarter == 3, row8 == 7),
    )
    far_x = ((0, X0 - 1), (1, 0))
    far_y = ((0, 3, 7), (1, 0, 0))
    kz[...] = inverse(cross_p, cross_z(zd[0], zd[1]))
    edge_x = [cross_z(pxz[i, 0], pxz[i, 1]) for i in range(2)]
    edge_y = [cross_z(pyz[i, 0], pyz[i, 1]) for i in range(2)]
    for n, (mask, p) in enumerate(zip(z_masks, to_z_faces(edge_x, edge_y))):
        rims[n] = jnp.where(mask, 0.5 * (cross_p + p), 0.0)
    edge_lane = jnp.logical_or(lane0 == 0, lane0 == LANES - 1)
    for i, x in far_x:
        ph = xa[i, 1]
        kx[i] = inverse(ph, xd[i])
        cxz[i] = jnp.where(edge_lane, 0.5 * (ph + at_edges(edge_x[i], 4 * x, 4)), 0.0)
        for j, y in rows0:
            rims[4 + 2 * i + j, :1] = 0.5 * (ph[y : y + 1] + pxy[i, j, :1])
    for i, j, r in far_y:
        crossed[i] = edge_y[i]
        for k, x in ends:
            rims[8 + 2 * i + k, :1] = 0.5 * (ya[i, 1, x, :1] + pxy[k, i, :1])

    edge_row = jnp.logical_or(iota((1, LANES), 1) == 0, iota((1, LANES), 1) == LANES - 1)

    def edge_of_y(packed, x, j):
        return roll(packed, LANES - (2 * (4 * x + j) + 1), 1)

    def static_y(x, _):
        for i, j, r in far_y:
            ph = ya[i, 1, x, :1]
            ky[i, x, :1] = inverse(ph, yd[i, x, :1])
            p = edge_of_y(crossed[i, r : r + 1], x, j)
            cyz[i, x, :1] = jnp.where(edge_row, 0.5 * (ph + p), 0.0)
        return 0

    loop(X0, static_y)

    wait(b2_xz)
    def one_of(*lanes):
        return jnp.logical_or(lane8 == lanes[0], lane8 == lanes[1])

    def from_z(xd, zd, turn, straight, turned):
        f = raw_b[xd, zd, 16:]
        return jnp.where(straight, f, jnp.where(turned, roll(f, turn, 1), 0.0))

    up_masks = one_of(Z2, 2 * Z2), one_of(0, 3 * Z2)
    down_masks = one_of(2 * Z2 - 1, 3 * Z2 - 1), one_of(Z2 - 1, 4 * Z2 - 1)
    near_z = lane8 % Z2 < Z2 // 2
    for xd in range(nx):
        blocks = []
        for zd in range(3):
            b = raw_b[xd, zd, :8]
            if xd > 0:
                b = b + jnp.where(lane8 < Z2, raw_b[xd - 1, zd, 16:], 0.0)
            if xd < nx - 1:
                b = b + jnp.where(lane8 >= 3 * Z2, raw_b[xd + 1, zd, 16:], 0.0)
            if zd > 0:
                b = b + from_z(xd, zd - 1, UP_TURN, *up_masks)
            if zd < 2:
                b = b + from_z(xd, zd + 1, DOWN_TURN, *down_masks)
            blocks.append((b, raw_b[xd, zd, 8:9], raw_b[xd, zd, 9:10]))
        low, own, high = blocks
        both = tuple(jnp.where(near_z[: h.shape[0]], h, l) for l, h in zip(low, high))
        for n, (b, down_y, up_y) in enumerate((low, high, own, both)):
            raw_e[REACH, xd, n, 8:16] = b
            raw_e[REACH, xd, n, 7:8] = down_y
            raw_e[REACH, xd, n, 16:17] = up_y
    b2_y = along_y(raw_e, 7, 10, 5, True)
    start(b2_y)

    for f in (p2, u2, p3, u3, v3, p4, wa, wb):
        n = f.shape[0]
        f[0] = jnp.zeros(f.shape[1:], F32)
        f[n - 1] = jnp.zeros(f.shape[1:], F32)

        def pad(x, _):
            f[x, :8] = jnp.zeros((8, LANES), F32)
            f[x, 8 + ROWS :] = jnp.zeros((8, LANES), F32)
            return 0

        loop(n, pad)
    for f in (v2, w2):
        loop(f.shape[0], lambda x, _: f.__setitem__(x, jnp.zeros(f.shape[1:], F32)) or 0)

    def region(blocks, x):
        lane = iota((ROWS, LANES), 1)
        part = [roll(blocks[zd], Z2 * (zd - x), 1) for zd in range(3)]
        return jnp.where(lane < Z2, part[0], jnp.where(lane < 2 * Z2, part[1], jnp.where(lane < 3 * Z2, part[2], 0.0)))

    wait(p2_y)

    def unpack_p(xd, _):
        blocks = [raw_p[:, xd, zd].reshape(ROWS, LANES) for zd in range(3)]
        for x in range(X2):
            p2[X2 * xd + x + 1, 8 : 8 + ROWS] = region(blocks, x)
        return 0

    loop(nx, unpack_p)

    def coarse(v, step):
        return 0.125 * pair_sum(pair_sum(v, step, 0), step, 1)

    def coarse_p(src, dst, step):
        def one(x, _):
            v = src[2 * x + 1, 8 : 8 + ROWS] + src[2 * x + 2, 8 : 8 + ROWS]
            dst[x + 1, 8 : 8 + ROWS] = coarse(v, step)
            return 0

        loop(dst.shape[0] - 2, one)

    coarse_p(p2, p3, 1)
    coarse_p(p3, p4, 2)

    def region_sides(field, x, step, first=8, rows=ROWS):
        v = field[x + 1, pl.ds(first, rows)]
        return v, sides(field, x, rows, first, step, roll(v, step, 1), roll(v, LANES - step, 1))

    def couple_region(p_ref, st, step, scale):
        def one(x, _):
            p, ns = region_sides(p_ref, x, step)
            cs, diag = couplings(scale, p, ns)
            for i, c in enumerate(cs):
                st[i, x] = c
            inside = p > 0.0
            st[6, x] = diag
            st[7, x] = jnp.where(inside, OMEGA / jnp.where(inside, diag, 1.0), 0.0)
            return 0

        loop(p_ref.shape[0] - 2, one)

    couple_region(p2, st2, 1, 0.5 / 16)
    couple_region(p3, st3, 2, 0.5 / 64)
    couple_region(p4, st4, 4, 0.5 / 256)

    net.finish()
    wait(b2_y)

    def unpack_b(xd, _):
        blocks = []
        for zd in range(3):

            def part(yd, rows):
                if zd == 1 or abs(yd - REACH) < 2:
                    return raw_e[yd, xd, (0, 2, 1)[zd], rows]
                v = raw_e[yd, xd, 3, rows]
                near = near_z[: v.shape[0]]
                return jnp.where(near, v, 0.0) if zd else jnp.where(near, 0.0, v)

            tiles = []
            for yd in range(2 * REACH + 1):
                b = part(yd, slice(8, 16))
                if yd > 0:
                    b = b + jnp.where(row8 == 0, part(yd - 1, slice(16, 17)), 0.0)
                if yd < 2 * REACH:
                    b = b + jnp.where(row8 == 7, part(yd + 1, slice(7, 8)), 0.0)
                tiles.append(b)
            blocks.append(jnp.concatenate(tiles, axis=0))
        for x in range(X2):
            at = X2 * xd + x
            b = region(blocks, x)
            b2[at] = b
            u2[at + 1, 8 : 8 + ROWS] = st2[7, at] * b
        return 0

    loop(nx, unpack_b)

    def remainder(u_ref, b_ref, st, x, step):
        u, us = region_sides(u_ref, x, step)
        return b_ref[x] - st[6, x] * u + weighted([st[i, x] for i in range(6)], us)

    def down(u_ref, b_ref, st, step, next_b, next_u, next_st):
        def sums(x, _):
            next_b[x] = remainder(u_ref, b_ref, st, 2 * x, step) + remainder(u_ref, b_ref, st, 2 * x + 1, step)
            return 0

        def one(x, _):
            b = coarse(next_b[x], step)
            next_b[x] = b
            next_u[x + 1, 8 : 8 + ROWS] = next_st[7, x] * b
            return 0

        loop(next_b.shape[0], sums)
        loop(next_b.shape[0], one)

    down(u2, b2, st2, 1, b3, u3, st3)
    down(u3, b3, st3, 2, b4, wa, st4)

    def relaxed(field, b, st, x, step, first=8, rows=ROWS, at=0):
        v, vs = region_sides(field, x, step, first, rows)
        s = weighted([st[i, x, at : at + rows] for i in range(6)], vs)
        return (1.0 - OMEGA) * v + st[7, x, at : at + rows] * (b[x, at : at + rows] + s)

    for src, dst in ((wa, wb), (wb, wa), (wa, wb)):

        def sweep(x, _):
            dst[x + 1, 8 : 8 + ROWS] = relaxed(src, b4, st4, x, 4)
            return 0

        loop(nx, sweep)

    near, span = OWN - 8, 24

    def up3(x, _):
        v3[x + 1, 8 : 8 + ROWS] = u3[x + 1, 8 : 8 + ROWS] + wb[x // 2 + 1, 8 : 8 + ROWS]
        return 0

    loop(2 * nx, up3)

    def relax3(x, _):
        w3[x] = relaxed(v3, b3, st3, x, 2, 8 + near, span, near)
        return 0

    loop(2 * nx, relax3)

    def up2(x, _):
        v2[x + 1, 8 : 8 + span] = u2[x + 1, 8 + near : 8 + near + span] + w3[x // 2]
        return 0

    loop(4 * nx, up2)

    def relax2(x, _):
        w2[x + 1] = relaxed(v2, b2, st2, x, 1, 8, span, near)
        return 0

    loop(4 * nx, relax2)

    wide = lax.dot_general(
        w2[pl.ds(X2 * ix, X2 + 2)].reshape((X2 + 2) * span, LANES), spread[...], (((1,), (0,)), ((), ())),
        precision=lax.Precision.HIGHEST, preferred_element_type=F32,
    ).reshape(X2 + 2, span, 2 * LANES)
    for x in range(X1 + 2):
        m = wide[(x + 1) // 2, :, :LANES]
        rw1[x, pl.ds(8, Y2, stride=2)] = m[8 : 8 + Y2]
        rw1[x, pl.ds(9, Y2, stride=2)] = m[8 : 8 + Y2]
        rw1[x, 7:8] = m[7:8]
        rw1[x, 8 + Y1 : 9 + Y1] = m[8 + Y2 : 9 + Y2]
    round_c.wait()
    both_u = merge_z(zr1[1], 2)
    inner1 = slice(8, 8 + Y1)
    for x in range(X1):
        v1[x + 1, inner1] = u1[x + 1, inner1] + rw1[x + 1, inner1]
        for y in (7, 8 + Y1):
            v1[x + 1, y : y + 1] = u1h[x + 1, y : y + 1] + rw1[x + 1, y : y + 1]
    for x in (0, X1 + 1):
        v1[x, inner1] = u1h[x, inner1] + rw1[x, inner1]
    for x in range(X2):
        h = wide[x + 1, 8 : 8 + Y2, LANES:]
        hw1[x, pl.ds(0, Y2, stride=2)] = h
        hw1[x, pl.ds(1, Y2, stride=2)] = h

    def up1(x, _):
        halo = unpack_z(both_u, 2 * x, 2, 2) + hw1[x // 2]
        v, vs = sides1(v1, x, halo)
        w = (1.0 - OMEGA) * v + st1[7, x] * (b1[x] + weighted([st1[i, x] for i in range(6)], vs))
        rw0[x, pl.ds(0, Y1, stride=2)] = w
        rw0[x, pl.ds(1, Y1, stride=2)] = w
        return 0

    def v_from(x, acc):
        for d in range(2):
            v = smooth[2 * x + d + 1, own0] + rw0[x]
            vn[0, 2 * x + d + 1, own0] = v
            acc = pack_z(acc, v, 4 * (2 * x + d), 1)
        return acc

    loop(X1, up1)
    zs0[2, 0] = loop(X1, v_from, zero)

    z_ways = ((1, 1), (0, -1))
    round_f = edge_copies(vn, (0,), zs0.at[2, 0], exy, exz, eyz)
    round_f[8:8] = [net.copy(zs0.at[2, 0], zf.at[1 - i, 0], (0, 0, d)) for i, d in z_ways]
    start(round_f)

    def last_part(x, acc):
        _, vs = inside0(vn, x, (0,))
        n = rhs[x] + sum0(x, vs)
        part[x] = n
        return pack_z(acc, n, 4 * x, 1)

    zs0[2, 1] = loop(X0, last_part, zero)
    for x in (0, X0 - 1):
        vn[1, x + 1, own0] = part[x]
    for y in (0, Y0 - 1):
        vn[1, 1 : X0 + 1, 8 + y : 9 + y] = part[:, y : y + 1]
    round_n = face_copies(
        vn, (slice(None),), lambda i: xf.at[i], lambda i: yf.at[i, :, :, pl.ds(0, 1)],
        zs0.at[2, 1], lambda i: zf.at[i, 1],
    )
    start(round_n)
    wait(round_f + round_n)

    edge_x = [cross_z(exz[i, 0], exz[i, 1]) for i in range(2)]
    edge_y = [cross_z(eyz[i, 0], eyz[i, 1]) for i in range(2)]
    cross_v = cross_z(zf[0, 0], zf[1, 0])
    n = cross_z(zf[0, 1], zf[1, 1]) + cz[...] * zs0[2, 0]
    for k, v in enumerate(to_z_faces(edge_x, edge_y)):
        n = n + rims[k] * v
    sum_x = cz[...] * ((1.0 - OMEGA) * cross_v + kz[...] * n)
    z_part = cz[...] * cross_v
    row0 = iota((Y0, LANES), 0)
    for (i, x), (_, far) in zip(ends, far_x):
        vh = xf[i, 0]
        n = xf[i, 1] + st0[i, x] * vn[0, x + 1, own0] + cxz[i] * at_edges(edge_x[i], 4 * far, 4)
        for j, y in rows0:
            n = n + jnp.where(row0 == y, rims[4 + 2 * i + j, :1] * exy[i, j, :1], 0.0)
        sol[X0 + 1 if i else 0, own0] = (1.0 - OMEGA) * vh + kx[i] * n
        part[x] += st0[i, x] * vh
    for i, j, r in far_y:
        crossed[i] = edge_y[i]
        for k, x in ends:
            yf[i, 1, x, :1] += rims[8 + 2 * i + k, :1] * exy[k, i, :1]

    def last_y(x, _):
        for (i, y), (_, j, r) in zip(rows0, far_y):
            row = slice(y, y + 1)
            vh = yf[i, 0, x, :1]
            c = st0[2 + i, x, row]
            n = yf[i, 1, x, :1] + c * vn[0, x + 1, 8 + y : 9 + y]
            n = n + cyz[i, x, :1] * edge_of_y(crossed[i, r : r + 1], x, j)
            at = 8 + Y0 if i else 7
            sol[x + 1, at : at + 1] = (1.0 - OMEGA) * vh + ky[i, x, :1] * n
            part[x, row] += c * vh
        return 0

    loop(X0, last_y)

    def last_z(x, _):
        n = part[x] + at_edges(z_part, 4 * x, 4)
        s = (1.0 - OMEGA) * vn[0, x + 1, own0] + st0[7, x] * n
        sol[x + 1, own0] = s
        sol_ref[x] = s
        return 0

    loop(X0, last_z)

    def residual(x, _):
        res_ref[x] = remainder0(sol, x, sum_x)
        return 0

    loop(X0, residual)
    net.finish()


def scratch(nx):
    def vmem(*shape):
        return pltpu.VMEM(shape + (LANES,), F32)

    padded0 = (X0 + 2, Y0 + 16)
    padded1 = (X1 + 2, Y1 + 16)
    n2, n3, n4, tall = 4 * nx, 2 * nx, nx, ROWS + 16
    reach = 2 * REACH + 1
    return [
        vmem(X0, Y0), vmem(2, *padded0), vmem(*padded0), vmem(2, *padded0), vmem(*padded0),
        vmem(8, X0, Y0), vmem(3, 2, 8), vmem(1, 2, 8), vmem(X0, Y0), vmem(8), vmem(8),
        vmem(2, 2, Y0), vmem(2, 2, X0, 8), vmem(2, 2, 8), vmem(2, Y0), vmem(2, X0, 8), vmem(2, 8),
        vmem(2, 2, Y0), vmem(2, 2, X0, 8), vmem(2, 2, 8),
        vmem(2, 2, 8), vmem(2, 2, 8), vmem(2, 2, 8), vmem(2, 2, 8), vmem(2, 2, 8), vmem(2, 2, 8),
        vmem(2, Y0), vmem(2, X0, 8), vmem(8), vmem(2, Y0), vmem(2, X0, 8), vmem(12, 8), vmem(2, 8),
        vmem(*padded1), vmem(*padded1), vmem(*padded1), vmem(*padded1), vmem(*padded1), vmem(X1, Y1), vmem(8, X1, Y1),
        vmem(X1, Y0), vmem(X2, Y1), vmem(X1, Y0), vmem(2, 8), vmem(2, 2, 8),
        vmem(X2 * LANES), pltpu.VMEM((LANES, 2 * LANES), F32),
        pltpu.VMEM((24, X2 * LANES), F32),
        vmem(reach, nx, 3, 8), vmem(nx, 3, 24), vmem(reach, nx, 4, 24),
        vmem(n2 + 2, tall), vmem(n2 + 2, tall), vmem(n2, ROWS), vmem(8, n2, ROWS),
        vmem(n3 + 2, tall), vmem(n3 + 2, tall), vmem(n3 + 2, tall), vmem(n3, ROWS), vmem(8, n3, ROWS),
        vmem(n4 + 2, tall), vmem(n4 + 2, tall), vmem(n4 + 2, tall), vmem(n4, ROWS), vmem(8, n4, ROWS),
        vmem(n3, 24), vmem(n2 + 2, 40), vmem(n2 + 2, 24),
        pltpu.SemaphoreType.DMA((3,)), pltpu.SemaphoreType.DMA((SEMS,)), pltpu.SemaphoreType.DMA((SEMS,)),
    ]


def solution(mesh):
    sizes = tuple(mesh.shape[a] for a in ("gx", "gy", "gz"))
    block = jax.ShapeDtypeStruct((X0, Y0, LANES), F32)
    spec = P("gx", "gy", "gz")

    def shards(right_side, dielectric, guess):
        return pl.pallas_call(
            functools.partial(kernel, sizes),
            out_shape=(block, block),
            in_specs=[pl.BlockSpec(memory_space=pl.ANY)] * 3,
            out_specs=[pl.BlockSpec(memory_space=pltpu.VMEM)] * 2,
            scratch_shapes=scratch(sizes[0]),
            compiler_params=pltpu.CompilerParams(
                collective_id=0, has_side_effects=True, vmem_limit_bytes=213 * 2**18
            ),
            name="vcycle",
        )(right_side, dielectric, guess)

    return jax.shard_map(
        shards, mesh=mesh, in_specs=(spec, spec, spec), out_specs=(spec, spec), check_vma=False
    )
```

```python
import functools

import jax
import jax.numpy as jnp
from jax import lax
from jax.experimental import pallas as pl
from jax.experimental.pallas import tpu as pltpu
from jax.sharding import PartitionSpec as P

OMEGA = 0.8
MESH = pl.DeviceIdType.MESH
F32 = jnp.float32

X0, Y0, LANES = 16, 32, 128
X1, Y1 = 8, 16
X2, Y2, Z2 = 4, 8, 32
REACH = 3
ROWS = (2 * REACH + 1) * Y2
OWN = REACH * Y2


def iota(shape, dim):
    return lax.broadcasted_iota(jnp.int32, shape, dim)


def roll(v, shift, axis):
    size = v.shape[axis]
    if isinstance(shift, int):
        shift = shift % size
        if shift == 0:
            return v
    return pltpu.roll(v, shift, axis=axis)


def loop(count, body, init=0, unroll=True):
    return lax.fori_loop(0, count, body, init, unroll=unroll)


class Faces:
    def __init__(self, net, field, into, sent, got, nx, ny):
        self.net = net
        self.copies = {}
        lead = (slice(None),) * (len(field.shape) - 3)
        for d in (-1, 1):
            src, dst = (1, nx + 1) if d < 0 else (nx, 0)
            self.copies[(d, 0, 0)] = net.copy(
                field.at[lead + (src, pl.ds(8, ny))], into.at[lead + (dst, pl.ds(8, ny))], (d, 0, 0)
            )
            src, dst = (8, 8 + ny) if d < 0 else (7 + ny, 7)
            self.copies[(0, d, 0)] = net.copy(
                field.at[lead + (pl.ds(1, nx), pl.ds(src, 1))],
                into.at[lead + (pl.ds(1, nx), pl.ds(dst, 1))],
                (0, d, 0),
            )
            self.copies[(0, 0, d)] = net.copy(sent, got.at[0 if d > 0 else 1], (0, 0, d))

    def start(self):
        order = ((0, 0, 1), (0, 0, -1), (1, 0, 0), (-1, 0, 0), (0, 1, 0), (0, -1, 0))
        self.net.start([self.copies[way] for way in order])

    def wait(self):
        self.net.wait_recv(list(self.copies.values()))


class Net:
    def __init__(self, sizes, send_sems, recv_sems):
        self.me = tuple(lax.axis_index(a) for a in ("gx", "gy", "gz"))
        self.sizes = sizes
        self.send_sems, self.recv_sems = send_sems, recv_sems
        self.used = 0
        self.started = []

    def there(self, way):
        found = None
        for at, size, d in zip(self.me, self.sizes, way):
            if d:
                ok = (at + d < size) if d > 0 else (at + d >= 0)
                found = ok if found is None else jnp.logical_and(found, ok)
        return found

    def when(self, way):
        found = self.there(way)
        return (lambda f: f()) if found is None else pl.when(found)

    def device(self, way, turn=0):
        x = self.me[0] + way[0]
        if turn:
            x = lax.rem(x + turn, self.sizes[0])
        return (x, self.me[1] + way[1], self.me[2] + way[2])

    def copy(self, src, dst, way, turn=0):
        i = self.used
        self.used += 1
        made = pltpu.make_async_remote_copy(
            src_ref=src,
            dst_ref=dst,
            send_sem=self.send_sems.at[i],
            recv_sem=self.recv_sems.at[i],
            device_id=self.device(way, turn),
            device_id_type=MESH,
        )
        return (made, way)

    def each(self, copies, act):
        ways = {way for _, way in copies if any(way)}
        if not ways:
            for made, _ in copies:
                act(made)
            return
        found = functools.reduce(jnp.logical_and, [self.there(way) for way in sorted(ways)])

        @pl.when(found)
        def _():
            for made, _ in copies:
                act(made)

        @pl.when(jnp.logical_not(found))
        def _():
            for made, way in copies:

                @self.when(way)
                def _():
                    act(made)

    def start(self, copies):
        self.started += copies
        self.each(copies, lambda made: made.start())

    def wait_recv(self, copies):
        self.each([(made, tuple(-d for d in way)) for made, way in copies], lambda made: made.wait_recv())

    def finish(self):
        started, self.started = self.started, []
        self.each(started, lambda made: made.wait_send())


SEMS = 104

DOWN_Z, DOWN_TURN = (92, 63, 95, 60), 67
UP_Z, UP_TURN = (66, 32, 64, 34), 62


def pack_z(acc, v, first, w):
    group = iota((8, LANES), 1) // (2 * w)
    for j in range(v.shape[0] // 8):
        k = first + j
        acc = jnp.where(group == k, roll(v[8 * j : 8 * j + 8], (2 * k + 1) * w, 1), acc)
    return acc


def cross_z(left, right):
    odd = iota((8, LANES), 1) % 2 == 1
    return jnp.where(odd, roll(left, 1, 1), roll(right, LANES - 1, 1))


def at_edges(packed, first, tiles):
    v = jnp.concatenate([roll(packed, LANES - (2 * (first + j) + 1), 1) for j in range(tiles)], axis=0)
    lane = iota(v.shape, 1)
    return jnp.where(jnp.logical_or(lane == 0, lane == LANES - 1), v, 0.0)


def merge_z(got, w):
    return jnp.where((iota((8, LANES), 1) // w) % 2 == 0, got[0], got[1])


def unpack_z(both, first, tiles, w):
    return jnp.concatenate([roll(both, LANES - (2 * (first + j) + 1) * w, 1) for j in range(tiles)], axis=0)


def z_sides(v, halo, w):
    lane = iota(v.shape, 1)
    below = roll(jnp.where(lane >= LANES - w, halo, v), w, 1)
    above = roll(jnp.where(lane < w, halo, v), LANES - w, 1)
    return below, above


def sides(field, x, rows, first, step, below, above, lead=()):
    f = lambda dx, dy: field[lead + (x + 1 + dx, pl.ds(first + dy, rows))]
    return (f(-1, 0), f(1, 0), f(0, -step), f(0, step), below, above)


def weighted(cs, vs):
    total = cs[0] * vs[0]
    for c, v in zip(cs[1:], vs[1:]):
        total = total + c * v
    return total


def pair_sum(v, step, axis):
    if axis == 0 and v.shape[0] > 8:
        tiles = [pair_sum(v[i : i + 8], step, 0) for i in range(0, v.shape[0], 8)]
        return jnp.concatenate(tiles, axis=0)
    size = v.shape[axis]
    if 2 * step == size:
        return v + roll(v, step, axis)
    even = (iota(v.shape, axis) // step) % 2 == 0
    return v + jnp.where(even, roll(v, size - step, axis), roll(v, step, axis))


def kernel(
    sizes,
    rhs_hbm, permit_hbm, guess_hbm,
    sol_ref, res_ref,
    rhs, gp, smooth, vn, sol, st0, zs0, zr0, part, pack_d, cz,
    xa, ya, za, xd, yd, zd, xf, yf, zf, exy, exz, eyz, pxy, pxz, pyz,
    kx, ky, kz, cxz, cyz, rims, crossed,
    p1, u1, u1h, v1, rw1, b1, st1, tmp, hw1, rw0, zs1, zr1, pick, spread, lhs,
    raw_p, raw_b, raw_e, p2, u2, b2, st2, p3, u3, v3, b3, st3, p4, wa, wb, b4, st4, w3, v2, w2,
    local_sems, send_sems, recv_sems,
):
    nx = sizes[0]
    net = Net(sizes, send_sems, recv_sems)
    ix, iy, iz = net.me
    inner0 = (pl.ds(1, X0), pl.ds(8, Y0))
    own0 = slice(8, 8 + Y0)

    ways = [(0, 0, 1), (0, 0, -1), (1, 0, 0), (-1, 0, 0), (0, 1, 0), (0, -1, 0)]
    greeted = ways + [(2, 0, 0), (-2, 0, 0)]
    barrier = pltpu.get_barrier_semaphore()
    for way in greeted:

        @net.when(way)
        def _():
            pl.semaphore_signal(barrier, inc=1, device_id=net.device(way), device_id_type=MESH)

    loads = [
        pltpu.make_async_copy(permit_hbm, gp.at[(1,) + inner0], local_sems.at[1]),
        pltpu.make_async_copy(guess_hbm, gp.at[(0,) + inner0], local_sems.at[0]),
        pltpu.make_async_copy(rhs_hbm, rhs, local_sems.at[2]),
    ]
    for load in loads:
        load.start()

    signs = (-1, 1)
    zeros = lambda *shape: jnp.zeros(shape + (LANES,), F32)

    def clear(fields, landings):
        todo = {}
        for f, fx, fy in fields:
            for i, d in enumerate(signs):
                todo.setdefault((d, 0, 0), []).append((f, (fx + 1 if i else 0,)))
                todo.setdefault((0, d, 0), []).append((f, (pl.ds(1, fx), pl.ds(8 + fy if i else 7, 1))))
        for ref, at, way in landings:
            todo.setdefault(way, []).append((ref, at))
        for way, items in todo.items():

            @pl.when(jnp.logical_not(net.there(way)))
            def _():
                for ref, at in items:
                    ref[at] = jnp.zeros(ref.at[at].shape, F32)

    def landings(x, y, z):
        return [(ref, (i,), tuple(d if n == axis else 0 for n in range(3)))
                for axis, ref in enumerate((x, y, z)) for i, d in enumerate(signs)]

    def edge_landings(xy, xz, yz):
        out = []
        for i, d in enumerate(signs):
            for j, e in enumerate(signs):
                out += [(xy, (i, j), (d, e, 0)), (xz, (i, j), (d, 0, e)), (yz, (i, j), (0, d, e))]
        return out

    def zero_halo(f, lead=(), fx=X0, fy=Y0):
        for x in (0, fx + 1):
            f[lead + (x,)] = zeros(fy + 16)

        def one(x, _):
            f[lead + (x + 1, slice(0, 8))] = zeros(8)
            f[lead + (x + 1, slice(8 + fy, 16 + fy))] = zeros(8)
            return 0

        loop(fx, one)

    zero_halo(gp, (0,))
    zero_halo(gp, (1,))
    zero_halo(vn, (0,))
    zero_halo(u1, (), X1, Y1)
    lhs[...] = jnp.zeros(lhs.shape, F32)
    clear([], landings(xa, ya, za))
    clear([(p1, X1, Y1), (u1h, X1, Y1), (smooth, X0, Y0)], [
        (zr, (r, i), (0, 0, d)) for zr, n in ((zr1, 2), (zr0, 1)) for r in range(n) for i, d in enumerate(signs)
    ])
    for x in range(X2):
        row, col = iota((LANES, LANES), 0), iota((LANES, LANES), 1)
        take = jnp.logical_and(col == Z2 * x + row // 4, row % 2 == 0)
        pick[pl.ds(x * LANES, LANES)] = jnp.where(take, 0.125, 0.0).astype(F32)
    row, col = iota((LANES, LANES), 0), iota((LANES, LANES), 1)
    spread[:, :LANES] = (row == Z2 + col // 4).astype(F32)
    left = jnp.logical_and(row == Z2 - 1, col >= LANES - 2)
    right = jnp.logical_and(row == 2 * Z2, col < 2)
    spread[:, LANES:] = jnp.logical_or(left, right).astype(F32)

    steps = [d for k in range(REACH, 0, -1) for d in (k, -k)]
    raw_p[0, :, :, :4] = zeros(nx, 3, 4)
    raw_p[2 * REACH, :, :, 4:] = zeros(nx, 3, 4)
    raw_e[0, :, :, :13] = zeros(nx, 4, 13)
    raw_e[2 * REACH, :, :, 11:] = zeros(nx, 4, 13)
    for d in steps:

        @pl.when(jnp.logical_not(net.there((0, d, 0))))
        def _():
            raw_p[REACH + d] = zeros(nx, 3, 8)
            raw_e[REACH + d] = zeros(nx, 4, 24)

    for d in signs:

        @pl.when(jnp.logical_not(net.there((0, 0, d))))
        def _():
            raw_p[REACH, ix, 1 + d] = zeros(8)
            raw_b[:, 1 + d] = zeros(nx, 24)

    loads[0].wait()
    loads[1].wait()

    lane0 = iota((Y0, LANES), 1)

    def couplings(scale, p, ns):
        cs = [scale * (p + n) for n in ns]
        return cs, cs[0] + cs[1] + cs[2] + cs[3] + cs[4] + cs[5]

    def inside0(field, x, lead=()):
        v = field[lead + (x + 1, pl.ds(8, Y0))]
        return v, sides(field, x, Y0, 8, 1, roll(v, 1, 1), roll(v, LANES - 1, 1), lead=lead)

    def sum0(x, vs):
        return weighted([st0[i, x] for i in range(6)], vs)

    zero = zeros(8)
    accs = loop(X0, lambda x, accs: tuple(
        pack_z(a, gp[i, x + 1, 8 : 8 + Y0], 4 * x, 1) for i, a in enumerate(accs)
    ), (zero, zero))
    zs0[0, 0] = accs[0]
    zs0[0, 1] = accs[1]

    pl.semaphore_wait(barrier, sum(net.there(way).astype(jnp.int32) for way in greeted))

    def face_copies(field, lead, x_to, y_to, z_from, z_to):
        copies = []
        for i, d in ((1, 1), (0, -1)):
            copies.append(net.copy(z_from, z_to(1 - i), (0, 0, d)))
        for i, d in ((1, 1), (0, -1)):
            copies.append(net.copy(field.at[lead + (X0 if i else 1, pl.ds(8, Y0))], x_to(1 - i), (d, 0, 0)))
        for i, d in ((1, 1), (0, -1)):
            row = 7 + Y0 if i else 8
            copies.append(net.copy(field.at[lead + (pl.ds(1, X0), pl.ds(row, 1))], y_to(1 - i), (0, d, 0)))
        return copies

    def edge_copies(field, lead, packed, xy, xz, yz):
        copies = []
        for i, d in enumerate(signs):
            for j, e in enumerate(signs):
                copies.append(net.copy(packed, xz.at[1 - i, 1 - j], (d, 0, e)))
                copies.append(net.copy(packed, yz.at[1 - i, 1 - j], (0, d, e)))
        for i, d in enumerate(signs):
            for j, e in enumerate(signs):
                line = field.at[lead + (X0 if i else 1, pl.ds(7 + Y0 if j else 8, 1))]
                copies.append(net.copy(line, xy.at[1 - i, 1 - j, pl.ds(0, 1)], (d, e, 0)))
        return copies

    start, wait = net.start, net.wait_recv

    round_a = face_copies(
        gp, (slice(None),), lambda i: xa.at[i], lambda i: ya.at[i, :, :, pl.ds(0, 1)],
        zs0.at[0], lambda i: za.at[i],
    )
    start(round_a)
    loads[2].wait()

    def first(x, _):
        p, ns = inside0(gp, x, (1,))
        ns = ns[:4] + (jnp.where(lane0 == 0, 0.0, ns[4]), jnp.where(lane0 == LANES - 1, 0.0, ns[5]))
        cs, diag = couplings(0.5, p, ns)
        cs[4] = jnp.where(lane0 == 0, 0.0, cs[4])
        cs[5] = jnp.where(lane0 == LANES - 1, 0.0, cs[5])
        for i, c in enumerate(cs):
            st0[i, x] = c
        st0[6, x] = diag
        v, vs = inside0(gp, x, (0,))
        part[x] = rhs[x] + weighted(cs, vs)
        return 0

    loop(X0, first)

    def coarse_p1(x, acc):
        tmp[x] = gp[1, 2 * x + 1, 8 : 8 + Y0] + gp[1, 2 * x + 2, 8 : 8 + Y0]
        v = tmp[x, pl.ds(0, Y1, stride=2)] + tmp[x, pl.ds(1, Y1, stride=2)]
        v = 0.125 * pair_sum(v, 1, 1)
        p1[x + 1, 8 : 8 + Y1] = v
        return pack_z(acc, v, 2 * x, 2)

    zs1[0] = loop(X1, coarse_p1, zero)
    faces_p1 = Faces(net, p1, p1, zs1.at[0], zr1.at[0], X1, Y1)
    faces_p1.start()

    def to_compact(parts):
        return lax.dot_general(
            parts, pick[...], (((1,), (0,)), ((), ())),
            precision=lax.Precision.HIGHEST, preferred_element_type=F32,
        )

    def compact(planes):
        parts = []
        for x in range(X2):
            tmp[x, :Y1] = planes(2 * x) + planes(2 * x + 1)
            parts.append(tmp[x, pl.ds(0, Y2, stride=2)] + tmp[x, pl.ds(1, Y2, stride=2)])
        return to_compact(jnp.concatenate(parts, axis=1))

    def along_y(raw, first, rows, half, packed=False):
        copies = []
        for d in steps:
            span = pl.ds(first, rows)
            if abs(d) == REACH:
                span = pl.ds(first + rows - half if d > 0 else first, half)
            slots = pl.ds(2, 2) if packed and abs(d) > 1 else pl.ds(0, 3)
            copies.append(net.copy(raw.at[REACH, :, slots, span], raw.at[REACH - d, :, slots, span], (0, d, 0)))
        return copies

    raw_p[REACH, ix, 1] = compact(lambda x: p1[x + 1, 8 : 8 + Y1])
    p2_z = [net.copy(raw_p.at[REACH, ix, 1], raw_p.at[REACH, ix, 1 - d], (0, 0, d)) for d in (1, -1)]
    start(p2_z)
    wait(round_a)
    own_p = zs0[0, 1]
    cross_p = cross_z(za[0, 1], za[1, 1])
    cz[...] = 0.5 * (own_p + cross_p)
    z_part = cz[...] * cross_z(za[0, 0], za[1, 0])
    z_diag = 0.5 * cross_p
    ends = ((0, 0), (1, X0 - 1))
    rows0 = ((0, 0), (1, Y0 - 1))
    for i, x in ends:
        ph = xa[i, 1]
        c = 0.5 * (gp[1, x + 1, own0] + ph)
        st0[i, x] = c
        st0[6, x] += 0.5 * ph
        part[x] += c * xa[i, 0]

    def first_y(x, _):
        for i, y in rows0:
            row = slice(y, y + 1)
            ph = ya[i, 1, x, :1]
            c = 0.5 * (gp[1, x + 1, 8 + y : 9 + y] + ph)
            st0[2 + i, x, row] = c
            st0[6, x, row] += 0.5 * ph
            part[x, row] += c * ya[i, 0, x, :1]
        return 0

    loop(X0, first_y)

    def first_z(x, acc):
        diag = st0[6, x] + at_edges(z_diag, 4 * x, 4)
        inv = OMEGA / diag
        st0[6, x] = diag
        st0[7, x] = inv
        s = (1.0 - OMEGA) * gp[0, x + 1, own0] + inv * (part[x] + at_edges(z_part, 4 * x, 4))
        smooth[x + 1, own0] = s
        return pack_z(acc, s, 4 * x, 1)

    zs0[1, 0] = loop(X0, first_z, zero)

    round_b = Faces(net, smooth, smooth, zs0.at[1, 0], zr0.at[0], X0, Y0)
    round_b.start()

    faces_p1.wait()
    both_p1 = merge_z(zr1[0], 2)

    def sides1(field, x, halo):
        v = field[x + 1, 8 : 8 + Y1]
        return v, sides(field, x, Y1, 8, 1, *z_sides(v, halo, 2))

    def couple1(x, _):
        p, ns = sides1(p1, x, unpack_z(both_p1, 2 * x, 2, 2))
        cs, diag = couplings(0.125, p, ns)
        for i, c in enumerate(cs):
            st1[i, x] = c
        st1[6, x] = diag
        st1[7, x] = OMEGA / diag
        return 0

    loop(X1, couple1)

    pack_d[...] = loop(X0, lambda x, acc: pack_z(acc, st0[6, x], 4 * x, 1), zero)

    wait(p2_z)
    p2_x = [net.copy(raw_p.at[REACH, ix], raw_p.at[REACH, ix], (0, 0, 0), k) for k in range(1, nx)]
    start(p2_x)

    clear([], landings(xd, yd, zd) + landings(xf, yf, zf) + edge_landings(exy, exz, eyz) + edge_landings(pxy, pxz, pyz))
    static = edge_copies(gp, (1,), zs0.at[0, 1], pxy, pxz, pyz)
    for i, d in ((1, 1), (0, -1)):
        static.append(net.copy(pack_d, zd.at[1 - i], (0, 0, d)))
        static.append(net.copy(st0.at[6, X0 - 1 if i else 0], xd.at[1 - i], (d, 0, 0)))
        static.append(net.copy(
            st0.at[6, :, pl.ds(Y0 - 1 if i else 0, 1)], yd.at[1 - i, :, pl.ds(0, 1)], (0, d, 0)
        ))
    start(static)

    round_b.wait()

    def remainder0(field, x, z_sum):
        v, vs = inside0(field, x)
        return rhs[x] - st0[6, x] * v + sum0(x, vs) + at_edges(z_sum, 4 * x, 4)

    sum_s = cz[...] * cross_z(zr0[0, 0], zr0[0, 1])

    def remainders0(x, _):
        tmp[x] = remainder0(smooth, 2 * x, sum_s) + remainder0(smooth, 2 * x + 1, sum_s)
        return 0

    def down0(x, acc):
        b = tmp[x, pl.ds(0, Y1, stride=2)] + tmp[x, pl.ds(1, Y1, stride=2)]
        b = 0.125 * pair_sum(b, 1, 1)
        b1[x] = b
        u = st1[7, x] * b
        u1[x + 1, 8 : 8 + Y1] = u
        return pack_z(acc, u, 2 * x, 2)

    loop(X1, remainders0)
    zs1[1] = loop(X1, down0, zero)


    lane16 = iota((Y1, LANES), 1)
    nothing = jnp.zeros((Y1, LANES), F32)

    def remainder1(x):
        u, us = sides1(u1, x, nothing)
        return b1[x] - st1[6, x] * u + weighted([st1[i, x] for i in range(6)], us)

    def halve(at):
        return tmp[at, pl.ds(0, Y2, stride=2)] + tmp[at, pl.ds(1, Y2, stride=2)]

    lane8 = iota((8, LANES), 1)
    z_out = zero
    for x in range(X2):
        pair = (2 * x, 2 * x + 1)
        tmp[x, :Y1] = remainder1(pair[0]) + remainder1(pair[1])
        out = [
            jnp.where(lane16 == 0, st1[4, k], jnp.where(lane16 == LANES - 1, st1[5, k], 0.0)) * u1[k + 1, 8 : 8 + Y1]
            for k in pair
        ]
        tmp[X2 + x, :Y1] = out[0] + out[1]
        for i, y in ((0, 0), (1, Y1 - 1)):
            lhs[8 + i : 9 + i, x * LANES : (x + 1) * LANES] = sum(
                st1[2 + i, k, y : y + 1] * u1[k + 1, 8 + y : 9 + y] for k in pair
            )
    x_out = ((0, 0, X2 - 1), (1, X1 - 1, 0))
    for i, x, _ in x_out:
        tmp[i, Y1:] = st1[i, x] * u1[x + 1, 8 : 8 + Y1]
    for x in range(X2):
        lhs[:8, x * LANES : (x + 1) * LANES] = halve(x)
        out = 0.125 * halve(X2 + x)
        z_out = z_out + jnp.where(lane8 == DOWN_Z[x], roll(out, DOWN_Z[x], 1), 0.0)
        z_out = z_out + jnp.where(lane8 == UP_Z[x], roll(out, UP_Z[x] + 1, 1), 0.0)
    for i, _, to in x_out:
        lhs[16:, to * LANES : (to + 1) * LANES] = (
            tmp[i, pl.ds(Y1, Y2, stride=2)] + tmp[i, pl.ds(Y1 + 1, Y2, stride=2)]
        )
    known = to_compact(lhs[...])
    raw_b[ix, 1, :10] = known[:10]
    raw_b[ix, 1, 10:18] = known[16:] + z_out

    mine = raw_b.at[ix, 1, pl.ds(0, 18)]
    b2_xz = []
    for d in (1, -1, 0):
        for k in sorted(range(nx), key=lambda k: -min(k, nx - k)):
            if d or k:
                b2_xz.append(net.copy(mine, raw_b.at[ix, 1 - d, pl.ds(0, 18)], (0, 0, d), k))
    start(b2_xz)

    round_c = Faces(net, u1, u1h, zs1.at[1], zr1.at[1], X1, Y1)
    round_c.start()

    wait(p2_x)
    p2_y = along_y(raw_p, 0, 8, 4)
    start(p2_y)

    wait(static)
    row8 = iota((8, LANES), 0)

    def inverse(p, diag):
        inside = p > 0.0
        return jnp.where(inside, OMEGA / jnp.where(inside, diag, 1.0), 0.0)

    def to_z_faces(x_edges, y_edges):
        return (
            roll(x_edges[0], 8, 1), roll(x_edges[1], LANES - 8, 1),
            roll(roll(y_edges[0], LANES - 6, 1), 1, 0), roll(roll(y_edges[1], 6, 1), 7, 0),
        )

    quarter = (lane8 // 2) % 4
    z_masks = (
        lane8 < 8, lane8 >= LANES - 8,
        jnp.logical_and(quarter == 0, row8 == 0), jnp.logical_and(quarter == 3, row8 == 7),
    )
    far_x = ((0, X0 - 1), (1, 0))
    far_y = ((0, 3, 7), (1, 0, 0))
    kz[...] = inverse(cross_p, cross_z(zd[0], zd[1]))
    edge_x = [cross_z(pxz[i, 0], pxz[i, 1]) for i in range(2)]
    edge_y = [cross_z(pyz[i, 0], pyz[i, 1]) for i in range(2)]
    for n, (mask, p) in enumerate(zip(z_masks, to_z_faces(edge_x, edge_y))):
        rims[n] = jnp.where(mask, 0.5 * (cross_p + p), 0.0)
    edge_lane = jnp.logical_or(lane0 == 0, lane0 == LANES - 1)
    for i, x in far_x:
        ph = xa[i, 1]
        kx[i] = inverse(ph, xd[i])
        cxz[i] = jnp.where(edge_lane, 0.5 * (ph + at_edges(edge_x[i], 4 * x, 4)), 0.0)
        for j, y in rows0:
            rims[4 + 2 * i + j, :1] = 0.5 * (ph[y : y + 1] + pxy[i, j, :1])
    for i, j, r in far_y:
        crossed[i] = edge_y[i]
        for k, x in ends:
            rims[8 + 2 * i + k, :1] = 0.5 * (ya[i, 1, x, :1] + pxy[k, i, :1])

    edge_row = jnp.logical_or(iota((1, LANES), 1) == 0, iota((1, LANES), 1) == LANES - 1)

    def edge_of_y(packed, x, j):
        return roll(packed, LANES - (2 * (4 * x + j) + 1), 1)

    def static_y(x, _):
        for i, j, r in far_y:
            ph = ya[i, 1, x, :1]
            ky[i, x, :1] = inverse(ph, yd[i, x, :1])
            p = edge_of_y(crossed[i, r : r + 1], x, j)
            cyz[i, x, :1] = jnp.where(edge_row, 0.5 * (ph + p), 0.0)
        return 0

    loop(X0, static_y)

    wait(b2_xz)
    def one_of(*lanes):
        return jnp.logical_or(lane8 == lanes[0], lane8 == lanes[1])

    def from_z(xd, zd, turn, straight, turned):
        f = raw_b[xd, zd, 10:18]
        return jnp.where(straight, f, jnp.where(turned, roll(f, turn, 1), 0.0))

    up_masks = one_of(Z2, 2 * Z2), one_of(0, 3 * Z2)
    down_masks = one_of(2 * Z2 - 1, 3 * Z2 - 1), one_of(Z2 - 1, 4 * Z2 - 1)
    near_z = lane8 % Z2 < Z2 // 2
    for xd in range(nx):
        blocks = []
        for zd in range(3):
            b = raw_b[xd, zd, :8]
            if xd > 0:
                b = b + jnp.where(lane8 < Z2, raw_b[xd - 1, zd, 10:18], 0.0)
            if xd < nx - 1:
                b = b + jnp.where(lane8 >= 3 * Z2, raw_b[xd + 1, zd, 10:18], 0.0)
            if zd > 0:
                b = b + from_z(xd, zd - 1, UP_TURN, *up_masks)
            if zd < 2:
                b = b + from_z(xd, zd + 1, DOWN_TURN, *down_masks)
            blocks.append((b, raw_b[xd, zd, 8:9], raw_b[xd, zd, 9:10]))
        low, own, high = blocks
        both = tuple(jnp.where(near_z[: h.shape[0]], h, l) for l, h in zip(low, high))
        for n, (b, down_y, up_y) in enumerate((low, high, own, both)):
            raw_e[REACH, xd, n, 8:16] = b
            raw_e[REACH, xd, n, 7:8] = down_y
            raw_e[REACH, xd, n, 16:17] = up_y
    b2_y = along_y(raw_e, 7, 10, 4, True)
    start(b2_y)

    for f in (p2, u2, p3, u3, v3, p4, wa, wb):
        n = f.shape[0]
        f[0] = jnp.zeros(f.shape[1:], F32)
        f[n - 1] = jnp.zeros(f.shape[1:], F32)

        def pad(x, _):
            f[x, :8] = jnp.zeros((8, LANES), F32)
            f[x, 8 + ROWS :] = jnp.zeros((8, LANES), F32)
            return 0

        loop(n, pad)
    for f in (v2, w2):
        loop(f.shape[0], lambda x, _: f.__setitem__(x, jnp.zeros(f.shape[1:], F32)) or 0)

    def region(blocks, x):
        lane = iota((ROWS, LANES), 1)
        part = [roll(blocks[zd], Z2 * (zd - x), 1) for zd in range(3)]
        return jnp.where(lane < Z2, part[0], jnp.where(lane < 2 * Z2, part[1], jnp.where(lane < 3 * Z2, part[2], 0.0)))

    wait(p2_y)

    def unpack_p(xd, _):
        blocks = [raw_p[:, xd, zd].reshape(ROWS, LANES) for zd in range(3)]
        for x in range(X2):
            p2[X2 * xd + x + 1, 8 : 8 + ROWS] = region(blocks, x)
        return 0

    loop(nx, unpack_p)

    def coarse(v, step):
        return 0.125 * pair_sum(pair_sum(v, step, 0), step, 1)

    def coarse_p(src, dst, step):
        def one(x, _):
            v = src[2 * x + 1, 8 : 8 + ROWS] + src[2 * x + 2, 8 : 8 + ROWS]
            dst[x + 1, 8 : 8 + ROWS] = coarse(v, step)
            return 0

        loop(dst.shape[0] - 2, one)

    coarse_p(p2, p3, 1)
    coarse_p(p3, p4, 2)

    def region_sides(field, x, step, first=8, rows=ROWS):
        v = field[x + 1, pl.ds(first, rows)]
        return v, sides(field, x, rows, first, step, roll(v, step, 1), roll(v, LANES - step, 1))

    def couple_region(p_ref, st, step, scale):
        def one(x, _):
            p, ns = region_sides(p_ref, x, step)
            cs, diag = couplings(scale, p, ns)
            for i, c in enumerate(cs):
                st[i, x] = c
            inside = p > 0.0
            st[6, x] = diag
            st[7, x] = jnp.where(inside, OMEGA / jnp.where(inside, diag, 1.0), 0.0)
            return 0

        loop(p_ref.shape[0] - 2, one)

    couple_region(p2, st2, 1, 0.5 / 16)
    couple_region(p3, st3, 2, 0.5 / 64)
    couple_region(p4, st4, 4, 0.5 / 256)

    net.finish()
    wait(b2_y)

    def unpack_b(xd, _):
        blocks = []
        for zd in range(3):

            def part(yd, rows):
                if zd == 1 or abs(yd - REACH) < 2:
                    return raw_e[yd, xd, (0, 2, 1)[zd], rows]
                v = raw_e[yd, xd, 3, rows]
                near = near_z[: v.shape[0]]
                return jnp.where(near, v, 0.0) if zd else jnp.where(near, 0.0, v)

            tiles = []
            for yd in range(2 * REACH + 1):
                b = part(yd, slice(8, 16))
                if yd > 0:
                    b = b + jnp.where(row8 == 0, part(yd - 1, slice(16, 17)), 0.0)
                if yd < 2 * REACH:
                    b = b + jnp.where(row8 == 7, part(yd + 1, slice(7, 8)), 0.0)
                tiles.append(b)
            blocks.append(jnp.concatenate(tiles, axis=0))
        for x in range(X2):
            at = X2 * xd + x
            b = region(blocks, x)
            b2[at] = b
            u2[at + 1, 8 : 8 + ROWS] = st2[7, at] * b
        return 0

    loop(nx, unpack_b)

    def remainder(u_ref, b_ref, st, x, step):
        u, us = region_sides(u_ref, x, step)
        return b_ref[x] - st[6, x] * u + weighted([st[i, x] for i in range(6)], us)

    def down(u_ref, b_ref, st, step, next_b, next_u, next_st):
        def sums(x, _):
            next_b[x] = remainder(u_ref, b_ref, st, 2 * x, step) + remainder(u_ref, b_ref, st, 2 * x + 1, step)
            return 0

        def one(x, _):
            b = coarse(next_b[x], step)
            next_b[x] = b
            next_u[x + 1, 8 : 8 + ROWS] = next_st[7, x] * b
            return 0

        loop(next_b.shape[0], sums)
        loop(next_b.shape[0], one)

    down(u2, b2, st2, 1, b3, u3, st3)
    down(u3, b3, st3, 2, b4, wa, st4)

    def relaxed(field, b, st, x, step, first=8, rows=ROWS, at=0):
        v, vs = region_sides(field, x, step, first, rows)
        s = weighted([st[i, x, at : at + rows] for i in range(6)], vs)
        return (1.0 - OMEGA) * v + st[7, x, at : at + rows] * (b[x, at : at + rows] + s)

    for src, dst in ((wa, wb), (wb, wa), (wa, wb)):

        def sweep(x, _):
            dst[x + 1, 8 : 8 + ROWS] = relaxed(src, b4, st4, x, 4)
            return 0

        loop(nx, sweep)

    near, span = OWN - 8, 24

    def up3(x, _):
        v3[x + 1, 8 : 8 + ROWS] = u3[x + 1, 8 : 8 + ROWS] + wb[x // 2 + 1, 8 : 8 + ROWS]
        return 0

    loop(2 * nx, up3)

    def relax3(x, _):
        w3[x] = relaxed(v3, b3, st3, x, 2, 8 + near, span, near)
        return 0

    loop(2 * nx, relax3)

    def up2(x, _):
        v2[x + 1, 8 : 8 + span] = u2[x + 1, 8 + near : 8 + near + span] + w3[x // 2]
        return 0

    loop(4 * nx, up2)

    def relax2(x, _):
        w2[x + 1] = relaxed(v2, b2, st2, x, 1, 8, span, near)
        return 0

    loop(4 * nx, relax2)

    wide = lax.dot_general(
        w2[pl.ds(X2 * ix, X2 + 2)].reshape((X2 + 2) * span, LANES), spread[...], (((1,), (0,)), ((), ())),
        precision=lax.Precision.HIGHEST, preferred_element_type=F32,
    ).reshape(X2 + 2, span, 2 * LANES)
    for x in range(X1 + 2):
        m = wide[(x + 1) // 2, :, :LANES]
        rw1[x, pl.ds(8, Y2, stride=2)] = m[8 : 8 + Y2]
        rw1[x, pl.ds(9, Y2, stride=2)] = m[8 : 8 + Y2]
        rw1[x, 7:8] = m[7:8]
        rw1[x, 8 + Y1 : 9 + Y1] = m[8 + Y2 : 9 + Y2]
    round_c.wait()
    both_u = merge_z(zr1[1], 2)
    inner1 = slice(8, 8 + Y1)
    for x in range(X1):
        v1[x + 1, inner1] = u1[x + 1, inner1] + rw1[x + 1, inner1]
        for y in (7, 8 + Y1):
            v1[x + 1, y : y + 1] = u1h[x + 1, y : y + 1] + rw1[x + 1, y : y + 1]
    for x in (0, X1 + 1):
        v1[x, inner1] = u1h[x, inner1] + rw1[x, inner1]
    for x in range(X2):
        h = wide[x + 1, 8 : 8 + Y2, LANES:]
        hw1[x, pl.ds(0, Y2, stride=2)] = h
        hw1[x, pl.ds(1, Y2, stride=2)] = h

    def up1(x, _):
        halo = unpack_z(both_u, 2 * x, 2, 2) + hw1[x // 2]
        v, vs = sides1(v1, x, halo)
        w = (1.0 - OMEGA) * v + st1[7, x] * (b1[x] + weighted([st1[i, x] for i in range(6)], vs))
        rw0[x, pl.ds(0, Y1, stride=2)] = w
        rw0[x, pl.ds(1, Y1, stride=2)] = w
        return 0

    def v_from(x, acc):
        for d in range(2):
            v = smooth[2 * x + d + 1, own0] + rw0[x]
            vn[0, 2 * x + d + 1, own0] = v
            acc = pack_z(acc, v, 4 * (2 * x + d), 1)
        return acc

    loop(X1, up1)
    zs0[2, 0] = loop(X1, v_from, zero)

    z_ways = ((1, 1), (0, -1))
    round_f = edge_copies(vn, (0,), zs0.at[2, 0], exy, exz, eyz)
    round_f[8:8] = [net.copy(zs0.at[2, 0], zf.at[1 - i, 0], (0, 0, d)) for i, d in z_ways]
    start(round_f)

    def last_part(x, acc):
        _, vs = inside0(vn, x, (0,))
        n = rhs[x] + sum0(x, vs)
        part[x] = n
        return pack_z(acc, n, 4 * x, 1)

    zs0[2, 1] = loop(X0, last_part, zero)
    for x in (0, X0 - 1):
        vn[1, x + 1, own0] = part[x]
    for y in (0, Y0 - 1):
        vn[1, 1 : X0 + 1, 8 + y : 9 + y] = part[:, y : y + 1]
    round_n = face_copies(
        vn, (slice(None),), lambda i: xf.at[i], lambda i: yf.at[i, :, :, pl.ds(0, 1)],
        zs0.at[2, 1], lambda i: zf.at[i, 1],
    )
    start(round_n)
    wait(round_f + round_n)

    edge_x = [cross_z(exz[i, 0], exz[i, 1]) for i in range(2)]
    edge_y = [cross_z(eyz[i, 0], eyz[i, 1]) for i in range(2)]
    cross_v = cross_z(zf[0, 0], zf[1, 0])
    n = cross_z(zf[0, 1], zf[1, 1]) + cz[...] * zs0[2, 0]
    for k, v in enumerate(to_z_faces(edge_x, edge_y)):
        n = n + rims[k] * v
    sum_x = cz[...] * ((1.0 - OMEGA) * cross_v + kz[...] * n)
    z_part = cz[...] * cross_v
    row0 = iota((Y0, LANES), 0)
    for (i, x), (_, far) in zip(ends, far_x):
        vh = xf[i, 0]
        n = xf[i, 1] + st0[i, x] * vn[0, x + 1, own0] + cxz[i] * at_edges(edge_x[i], 4 * far, 4)
        for j, y in rows0:
            n = n + jnp.where(row0 == y, rims[4 + 2 * i + j, :1] * exy[i, j, :1], 0.0)
        sol[X0 + 1 if i else 0, own0] = (1.0 - OMEGA) * vh + kx[i] * n
        part[x] += st0[i, x] * vh
    for i, j, r in far_y:
        crossed[i] = edge_y[i]
        for k, x in ends:
            yf[i, 1, x, :1] += rims[8 + 2 * i + k, :1] * exy[k, i, :1]

    def last_y(x, _):
        for (i, y), (_, j, r) in zip(rows0, far_y):
            row = slice(y, y + 1)
            vh = yf[i, 0, x, :1]
            c = st0[2 + i, x, row]
            n = yf[i, 1, x, :1] + c * vn[0, x + 1, 8 + y : 9 + y]
            n = n + cyz[i, x, :1] * edge_of_y(crossed[i, r : r + 1], x, j)
            at = 8 + Y0 if i else 7
            sol[x + 1, at : at + 1] = (1.0 - OMEGA) * vh + ky[i, x, :1] * n
            part[x, row] += c * vh
        return 0

    loop(X0, last_y)

    def last_z(x, _):
        n = part[x] + at_edges(z_part, 4 * x, 4)
        s = (1.0 - OMEGA) * vn[0, x + 1, own0] + st0[7, x] * n
        sol[x + 1, own0] = s
        sol_ref[x] = s
        return 0

    loop(X0, last_z)

    def residual(x, _):
        res_ref[x] = remainder0(sol, x, sum_x)
        return 0

    loop(X0, residual)
    net.finish()


def scratch(nx):
    def vmem(*shape):
        return pltpu.VMEM(shape + (LANES,), F32)

    padded0 = (X0 + 2, Y0 + 16)
    padded1 = (X1 + 2, Y1 + 16)
    n2, n3, n4, tall = 4 * nx, 2 * nx, nx, ROWS + 16
    reach = 2 * REACH + 1
    return [
        vmem(X0, Y0), vmem(2, *padded0), vmem(*padded0), vmem(2, *padded0), vmem(*padded0),
        vmem(8, X0, Y0), vmem(3, 2, 8), vmem(1, 2, 8), vmem(X0, Y0), vmem(8), vmem(8),
        vmem(2, 2, Y0), vmem(2, 2, X0, 8), vmem(2, 2, 8), vmem(2, Y0), vmem(2, X0, 8), vmem(2, 8),
        vmem(2, 2, Y0), vmem(2, 2, X0, 8), vmem(2, 2, 8),
        vmem(2, 2, 8), vmem(2, 2, 8), vmem(2, 2, 8), vmem(2, 2, 8), vmem(2, 2, 8), vmem(2, 2, 8),
        vmem(2, Y0), vmem(2, X0, 8), vmem(8), vmem(2, Y0), vmem(2, X0, 8), vmem(12, 8), vmem(2, 8),
        vmem(*padded1), vmem(*padded1), vmem(*padded1), vmem(*padded1), vmem(*padded1), vmem(X1, Y1), vmem(8, X1, Y1),
        vmem(X1, Y0), vmem(X2, Y1), vmem(X1, Y0), vmem(2, 8), vmem(2, 2, 8),
        vmem(X2 * LANES), pltpu.VMEM((LANES, 2 * LANES), F32),
        pltpu.VMEM((24, X2 * LANES), F32),
        vmem(reach, nx, 3, 8), vmem(nx, 3, 24), vmem(reach, nx, 4, 24),
        vmem(n2 + 2, tall), vmem(n2 + 2, tall), vmem(n2, ROWS), vmem(8, n2, ROWS),
        vmem(n3 + 2, tall), vmem(n3 + 2, tall), vmem(n3 + 2, tall), vmem(n3, ROWS), vmem(8, n3, ROWS),
        vmem(n4 + 2, tall), vmem(n4 + 2, tall), vmem(n4 + 2, tall), vmem(n4, ROWS), vmem(8, n4, ROWS),
        vmem(n3, 24), vmem(n2 + 2, 40), vmem(n2 + 2, 24),
        pltpu.SemaphoreType.DMA((3,)), pltpu.SemaphoreType.DMA((SEMS,)), pltpu.SemaphoreType.DMA((SEMS,)),
    ]


def solution(mesh):
    sizes = tuple(mesh.shape[a] for a in ("gx", "gy", "gz"))
    block = jax.ShapeDtypeStruct((X0, Y0, LANES), F32)
    spec = P("gx", "gy", "gz")

    def shards(right_side, dielectric, guess):
        return pl.pallas_call(
            functools.partial(kernel, sizes),
            out_shape=(block, block),
            in_specs=[pl.BlockSpec(memory_space=pl.ANY)] * 3,
            out_specs=[pl.BlockSpec(memory_space=pltpu.VMEM)] * 2,
            scratch_shapes=scratch(sizes[0]),
            compiler_params=pltpu.CompilerParams(
                collective_id=0, has_side_effects=True, vmem_limit_bytes=213 * 2**18
            ),
            name="vcycle",
        )(right_side, dielectric, guess)

    return jax.shard_map(
        shards, mesh=mesh, in_specs=(spec, spec, spec), out_specs=(spec, spec), check_vma=False
    )
```
